32 devices in a mesh: tile: 8 (over y, x, core), grp: 4 (over z).
Axes of the slice: x: 2, y: 2, z: 4, core: 2. Of those that a mesh axis runs over, the one named last changes fastest.
Arguments:
- forcing_vector: float32 [70, 64, 512], P(None, 'tile', 'grp'), may hold values from -8 to 8
- shift_weights: float32 [70, 64, 512], P(None, 'tile', 'grp'), may hold values from 0.0001 to 0.0004
- layer_link_factor: float32 [69], replicated, may hold values from 0.5 to 8
- previous_kelvin_field: float32 [70, 8, 4096], P(None, None, ('tile', 'grp')), may hold values from 0.8 to 1.2
- longwave_opacity: float32 [70], replicated, may hold values from 0.02 to 0.5
- shortwave_opacity: float32 [70], replicated, may hold values from 0.01 to 0.05
Outputs:
- solution_field: float32 [70, 64, 512], P(None, 'tile', 'grp')
- radiation_state: float32 [70, 8, 4096], P(None, None, ('tile', 'grp'))
The draws below stay inside these ranges and needn't reach their ends.
All inputs are finite; a program needn't handle non-finite values.
Results may differ from the reference program's by a relative error of at most 0.0003.
Values sent between devices are 32-bit elements; how exact they have to be, the bound alone decides.
No kernel may reach another device: no remote copies, remote signals or barrier semaphores. Data moves between devices by JAX's collectives and lax.ppermute only.
A program may use at most 64 MiB of HBM per device.

```python
import math
import jax
import jax.numpy as jnp
from jax import lax

LAYER_TOTAL = 70
SHARD_POINTS = 8
CY = 128
ITERS = 2
STRIP_POINTS = 64
SPAN_POINTS = 512
N_TILE = 8
N_GRP = 4


def block_scale(rng, dims, shards, least, high):
    factor_of, own = 1.0, jax.random.fold_in(rng, 6)
    for axis_at, blocks in shards:
        draws = jnp.exp(jax.random.uniform(jax.random.fold_in(own, axis_at), (blocks,), jnp.float32, least / len(shards), high / len(shards)))
        factor_of = factor_of * jnp.repeat(draws, dims[axis_at] // blocks).reshape([-1 if axis == axis_at else 1 for axis in range(len(dims))])
    return factor_of


def noise(key, dims, scale, reach, split=(), kind=jnp.bfloat16):
    array = jax.random.normal(key, dims, jnp.float32) * scale
    if len(split) > 0:
        array = block_scale(key, dims, split, -0.22, 0.18) * array
    return jnp.clip(array, min=-reach, max=reach).astype(kind)


def setup_inputs(seed: int = 0) -> dict:
    splits = jax.random.split(jax.random.key(seed), 7)
    return {
        "forcing_vector": noise(splits[0], (LAYER_TOTAL, STRIP_POINTS, SPAN_POINTS), 1.0, 8.0, ((1, 8), (2, 4)), jnp.float32),
        "shift_weights": jnp.clip(jnp.exp(math.log(0.0004) - 1.3862944 * jax.random.uniform(splits[1], (LAYER_TOTAL, STRIP_POINTS, SPAN_POINTS), jnp.float32) ** block_scale(splits[1], (LAYER_TOTAL, STRIP_POINTS, SPAN_POINTS), ((1, 8), (2, 4)), -0.2, 0.2)), 0.0001, 0.0004),
        "layer_link_factor": jnp.clip(jnp.exp(jax.random.uniform(splits[2], (LAYER_TOTAL - 1,), jnp.float32, math.log(0.5), math.log(8.0))), 0.5, 8.0),
        "previous_kelvin_field": jnp.clip(0.8 + 0.40000004 * jax.random.uniform(splits[3], (LAYER_TOTAL, SHARD_POINTS, STRIP_POINTS // SHARD_POINTS * SPAN_POINTS), jnp.float32) ** block_scale(splits[3], (LAYER_TOTAL, SHARD_POINTS, STRIP_POINTS // SHARD_POINTS * SPAN_POINTS), ((2, 32),), -0.2, 0.2), 0.8, 1.2),
        "longwave_opacity": jnp.clip(jnp.exp(jax.random.uniform(splits[4], (LAYER_TOTAL,), jnp.float32, math.log(0.02), math.log(0.5))), 0.02, 0.5),
        "shortwave_opacity": jnp.clip(jnp.exp(jax.random.uniform(splits[5], (LAYER_TOTAL,), jnp.float32, math.log(0.01), math.log(0.05))), 0.01, 0.05),
    }


def column_inverse(layer_link_factor):
    size = layer_link_factor.shape[0] + 1
    zero_one = jnp.zeros((1,), jnp.float32)
    upper = jnp.concatenate([layer_link_factor, zero_one])
    lower = jnp.concatenate([zero_one, layer_link_factor])
    matrix = jnp.diag(4.0 + upper + lower) - jnp.diag(layer_link_factor, 1) - jnp.diag(layer_link_factor, -1)
    factor = jnp.linalg.cholesky(matrix)
    return jax.scipy.linalg.cho_solve((factor, True), jnp.eye(size, dtype=jnp.float32))

def radiation_tables(longwave_opacity, shortwave_opacity):
    levels = longwave_opacity.shape[0]
    transmitted = jnp.exp(-longwave_opacity)
    zero_one = jnp.zeros((1,), jnp.float32)
    interfaces = jnp.concatenate([zero_one, jnp.cumsum(longwave_opacity)])
    interface_index = jnp.arange(levels + 1)[:, None]
    layer_index = jnp.arange(levels)[None, :]
    below_mask = layer_index < interface_index
    gap_down = jnp.where(below_mask, interfaces[:, None] - interfaces[None, 1:], 0.0)
    downward = jnp.where(below_mask, jnp.exp(-gap_down), 0.0) * (1.0 - transmitted)[None, :]
    above_mask = layer_index >= interface_index
    gap_up = jnp.where(above_mask, interfaces[None, :-1] - interfaces[:, None], 0.0)
    upward = jnp.where(above_mask, jnp.exp(-gap_up), 0.0) * (1.0 - transmitted)[None, :]
    surface = jnp.exp(-(interfaces[-1] - interfaces))
    upward = upward.at[:, levels - 1].add(surface)
    matrix = downward[:-1] - downward[1:] + upward[1:] - upward[:-1]
    solar_edges = jnp.concatenate([zero_one, jnp.cumsum(shortwave_opacity)])
    absorbed = 10.0 * (jnp.exp(-solar_edges[:-1]) - jnp.exp(-solar_edges[1:]))
    return (matrix, absorbed)

def sun_cosine(global_row, total_rows):
    latitude = ((global_row.astype(jnp.float32) + 0.5) / total_rows - 0.5) * (math.pi / 2)
    return jnp.cos(latitude - 0.4)

def vertical(source, layer_link_factor):
    fluxes = layer_link_factor[:, None, None] * (source[:-1] - source[1:])
    zeros_level = jnp.zeros_like(source[:1])
    return jnp.concatenate([fluxes, zeros_level], axis=0) - jnp.concatenate([zeros_level, fluxes], axis=0)

def operate(source, shift_weights, layer_link_factor):
    western = jnp.roll(source, 1, axis=1)
    eastern = jnp.roll(source, -1, axis=1)
    padded = jnp.concatenate([source[:, :, :1], source, source[:, :, -1:]], axis=2)
    beside = western + eastern + padded[:, :, 2:] + padded[:, :, :-2]
    return shift_weights * source + 4.0 * source - beside + vertical(source, layer_link_factor)

def coarse_matrix(block_mass, tile_count, group_count):
    block_count = tile_count * group_count
    ordering = jnp.arange(block_count)
    tile_of = ordering // group_count
    group_of = ordering % group_count
    same_group = group_of[:, None] == group_of[None, :]
    tile_gap = (tile_of[:, None] - tile_of[None, :]) % tile_count
    x_near = same_group & ((tile_gap == 1) | (tile_gap == tile_count - 1))
    same_tile = tile_of[:, None] == tile_of[None, :]
    y_near = (same_tile & (jnp.abs(group_of[:, None] - group_of[None, :]) == 1)).astype(jnp.float32)
    y_count = jnp.sum(y_near, axis=1)
    diagonal = block_mass + 2.0 * LAYER_TOTAL * CY + LAYER_TOTAL * SHARD_POINTS * y_count
    return jnp.diag(diagonal) - LAYER_TOTAL * CY * x_near.astype(jnp.float32) - LAYER_TOTAL * SHARD_POINTS * y_near

def radiation_layout(full):
    share_rows = CY // N_TILE
    shaped = full.reshape(LAYER_TOTAL, N_TILE, SHARD_POINTS, N_GRP, N_TILE, share_rows)
    return shaped.transpose(0, 2, 4, 3, 1, 5).reshape(LAYER_TOTAL, SHARD_POINTS, N_TILE * N_GRP * CY)

def grid_layout(columns):
    share_rows = CY // N_TILE
    shaped = columns.reshape(LAYER_TOTAL, SHARD_POINTS, N_TILE, N_GRP, N_TILE, share_rows)
    return shaped.transpose(0, 4, 1, 3, 2, 5).reshape(LAYER_TOTAL, N_TILE * SHARD_POINTS, N_GRP * CY)

def reference(forcing_vector, shift_weights, layer_link_factor, previous_kelvin_field, longwave_opacity, shortwave_opacity):
    highest = lax.Precision.HIGHEST
    matrix, absorbed = radiation_tables(longwave_opacity, shortwave_opacity)
    share_rows = CY // N_TILE
    position = jnp.arange(N_TILE * N_GRP * CY)
    block_index = position // CY
    inside = position % CY
    device_tile = block_index // N_GRP
    device_group = block_index % N_GRP
    global_row = device_group * CY + device_tile * share_rows + inside % share_rows
    cosine = sun_cosine(global_row, N_GRP * CY)
    second_power_entry = previous_kelvin_field * previous_kelvin_field
    emission = second_power_entry * second_power_entry
    column_heating = jnp.dot(matrix, emission.reshape(LAYER_TOTAL, -1), precision=highest).reshape(emission.shape)
    column_heating = column_heating + absorbed[:, None, None] * cosine[None, None, :]
    column_heating = column_heating - jnp.mean(column_heating, axis=0, keepdims=True)
    forcing = forcing_vector + grid_layout(column_heating)
    inverse = column_inverse(layer_link_factor)
    block_mass = shift_weights.reshape(LAYER_TOTAL, N_TILE, SHARD_POINTS, N_GRP, CY).sum(axis=(0, 2, 4)).reshape(-1)
    factor = jnp.linalg.cholesky(coarse_matrix(block_mass, N_TILE, N_GRP))
    solution = jnp.zeros_like(forcing)
    residual = forcing
    directions = []
    images = []
    image_norms = []
    for number in range(ITERS):
        smooth = jnp.dot(inverse, residual.reshape(LAYER_TOTAL, -1), precision=highest).reshape(residual.shape)
        remainder = residual - operate(smooth, shift_weights, layer_link_factor)
        block_sums = remainder.reshape(LAYER_TOTAL, N_TILE, SHARD_POINTS, N_GRP, CY).sum(axis=(0, 2, 4)).reshape(-1)
        coarse = jax.scipy.linalg.cho_solve((factor, True), block_sums)
        spread = jnp.repeat(jnp.repeat(coarse.reshape(N_TILE, N_GRP), SHARD_POINTS, axis=0), CY, axis=1)
        direction = smooth + spread[None]
        operator_image = operate(direction, shift_weights, layer_link_factor)
        weights = [jnp.sum(operator_image * earlier) / norm_value for earlier, norm_value in zip(images, image_norms)]
        for weight, earlier_direction, earlier_image in zip(weights, directions, images):
            direction = direction - weight * earlier_direction
            operator_image = operator_image - weight * earlier_image
        image_norm = jnp.sum(operator_image * operator_image)
        step_size = jnp.sum(residual * operator_image) / image_norm
        solution = solution + step_size * direction
        residual = residual - step_size * operator_image
        directions.append(direction)
        images.append(operator_image)
        image_norms.append(image_norm)
    return (solution, radiation_layout(solution))
```

```python
import math

import jax
import jax.numpy as jnp
from jax import lax
from jax.experimental import pallas as pl
from jax.experimental.pallas import tpu as pltpu
from jax.sharding import PartitionSpec as P

F32 = jnp.float32
HIGHEST = lax.Precision.HIGHEST
VMEM = pl.BlockSpec(memory_space=pltpu.VMEM)


def iota(shape, dim):
    return lax.broadcasted_iota(jnp.int32, shape, dim)


def turn(value, shift, axis=1):
    shift = shift % value.shape[axis]
    return pltpu.roll(value, shift, axis) if shift else value


def total(value):
    return jnp.sum(value, axis=(0, 1), keepdims=True)


def call(kernel, outs, *args):
    return pl.pallas_call(
        kernel,
        out_shape=[jax.ShapeDtypeStruct(shape, F32) for shape in outs],
        in_specs=[VMEM] * len(args),
        out_specs=[VMEM] * len(outs),
        compiler_params=pltpu.CompilerParams(vmem_limit_bytes=32 * 1024 * 1024),
    )(*args)


def load_columns(ref, points, levels, padded):
    tiles = []
    for i in range(points):
        tile = ref[pl.ds(i, levels, stride=points), :]
        if padded > levels:
            tile = jnp.concatenate([tile, jnp.zeros((padded - levels, tile.shape[1]), F32)], axis=0)
        tiles.append(tile)
    return tiles


def store_columns(ref, tiles, levels):
    for i, tile in enumerate(tiles):
        ref[pl.ds(i, levels, stride=len(tiles)), :] = tile[:levels]


def swap_groups(tiles):
    count, lanes = len(tiles), tiles[0].shape[1]
    width = lanes // count
    group = iota(tiles[0].shape, 1) // width
    tiles = list(tiles)
    step = count // 2
    while step:
        low = (group & step) == 0
        for j in range(count):
            if j & step == 0:
                a, b = tiles[j], tiles[j + step]
                tiles[j] = jnp.where(low, a, turn(b, step * width))
                tiles[j + step] = jnp.where(low, turn(a, -step * width), b)
        step //= 2
    return tiles


def pack_kernel(levels, x_ref, out_ref):
    points, padded, _ = out_ref.shape
    for s, tile in enumerate(swap_groups(load_columns(x_ref, points, levels, padded))):
        out_ref[s] = tile


def unpack_kernel(levels, x_ref, out_ref):
    points = x_ref.shape[0]
    store_columns(out_ref, swap_groups([x_ref[s] for s in range(points)]), levels)


def tables_kernel(levels, rows_ref, inverse_ref, matrix_ref, absorbed_ref):
    shape = inverse_ref.shape
    sub, lane = iota(shape, 0), iota(shape, 1)

    def column(row, mask):
        return jnp.broadcast_to(jnp.sum(jnp.where(mask, row, 0.0), axis=1, keepdims=True), shape)

    link, thermal, solar = rows_ref[0:1, :], rows_ref[1:2, :], rows_ref[2:3, :]
    lower = column(link, lane == sub - 1)
    upper = column(link, lane == sub)
    diagonal = 4.0 + lower + upper
    lower, upper = -lower, -upper
    result = jnp.where(lane == sub, 1.0, 0.0).astype(F32)
    step = 1
    while step < levels:
        inverse = 1.0 / diagonal
        a = -lower * turn(inverse, step, 0)
        c = -upper * turn(inverse, -step, 0)
        diagonal = diagonal + a * turn(upper, step, 0) + c * turn(lower, -step, 0)
        result = result + a * turn(result, step, 0) + c * turn(result, -step, 0)
        lower, upper = a * turn(lower, step, 0), c * turn(upper, -step, 0)
        step *= 2
    valid = (sub < levels) & (lane < levels)
    inverse_ref[...] = jnp.where(valid, result / diagonal, 0.0)

    own = column(thermal, lane == sub)
    top_column = column(thermal, lane < sub)
    bottom_column = column(thermal, lane <= sub)
    top_row = jnp.sum(jnp.where(sub < lane, own, 0.0), axis=0, keepdims=True)
    bottom_row = jnp.sum(jnp.where(sub <= lane, own, 0.0), axis=0, keepdims=True)
    whole = jnp.sum(thermal, axis=1, keepdims=True)
    emitted = 1.0 - jnp.exp(-thermal)

    def decay(mask, gap):
        return jnp.where(mask, jnp.exp(-jnp.where(mask, gap, 0.0)), 0.0)

    below, above = lane < sub, lane > sub
    matrix = decay(below, top_column - bottom_row) - decay(below, bottom_column - bottom_row)
    matrix = matrix + decay(above, top_row - bottom_column) - decay(above, top_row - top_column)
    matrix = (matrix - jnp.where(lane == sub, 2.0, 0.0)) * emitted
    surface = (lane == levels - 1) & (sub < levels)
    matrix = matrix + decay(surface, whole - bottom_column) - decay(surface, whole - top_column)
    matrix_ref[...] = jnp.where(valid, matrix, 0.0)
    entering = column(solar, lane < sub)
    leaving = column(solar, lane <= sub)
    absorbed = 10.0 * (jnp.exp(-entering) - jnp.exp(-leaving))
    absorbed_ref[...] = jnp.where(sub < levels, absorbed, 0.0)


def scalars_row(values, lanes):
    count = len(values)
    padded = -(-count // 8) * 8
    rows = [jnp.sum(value, axis=0, keepdims=True) for value in values]
    rows += [jnp.zeros_like(rows[0])] * (padded - count)
    sums = jnp.sum(jnp.concatenate(rows, axis=0), axis=1, keepdims=True)
    shape = (padded, lanes)
    spread = jnp.where(iota(shape, 0) == iota(shape, 1), sums, 0.0)
    return jnp.sum(spread, axis=0, keepdims=True)


def fold(tile):
    parts = [tile[8 * j : 8 * j + 8] for j in range(tile.shape[0] // 8)]
    while len(parts) > 1:
        parts = [a + b for a, b in zip(parts[::2], parts[1::2])] + parts[len(parts) // 2 * 2 :]
    return parts[0]


def add_all(parts):
    parts = list(parts)
    while len(parts) > 1:
        parts = [a + b for a, b in zip(parts[::2], parts[1::2])] + parts[len(parts) // 2 * 2 :]
    return parts[0]


def smooth_kernel(
    levels,
    swap,
    kelvin_ref,
    forcing_ref,
    weight_ref,
    inverse_ref,
    matrix_ref,
    absorbed_ref,
    cosine_ref,
    residual_ref,
    smooth_ref,
    rim_ref,
    west_ref,
    east_ref,
    message_ref,
):
    points, padded, across = residual_ref.shape
    kelvin = [kelvin_ref[i] for i in range(points)]
    if swap:
        kelvin = swap_groups(kelvin)
    squares = [tile * tile for tile in kelvin]
    emission = jnp.concatenate([tile * tile for tile in squares], axis=1)
    heating = jnp.dot(matrix_ref[:, :padded], emission, precision=HIGHEST, preferred_element_type=F32)
    sun = absorbed_ref[...] * cosine_ref[...]
    forcing = load_columns(forcing_ref, points, levels, padded)
    weight = load_columns(weight_ref, points, levels, padded)
    real = iota(sun.shape, 0) < levels
    residual = []
    for i in range(points):
        heat = heating[:, i * across : (i + 1) * across] + sun
        mean = jnp.sum(fold(heat), axis=0, keepdims=True) * (1.0 / levels)
        residual.append(forcing[i] + jnp.where(real, heat - mean, 0.0))
    smooth = jnp.dot(
        inverse_ref[:, :padded],
        jnp.concatenate(residual, axis=1),
        precision=HIGHEST,
        preferred_element_type=F32,
    )
    smooth = [smooth[:, i * across : (i + 1) * across] for i in range(points)]
    for i in range(points):
        residual_ref[i] = residual[i]
        smooth_ref[i] = smooth[i]
    west_ref[0], west_ref[1], west_ref[2] = smooth[0], smooth[1], weight[0]
    east_ref[0], east_ref[1], east_ref[2] = smooth[-2], smooth[-1], weight[-1]
    stride = across // points
    lane = iota((padded, across), 1)
    rim = jnp.zeros((padded, across), F32)
    for i in range(points):
        place = (lane - stride * i + 2) & (across - 1)
        rim = jnp.where(place < 4, turn(smooth[i], stride * i), rim)
        rim = jnp.where((place == 5) | (place == 6), turn(weight[i], stride * i + 4), rim)
    rim_ref[...] = rim
    folded = [fold(tile) for tile in smooth]
    loss = add_all([fold(a * b) for a, b in zip(smooth, weight)])
    mass = add_all([fold(tile) for tile in weight])
    every = add_all(folded)
    lane = iota(every.shape, 1)
    scalars = scalars_row(
        [
            add_all([fold(tile) for tile in residual]) - loss,
            folded[0],
            folded[-1],
            jnp.where(lane == 0, every, 0.0),
            jnp.where(lane == across - 1, every, 0.0),
            mass,
        ],
        across,
    )
    levels_row = jnp.concatenate([rim, jnp.zeros((across - padded, across), F32)], axis=0).T
    last = stride * (points - 1)
    message = jnp.concatenate(
        [
            levels_row[0:1],
            levels_row[across - 1 : across],
            levels_row[last : last + 1],
            levels_row[last - 1 : last],
            scalars,
            jnp.zeros((3, across), F32),
        ],
        axis=0,
    )
    for n in range(message_ref.shape[0]):
        message_ref[n] = message


def small_inverse(block):
    size = len(block)
    block = [list(row) for row in block]
    for k in range(size):
        pivot = 1.0 / block[k][k]
        row = [block[k][j] * pivot for j in range(size)]
        for i in range(size):
            if i != k:
                factor = block[i][k]
                for j in range(size):
                    if j != k:
                        block[i][j] = block[i][j] - factor * row[j]
                block[i][k] = -factor * pivot
        for j in range(size):
            block[k][j] = row[j]
        block[k][k] = pivot
    return block


def product(a, b):
    size = range(len(a))
    return [[add_all([a[i][k] * b[k][j] for k in size]) for j in size] for i in size]


def apply(a, v):
    size = range(len(a))
    return [add_all([a[i][k] * v[k] for k in size]) for i in size]


def flip(a):
    return [list(row) for row in zip(*a)]


def turn_block(a, shift):
    return [[turn(value, shift) for value in row] for row in a]


def with_diagonal(block, row_sums, beside):
    size = range(len(block))
    return [
        [
            row_sums[i] - add_all([block[i][k] for k in size if k != i] + beside[i]) if i == j else block[i][j]
            for j in size
        ]
        for i in size
    ]


def coarse_factor(mass, tiles, groups, x_face, y_face):
    zero = jnp.zeros_like(mass)
    size = range(groups)
    diagonal = [[zero - y_face if abs(i - j) == 1 else zero for i in size] for j in size]
    coupling = [[zero - x_face if i == j else zero for i in size] for j in size]
    row_sums = [turn(mass, -j) for j in size]
    diagonal = with_diagonal(diagonal, row_sums, [[zero - 2.0 * x_face]] * groups)
    steps = []
    step = 1
    while step < tiles:
        inverse = small_inverse(diagonal)
        shift = step * groups
        steps.append((inverse, coupling))
        left = product(coupling, turn_block(inverse, shift))
        low = product(left, flip(coupling))
        high = turn_block(product(flip(coupling), product(inverse, coupling)), -shift)
        row_sums = reduce_sums(inverse, coupling, row_sums, shift)
        diagonal = [[diagonal[i][j] - (low[i][j] + high[i][j]) for j in size] for i in size]
        coupling = [[-v for v in row] for row in product(left, turn_block(coupling, shift))]
        step *= 2
        beside = [
            [add_all(coupling[i]), turn(add_all(flip(coupling)[i]), -step * groups)] for i in size
        ]
        diagonal = with_diagonal(diagonal, row_sums, beside)
    last = [[diagonal[i][j] + (coupling[i][j] + coupling[j][i]) for j in size] for i in size]
    last = with_diagonal(last, row_sums, [[]] * groups)
    return steps, small_inverse(last)


def reduce_sums(inverse, coupling, values, shift):
    scaled = apply(inverse, values)
    low = apply(coupling, [turn(v, shift) for v in scaled])
    high = [turn(v, -shift) for v in apply(flip(coupling), scaled)]
    return [v - (a + b) for v, a, b in zip(values, low, high)]


def coarse_solve(steps, last, sums, groups):
    values = [turn(sums, -j) for j in range(groups)]
    shift = groups
    for inverse, coupling in steps:
        values = reduce_sums(inverse, coupling, values, shift)
        shift *= 2
    values = apply(last, values)
    residue = iota(sums.shape, 1) % groups
    result = values[0]
    for j in range(1, groups):
        result = jnp.where(residue == j, turn(values[j], j), result)
    return result


def around(row, groups):
    residue = iota(row.shape, 1) % groups
    south = jnp.where(residue == 0, row, turn(row, 1))
    north = jnp.where(residue == groups - 1, row, turn(row, -1))
    return turn(row, groups), turn(row, -groups), south, north


def by_block(received):
    blocks, lanes = received.shape
    if blocks < lanes:
        received = jnp.concatenate([received] * (lanes // blocks), axis=0)
    return received.T


def save_steps(ref, steps, last):
    rows = [v for inverse, coupling in steps for block in (inverse, coupling) for row in block for v in row]
    rows += [v for row in last for v in row]
    for n, row in enumerate(rows):
        ref[n : n + 1, :] = row


def saved_rows(tiles, groups):
    steps = max(tiles - 1, 0).bit_length()
    return (2 * steps + 1) * groups * groups


def load_steps(ref, tiles, groups):
    place = 0
    blocks = []
    for _ in range(2 * max(tiles - 1, 0).bit_length() + 1):
        block = []
        for _ in range(groups):
            block.append([ref[place + j : place + j + 1, :] for j in range(groups)])
            place += groups
        blocks.append(block)
    return list(zip(blocks[:-1:2], blocks[1::2])), blocks[-1]


def second_kernel(
    levels,
    tiles,
    groups,
    received_ref,
    from_west_ref,
    from_east_ref,
    from_south_ref,
    from_north_ref,
    rim_ref,
    smooth_ref,
    residual_ref,
    weight_ref,
    inverse_ref,
    second_ref,
    steps_ref,
    coarse_ref,
    message_ref,
):
    points, padded, across = smooth_ref.shape
    blocks = tiles * groups
    stride = across // points
    tile_index, group_index = lax.axis_index("tile"), lax.axis_index("grp")
    at_south, at_north = group_index == 0, group_index == groups - 1

    scalars = by_block(received_ref[pl.ds(4, blocks, stride=8), :])
    base, west, east, south, north, mass = [scalars[j : j + 1, :] for j in range(6)]
    residue = iota(base.shape, 1) % groups
    facing_south = jnp.where(residue == 0, south, turn(north, 1))
    facing_north = jnp.where(residue == groups - 1, north, turn(south, -1))
    sums = base + (
        (turn(east, groups) - west)
        + (turn(west, -groups) - east)
        + (facing_south - south)
        + (facing_north - north)
    )
    steps, last = coarse_factor(
        mass, tiles, groups, float(levels * across), float(levels * points)
    )
    coarse = coarse_solve(steps, last, sums, groups)
    save_steps(steps_ref, steps, last)
    coarse_ref[...] = coarse

    west_tile = lax.rem(tile_index + tiles - 1, tiles)
    east_tile = lax.rem(tile_index + 1, tiles)
    south_group = jnp.maximum(group_index - 1, 0)
    north_group = jnp.minimum(group_index + 1, groups - 1)
    places = [
        tile * groups + group
        for tile, group in (
            (tile_index, group_index),
            (west_tile, group_index),
            (east_tile, group_index),
            (tile_index, south_group),
            (tile_index, north_group),
            (west_tile, south_group),
            (east_tile, south_group),
            (west_tile, north_group),
            (east_tile, north_group),
        )
    ]
    lane = iota(coarse.shape, 1)
    picked = [jnp.sum(jnp.where(lane == place, coarse, 0.0), axis=1, keepdims=True) for place in places]
    shape = (padded, across)
    real = iota(shape, 0) < levels
    own, e_west, e_east, e_south, e_north, e_sw, e_se, e_nw, e_ne = [
        jnp.where(real, value, 0.0) for value in picked
    ]

    corner_rows = [
        received_ref[pl.ds(8 * places[5] + 3, 1), :],
        received_ref[pl.ds(8 * places[6] + 1, 1), :],
        received_ref[pl.ds(8 * places[7] + 2, 1), :],
        received_ref[pl.ds(8 * places[8], 1), :],
    ]
    corners = jnp.concatenate(corner_rows + [jnp.zeros((across - 4, across), F32)], axis=0).T
    c_sw, c_se, c_nw, c_ne = [corners[:padded, j : j + 1] for j in range(4)]

    lane = iota(shape, 1)
    first, final = lane == 0, lane == across - 1

    def across_sum(tile, low, high):
        low = jnp.where(first, jnp.where(at_south, tile, low), turn(tile, 1))
        high = jnp.where(final, jnp.where(at_north, tile, high), turn(tile, -1))
        return low + high

    weight = load_columns(weight_ref, points, levels, padded)
    weight = [from_west_ref[2]] + weight + [from_east_ref[2]]
    field = (
        [from_west_ref[0], from_west_ref[1]]
        + [smooth_ref[i] for i in range(points)]
        + [from_east_ref[0], from_east_ref[1]]
    )

    def spread_image(tile_weight, here, ends, low, high):
        value = tile_weight * here
        if ends:
            value = value + add_all([here - there for there in ends])
        return value + jnp.where(first, here - low, jnp.where(final, here - high, 0.0))

    rim, from_south, from_north = rim_ref[...], from_south_ref[...], from_north_ref[...]
    lows = [c_sw] + [turn(from_south, 1 - stride * i) for i in range(points)] + [c_se]
    highs = [c_nw] + [turn(from_north, -1 - stride * i) for i in range(points)] + [c_ne]
    near = [(e_west, (own,), e_sw, e_nw)] + [(own, (), e_south, e_north)] * points
    near += [(e_east, (own,), e_se, e_ne)]
    near[1] = (own, (e_west,), e_south, e_north)
    near[points] = (own, (e_east,), e_south, e_north)
    image = [
        (field[i] + field[i + 2])
        + across_sum(field[i + 1], lows[i], highs[i])
        - (weight[i] * field[i + 1] + spread_image(weight[i], *near[i]))
        for i in range(points + 2)
    ]
    edge = stride * (points - 1)

    def ring_image(tile, step, here, west, east, west_lane, east_lane, c_west, c_east):
        rim_weight = turn(tile, -4)
        spread = rim_weight * here + (here - own)
        spread = spread + jnp.where(lane == west_lane, here - west, jnp.where(lane == east_lane, here - east, 0.0))
        return (
            jnp.where(lane == west_lane, c_west, turn(tile, stride))
            + jnp.where(lane == east_lane, c_east, turn(tile, -stride))
            + (turn(tile, step) + turn(rim, -step))
            - (rim_weight * tile + spread)
        )

    ring_south = ring_image(from_south, 1, e_south, e_sw, e_se, across - 1, edge - 1, c_sw, c_se)
    ring_north = ring_image(from_north, -1, e_north, e_nw, e_ne, 0, edge, c_nw, c_ne)
    inside = lane & (stride - 1)
    is_south, is_north = inside == stride - 1, inside == 0
    ring = jnp.where(is_south, ring_south, jnp.where(is_north, ring_north, 0.0))
    ring_field = jnp.where(is_south, from_south, from_north)
    second = jnp.dot(
        inverse_ref[:, :padded],
        jnp.concatenate(image + [ring], axis=1),
        precision=HIGHEST,
        preferred_element_type=F32,
    )
    second = [second[:, i * across : (i + 1) * across] for i in range(points + 3)]
    ring = ring_field - second.pop()
    second = [field[i + 1] - tile for i, tile in enumerate(second)]

    names = ("image", "change", "residual")
    pairs = {}
    sides = {name: [] for name in names}
    left = []

    def collect(key, value):
        pairs.setdefault(key, []).append(fold(value))

    for i in range(points):
        tile = second[i + 1]
        second_ref[i] = tile
        again = (
            (second[i] + second[i + 2])
            + across_sum(tile, turn(ring, 1 - stride * i), turn(ring, -1 - stride * i))
            - weight[i + 1] * tile
        )
        residual = residual_ref[i]
        result = residual - image[i + 1]
        change = result - again
        left.append(fold(again + (result - 4.0 * tile)))
        heavy = weight[i + 1]
        collect("qq", result * result)
        collect("rq", residual * result)
        collect("qd", result * change)
        collect("dd", change * change)
        collect("rd", residual * change)
        collect("ww", heavy * heavy)
        sides.setdefault("weight", []).append(fold(heavy))
        for name, value in zip(names, (result, change, residual)):
            sides[name].append(fold(value))
            collect("w" + name, heavy * value)
    pairs = {key: add_all(value) for key, value in pairs.items()}
    lane = iota(pairs["qq"].shape, 1)
    out = [pairs[key] for key in ("qq", "rq", "qd", "dd", "rd")]
    for name in names + ("weight",):
        every = add_all(sides[name])
        out += [
            pairs["ww"] if name == "weight" else pairs["w" + name],
            sides[name][0],
            sides[name][-1],
            jnp.where(lane == 0, every, 0.0),
            jnp.where(lane == across - 1, every, 0.0),
        ]
    out.append(add_all(left))
    row = scalars_row(out, across)
    message_ref[...] = jnp.broadcast_to(row, message_ref.shape)


def final_kernel(
    levels,
    tiles,
    groups,
    swap,
    received_ref,
    steps_ref,
    coarse_ref,
    smooth_ref,
    second_ref,
    field_ref,
    packed_ref,
):
    points, padded, across = smooth_ref.shape
    blocks = tiles * groups
    rows = by_block(received_ref[...])
    rows = [rows[j : j + 1, :] for j in range(26)]
    steps, last = load_steps(steps_ref, tiles, groups)
    coarse = coarse_solve(steps, last, rows[25], groups)
    jumps = [coarse - near for near in around(coarse, groups)]

    def against(part):
        return add_all([rows[part] * coarse] + [rows[part + 1 + j] * jumps[j] for j in range(4)])

    j_w, j_e, j_s, j_n = jumps
    x_face, y_face = float(levels * across), float(levels * points)
    weighted = add_all([rows[21 + j] * jumps[j] for j in range(4)])
    square = (
        coarse * (rows[20] * coarse + 2.0 * weighted)
        + x_face * (j_w * j_w + j_e * j_e)
        + y_face * (j_s * j_s + j_n * j_n)
        + (2.0 * levels) * ((j_w + j_e) * (j_s + j_n))
    )
    lane = iota(coarse.shape, 1)
    place = lax.axis_index("tile") * groups + lax.axis_index("grp")
    parts = [
        rows[0],
        rows[1],
        rows[2] + against(5),
        rows[3] + 2.0 * against(10) + square,
        rows[4] + against(15),
    ]
    parts = [jnp.where(lane < blocks, part, 0.0) for part in parts]
    parts += [jnp.where(lane == place, value, 0.0) for value in (coarse_ref[...], coarse)]
    parts.append(jnp.zeros_like(coarse))
    sums = jnp.sum(jnp.concatenate(parts, axis=0), axis=1, keepdims=True)
    qq, rq, qv, vv, rv, first, second = [sums[j : j + 1, :] for j in range(7)]
    alpha = rq / qq
    beta = qv / qq
    kappa = (rv - alpha * qv) / (vv - beta * qv)
    scale = alpha - kappa * beta
    shift = scale * first + kappa * second
    result = [scale * smooth_ref[i] + (kappa * second_ref[i] + shift) for i in range(points)]
    store_columns(field_ref, result, levels)
    if swap:
        result = swap_groups(result)
    for i in range(points):
        packed_ref[i] = result[i]


def per_device(
    forcing_vector,
    shift_weights,
    layer_link_factor,
    previous_kelvin_field,
    longwave_opacity,
    shortwave_opacity,
):
    tiles, groups = lax.axis_size("tile"), lax.axis_size("grp")
    levels, points, across = forcing_vector.shape
    padded = -(-levels // 8) * 8
    blocks = tiles * groups
    lanes = max(across, blocks)
    width = across // tiles
    swap = tiles == points
    flat = (levels * points, across)

    def to_tiles(value):
        return lax.all_to_all(value, "tile", split_axis=0, concat_axis=0, tiled=True)

    def gather(value):
        return lax.all_to_all(value, ("tile", "grp"), split_axis=0, concat_axis=0, tiled=True)

    def part(kernel, *settings):
        return lambda *refs: kernel(*settings, *refs)

    kelvin = previous_kelvin_field
    if swap:
        (kelvin,) = call(
            part(pack_kernel, levels), [(points, padded, across)], kelvin.reshape(flat)
        )
        kelvin = to_tiles(kelvin)
    else:
        kelvin = kelvin.reshape(levels, points, tiles, width).transpose(2, 1, 0, 3)
        kelvin = to_tiles(kelvin).transpose(1, 2, 0, 3).reshape(points, levels, across)
        kelvin = jnp.pad(kelvin, ((0, 0), (0, padded - levels), (0, 0)))

    vectors = (layer_link_factor, longwave_opacity, shortwave_opacity)
    rows = jnp.stack([jnp.pad(v, (0, across - v.shape[0])) for v in vectors])
    rows = jnp.pad(rows, ((0, 8 - len(vectors)), (0, 0)))
    inverse, matrix, absorbed = call(
        part(tables_kernel, levels), [(padded, across)] * 3, rows
    )
    global_row = lax.axis_index("grp") * across + jnp.arange(across)
    latitude = ((global_row.astype(F32) + 0.5) / (across * groups) - 0.5) * (math.pi / 2)
    cosine = jnp.cos(latitude - 0.4)[None, :]

    forcing = forcing_vector.reshape(flat)
    weights = shift_weights.reshape(flat)
    field = (points, padded, across)
    residual, smooth, rim, west, east, message = call(
        part(smooth_kernel, levels, swap),
        [field, field, (padded, across), (3, padded, across), (3, padded, across), (blocks, 8, across)],
        kelvin,
        forcing,
        weights,
        inverse,
        matrix,
        absorbed,
        cosine,
    )
    received = gather(message).reshape(blocks * 8, across)
    forward = [(i, (i + 1) % tiles) for i in range(tiles)]
    backward = [(j, i) for i, j in forward]
    upward = [(i, (i + 1) % groups) for i in range(groups)]
    downward = [(j, i) for i, j in upward]
    from_west = lax.ppermute(east, "tile", forward)
    from_east = lax.ppermute(west, "tile", backward)
    from_south = lax.ppermute(rim, "grp", upward)
    from_north = lax.ppermute(rim, "grp", downward)
    second, steps, coarse, message = call(
        part(second_kernel, levels, tiles, groups),
        [field, (saved_rows(tiles, groups), lanes), (1, lanes), (blocks, across)],
        received,
        from_west,
        from_east,
        from_south,
        from_north,
        rim,
        smooth,
        residual,
        weights,
        inverse,
    )
    received = gather(message)
    solution_field, packed = call(
        part(final_kernel, levels, tiles, groups, swap),
        [flat, field],
        received,
        steps,
        coarse,
        smooth,
        second,
    )
    if swap:
        packed = to_tiles(packed)
        (state,) = call(part(unpack_kernel, levels), [flat], packed)
        state = state.reshape(levels, points, across)
    else:
        packed = packed[:, :levels].reshape(points, levels, tiles, width).transpose(2, 1, 0, 3)
        state = to_tiles(packed).transpose(2, 1, 0, 3).reshape(levels, points, across)
    return solution_field.reshape(levels, points, across), state


def solution(mesh):
    return jax.shard_map(
        per_device,
        mesh=mesh,
        in_specs=(
            P(None, "tile", "grp"),
            P(None, "tile", "grp"),
            P(),
            P(None, None, ("tile", "grp")),
            P(),
            P(),
        ),
        out_specs=(P(None, "tile", "grp"), P(None, None, ("tile", "grp"))),
        check_vma=False,
    )
```

```python
import math

import jax
import jax.numpy as jnp
from jax import lax
from jax.experimental import pallas as pl
from jax.experimental.pallas import tpu as pltpu
from jax.sharding import PartitionSpec as P

F32 = jnp.float32
HIGHEST = lax.Precision.HIGHEST
MESSAGE_ROWS = 4
LAST_ROWS = 4
VMEM = pl.BlockSpec(memory_space=pltpu.VMEM)


def iota(shape, dim):
    return lax.broadcasted_iota(jnp.int32, shape, dim)


def turn(value, shift, axis=1):
    shift = shift % value.shape[axis]
    return pltpu.roll(value, shift, axis) if shift else value


def total(value):
    return jnp.sum(value, axis=(0, 1), keepdims=True)


def call(kernel, outs, *args, scratch=()):
    return pl.pallas_call(
        kernel,
        out_shape=[jax.ShapeDtypeStruct(shape, F32) for shape in outs],
        in_specs=[VMEM] * len(args),
        out_specs=[VMEM] * len(outs),
        scratch_shapes=[pltpu.VMEM(shape, F32) for shape in scratch],
        compiler_params=pltpu.CompilerParams(vmem_limit_bytes=32 * 1024 * 1024),
    )(*args)


def load_columns(ref, points, levels, padded):
    tiles = []
    for i in range(points):
        tile = ref[pl.ds(i, levels, stride=points), :]
        if padded > levels:
            tile = jnp.concatenate([tile, jnp.zeros((padded - levels, tile.shape[1]), F32)], axis=0)
        tiles.append(tile)
    return tiles


def store_columns(ref, tiles, levels):
    for i, tile in enumerate(tiles):
        ref[pl.ds(i, levels, stride=len(tiles)), :] = tile[:levels]


def swap_groups(tiles):
    count, lanes = len(tiles), tiles[0].shape[1]
    width = lanes // count
    group = iota(tiles[0].shape, 1) // width
    tiles = list(tiles)
    step = count // 2
    while step:
        low = (group & step) == 0
        for j in range(count):
            if j & step == 0:
                a, b = tiles[j], tiles[j + step]
                tiles[j] = jnp.where(low, a, turn(b, step * width))
                tiles[j + step] = jnp.where(low, turn(a, -step * width), b)
        step //= 2
    return tiles


def pack_kernel(levels, x_ref, out_ref):
    points, padded, _ = out_ref.shape
    for s, tile in enumerate(swap_groups(load_columns(x_ref, points, levels, padded))):
        out_ref[s] = tile


def tables_kernel(levels, rows_ref, inverse_ref, matrix_ref, absorbed_ref):
    shape = inverse_ref.shape
    sub, lane = iota(shape, 0), iota(shape, 1)

    def column(row, mask):
        return jnp.broadcast_to(jnp.sum(jnp.where(mask, row, 0.0), axis=1, keepdims=True), shape)

    link, thermal, solar = rows_ref[0:1, :], rows_ref[1:2, :], rows_ref[2:3, :]
    lower = column(link, lane == sub - 1)
    upper = column(link, lane == sub)
    diagonal = 4.0 + lower + upper
    lower, upper = -lower, -upper
    result = jnp.where(lane == sub, 1.0, 0.0).astype(F32)
    step = 1
    while step < levels:
        inverse = 1.0 / diagonal
        a = -lower * turn(inverse, step, 0)
        c = -upper * turn(inverse, -step, 0)
        diagonal = diagonal + a * turn(upper, step, 0) + c * turn(lower, -step, 0)
        result = result + a * turn(result, step, 0) + c * turn(result, -step, 0)
        lower, upper = a * turn(lower, step, 0), c * turn(upper, -step, 0)
        step *= 2
    valid = (sub < levels) & (lane < levels)
    inverse_ref[...] = jnp.where(valid, result / diagonal, 0.0)

    own = column(thermal, lane == sub)
    top_column = column(thermal, lane < sub)
    bottom_column = column(thermal, lane <= sub)
    top_row = jnp.sum(jnp.where(sub < lane, own, 0.0), axis=0, keepdims=True)
    bottom_row = jnp.sum(jnp.where(sub <= lane, own, 0.0), axis=0, keepdims=True)
    whole = jnp.sum(thermal, axis=1, keepdims=True)
    emitted = 1.0 - jnp.exp(-thermal)

    def decay(mask, gap):
        return jnp.where(mask, jnp.exp(-jnp.where(mask, gap, 0.0)), 0.0)

    below, above = lane < sub, lane > sub
    matrix = decay(below, top_column - bottom_row) - decay(below, bottom_column - bottom_row)
    matrix = matrix + decay(above, top_row - bottom_column) - decay(above, top_row - top_column)
    matrix = (matrix - jnp.where(lane == sub, 2.0, 0.0)) * emitted
    surface = (lane == levels - 1) & (sub < levels)
    matrix = matrix + decay(surface, whole - bottom_column) - decay(surface, whole - top_column)
    matrix_ref[...] = jnp.where(valid, matrix, 0.0)
    entering = column(solar, lane < sub)
    leaving = column(solar, lane <= sub)
    absorbed = 10.0 * (jnp.exp(-entering) - jnp.exp(-leaving))
    absorbed_ref[...] = jnp.where(sub < levels, absorbed, 0.0)


def scalars_row(values, lanes):
    count = len(values)
    padded = -(-count // 8) * 8
    rows = [jnp.sum(value, axis=0, keepdims=True) for value in values]
    rows += [jnp.zeros_like(rows[0])] * (padded - count)
    sums = jnp.sum(jnp.concatenate(rows, axis=0), axis=1, keepdims=True)
    shape = (padded, lanes)
    spread = jnp.where(iota(shape, 0) == iota(shape, 1), sums, 0.0)
    return jnp.sum(spread, axis=0, keepdims=True)


def fold(tile):
    parts = [tile[8 * j : 8 * j + 8] for j in range(tile.shape[0] // 8)]
    while len(parts) > 1:
        parts = [a + b for a, b in zip(parts[::2], parts[1::2])] + parts[len(parts) // 2 * 2 :]
    return parts[0]


def add_all(parts):
    parts = list(parts)
    while len(parts) > 1:
        parts = [a + b for a, b in zip(parts[::2], parts[1::2])] + parts[len(parts) // 2 * 2 :]
    return parts[0]


def smooth_kernel(
    levels,
    tiles,
    groups,
    swap,
    kelvin_ref,
    forcing_ref,
    weight_ref,
    inverse_ref,
    matrix_ref,
    absorbed_ref,
    cosine_ref,
    residual_ref,
    smooth_ref,
    message_ref,
):
    points, padded, across = residual_ref.shape
    kelvin = [kelvin_ref[i] for i in range(points)]
    if swap:
        kelvin = swap_groups(kelvin)
    squares = [tile * tile for tile in kelvin]
    emission = jnp.concatenate([tile * tile for tile in squares], axis=1)
    heating = jnp.dot(matrix_ref[:, :padded], emission, precision=HIGHEST, preferred_element_type=F32)
    sun = absorbed_ref[...] * cosine_ref[...]
    forcing = load_columns(forcing_ref, points, levels, padded)
    weight = load_columns(weight_ref, points, levels, padded)
    real = iota(sun.shape, 0) < levels
    residual = []
    for i in range(points):
        heat = heating[:, i * across : (i + 1) * across] + sun
        mean = jnp.sum(fold(heat), axis=0, keepdims=True) * (1.0 / levels)
        residual.append(forcing[i] + jnp.where(real, heat - mean, 0.0))
    smooth = jnp.dot(
        inverse_ref[:, :padded],
        jnp.concatenate(residual, axis=1),
        precision=HIGHEST,
        preferred_element_type=F32,
    )
    smooth = [smooth[:, i * across : (i + 1) * across] for i in range(points)]
    for i in range(points):
        residual_ref[i] = residual[i]
        smooth_ref[i] = smooth[i]
    folded = [fold(tile) for tile in smooth]
    loss = add_all([fold(a * b) for a, b in zip(smooth, weight)])
    mass = add_all([fold(tile) for tile in weight])
    every = add_all(folded)
    lane = iota(every.shape, 1)
    scalars = scalars_row(
        [
            add_all([fold(tile) for tile in residual]) - loss,
            folded[0],
            folded[-1],
            jnp.where(lane == 0, every, 0.0),
            jnp.where(lane == across - 1, every, 0.0),
            mass,
        ],
        across,
    )
    lane = iota((padded, across), 1)
    corner = jnp.where((lane == 0) | (lane == across - 1), smooth[0], turn(smooth[-1], 2))
    rows = jnp.concatenate([corner, jnp.zeros((across - padded, across), F32)], axis=0).T
    scalars = turn(scalars, padded)
    message_ref[...] = jnp.zeros(message_ref.shape, F32)
    message_ref[:, 0, :] = jnp.broadcast_to(scalars, (message_ref.shape[0], across))
    corners = (0, 2, across - 1, 1)
    for place, corner in zip(neighbours(tiles, groups)[5:], corners):
        message_ref[pl.ds(place, 1), 0, :] = rows[corner : corner + 1] + scalars


def rim_kernel(levels, smooth_ref, weight_ref, rim_ref):
    points, padded, across = smooth_ref.shape
    weight = load_columns(weight_ref, points, levels, padded)
    stride = across // points
    lane = iota((padded, across), 1)
    rim = jnp.zeros((padded, across), F32)
    for i in range(points):
        place = (lane - stride * i + 2) & (across - 1)
        rim = jnp.where(place < 4, turn(smooth_ref[i], stride * i), rim)
        rim = jnp.where((place == 5) | (place == 6), turn(weight[i], stride * i + 4), rim)
    rim_ref[...] = rim


def side_kernel(levels, swap, smooth_ref, weight_ref, _, inner_ref, outer_ref, *packed_ref):
    points, padded, _ = smooth_ref.shape
    even = lax.rem(lax.axis_index("tile"), 2) == 0
    for j, place in enumerate((0, 1)):
        west, east = smooth_ref[place], smooth_ref[points - 2 + place]
        inner_ref[j] = jnp.where(even, east, west)
        outer_ref[j] = jnp.where(even, west, east)
    extra = jnp.zeros((padded - levels, inner_ref.shape[2]), F32)
    west, east = [
        jnp.concatenate([weight_ref[pl.ds(i, levels, stride=points), :], extra], axis=0)
        for i in (0, points - 1)
    ]
    inner_ref[2] = jnp.where(even, east, west)
    outer_ref[2] = jnp.where(even, west, east)
    if swap:
        for s, tile in enumerate(swap_groups([smooth_ref[i] for i in range(points)])):
            packed_ref[0][s] = tile


def send_kernel(smooth_ref, second_ref, *out_refs):
    *out_refs, packed_ref = out_refs
    points = second_ref.shape[0]
    for s, tile in enumerate(swap_groups([second_ref[i] for i in range(points)])):
        packed_ref[s] = tile
    tile = lax.axis_index("tile")
    for k, out_ref in enumerate(out_refs):
        out_ref[0] = smooth_ref[tile ^ k]
        out_ref[1] = packed_ref[tile ^ k]


def neighbours(tiles, groups):
    tile, group = lax.axis_index("tile"), lax.axis_index("grp")
    west, east = lax.rem(tile + tiles - 1, tiles), lax.rem(tile + 1, tiles)
    south, north = jnp.maximum(group - 1, 0), jnp.minimum(group + 1, groups - 1)
    pairs = [(tile, group), (west, group), (east, group), (tile, south), (tile, north)]
    pairs += [(west, south), (east, south), (west, north), (east, north)]
    return [x * groups + y for x, y in pairs]


def small_inverse(block):
    size = len(block)
    block = [list(row) for row in block]
    for k in range(size):
        pivot = 1.0 / block[k][k]
        row = [block[k][j] * pivot for j in range(size)]
        for i in range(size):
            if i != k:
                factor = block[i][k]
                for j in range(size):
                    if j != k:
                        block[i][j] = block[i][j] - factor * row[j]
                block[i][k] = -factor * pivot
        for j in range(size):
            block[k][j] = row[j]
        block[k][k] = pivot
    return block


def product(a, b):
    size = range(len(a))
    return [[add_all([a[i][k] * b[k][j] for k in size]) for j in size] for i in size]


def apply(a, v):
    size = range(len(a))
    return [add_all([a[i][k] * v[k] for k in size]) for i in size]


def flip(a):
    return [list(row) for row in zip(*a)]


def turn_block(a, shift):
    return [[turn(value, shift) for value in row] for row in a]


def with_diagonal(block, row_sums, beside):
    size = range(len(block))
    return [
        [
            row_sums[i] - add_all([block[i][k] for k in size if k != i] + beside[i]) if i == j else block[i][j]
            for j in size
        ]
        for i in size
    ]


def coarse_factor(mass, tiles, groups, x_face, y_face):
    zero = jnp.zeros_like(mass)
    size = range(groups)
    diagonal = [[zero - y_face if abs(i - j) == 1 else zero for i in size] for j in size]
    coupling = [[zero - x_face if i == j else zero for i in size] for j in size]
    row_sums = [turn(mass, -j) for j in size]
    diagonal = with_diagonal(diagonal, row_sums, [[zero - 2.0 * x_face]] * groups)
    steps = []
    step = 1
    while step < tiles:
        inverse = small_inverse(diagonal)
        shift = step * groups
        steps.append((inverse, coupling))
        left = product(coupling, turn_block(inverse, shift))
        low = product(left, flip(coupling))
        high = turn_block(product(flip(coupling), product(inverse, coupling)), -shift)
        row_sums = reduce_sums(inverse, coupling, row_sums, shift)
        diagonal = [[diagonal[i][j] - (low[i][j] + high[i][j]) for j in size] for i in size]
        coupling = [[-v for v in row] for row in product(left, turn_block(coupling, shift))]
        step *= 2
        beside = [
            [add_all(coupling[i]), turn(add_all(flip(coupling)[i]), -step * groups)] for i in size
        ]
        diagonal = with_diagonal(diagonal, row_sums, beside)
    last = [[diagonal[i][j] + (coupling[i][j] + coupling[j][i]) for j in size] for i in size]
    last = with_diagonal(last, row_sums, [[]] * groups)
    return steps, small_inverse(last)


def reduce_sums(inverse, coupling, values, shift):
    scaled = apply(inverse, values)
    low = apply(coupling, [turn(v, shift) for v in scaled])
    high = [turn(v, -shift) for v in apply(flip(coupling), scaled)]
    return [v - (a + b) for v, a, b in zip(values, low, high)]


def coarse_solve(steps, last, sums, groups):
    values = [turn(sums, -j) for j in range(groups)]
    shift = groups
    for inverse, coupling in steps:
        values = reduce_sums(inverse, coupling, values, shift)
        shift *= 2
    values = apply(last, values)
    residue = iota(sums.shape, 1) % groups
    result = values[0]
    for j in range(1, groups):
        result = jnp.where(residue == j, turn(values[j], j), result)
    return result


def around(row, groups):
    residue = iota(row.shape, 1) % groups
    south = jnp.where(residue == 0, row, turn(row, 1))
    north = jnp.where(residue == groups - 1, row, turn(row, -1))
    return turn(row, groups), turn(row, -groups), south, north


def by_block(received):
    blocks, lanes = received.shape
    if blocks < lanes:
        received = jnp.concatenate([received] * (lanes // blocks), axis=0)
    return received.T


def save_steps(ref, steps, last):
    rows = [v for inverse, coupling in steps for block in (inverse, coupling) for row in block for v in row]
    rows += [v for row in last for v in row]
    for n, row in enumerate(rows):
        ref[n : n + 1, :] = row


def saved_rows(tiles, groups):
    steps = max(tiles - 1, 0).bit_length()
    return (2 * steps + 1) * groups * groups


def load_steps(ref, tiles, groups):
    place = 0
    blocks = []
    for _ in range(2 * max(tiles - 1, 0).bit_length() + 1):
        block = []
        for _ in range(groups):
            block.append([ref[place + j : place + j + 1, :] for j in range(groups)])
            place += groups
        blocks.append(block)
    return list(zip(blocks[:-1:2], blocks[1::2])), blocks[-1]


def coarse_kernel(levels, points, tiles, groups, received_ref, steps_ref, coarse_ref):
    padded = -(-levels // 8) * 8
    scalars = by_block(received_ref[:, 0, :])
    base, west, east, south, north, mass = [scalars[padded + j : padded + j + 1, :] for j in range(6)]
    residue = iota(base.shape, 1) % groups
    facing_south = jnp.where(residue == 0, south, turn(north, 1))
    facing_north = jnp.where(residue == groups - 1, north, turn(south, -1))
    sums = base + (
        (turn(east, groups) - west)
        + (turn(west, -groups) - east)
        + (facing_south - south)
        + (facing_north - north)
    )
    steps, last = coarse_factor(
        mass, tiles, groups, float(levels * received_ref.shape[2]), float(levels * points)
    )
    coarse = coarse_solve(steps, last, sums, groups)
    save_steps(steps_ref, steps, last)
    coarse_ref[...] = coarse


def second_kernel(
    levels,
    tiles,
    groups,
    received_ref,
    inner_ref,
    outer_ref,
    low_ref,
    high_ref,
    rim_ref,
    smooth_ref,
    residual_ref,
    weight_ref,
    inverse_ref,
    coarse_ref,
    second_ref,
    message_ref,
):
    points, padded, across = smooth_ref.shape
    blocks = tiles * groups
    stride = across // points
    group_index = lax.axis_index("grp")
    even_tile = lax.rem(lax.axis_index("tile"), 2) == 0
    even_group = lax.rem(group_index, 2) == 0
    at_south, at_north = group_index == 0, group_index == groups - 1

    coarse = coarse_ref[...]
    places = neighbours(tiles, groups)
    lane = iota(coarse.shape, 1)
    picked = [jnp.sum(jnp.where(lane == place, coarse, 0.0), axis=1, keepdims=True) for place in places]
    shape = (padded, across)
    real = iota(shape, 0) < levels
    own, e_west, e_east, e_south, e_north, e_sw, e_se, e_nw, e_ne = [
        jnp.where(real, value, 0.0) for value in picked
    ]

    corner_rows = [received_ref[pl.ds(place, 1), 0, :] for place in places[5:]]
    corner_rows = [jnp.where(iota(row.shape, 1) < padded, row, 0.0) for row in corner_rows]
    corners = jnp.concatenate(corner_rows + [jnp.zeros((across - 4, across), F32)], axis=0).T
    c_sw, c_se, c_nw, c_ne = [corners[:padded, j : j + 1] for j in range(4)]

    lane = iota(shape, 1)
    first, final = lane == 0, lane == across - 1

    def across_sum(tile, low, high):
        low = jnp.where(first, jnp.where(at_south, tile, low), turn(tile, 1))
        high = jnp.where(final, jnp.where(at_north, tile, high), turn(tile, -1))
        return low + high

    weight = load_columns(weight_ref, points, levels, padded)
    from_west = [jnp.where(even_tile, outer_ref[j], inner_ref[j]) for j in range(3)]
    from_east = [jnp.where(even_tile, inner_ref[j], outer_ref[j]) for j in range(3)]
    weight = from_west[2:] + weight + from_east[2:]
    field = from_west[:2] + [smooth_ref[i] for i in range(points)] + from_east[:2]

    def spread_image(tile_weight, here, ends, low, high):
        value = tile_weight * here
        if ends:
            value = value + add_all([here - there for there in ends])
        return value + jnp.where(first, here - low, jnp.where(final, here - high, 0.0))

    rim, low, high = rim_ref[...], low_ref[...], high_ref[...]
    from_south = jnp.where(even_group, high, low)
    from_north = jnp.where(even_group, low, high)
    lows = [c_sw] + [turn(from_south, 1 - stride * i) for i in range(points)] + [c_se]
    highs = [c_nw] + [turn(from_north, -1 - stride * i) for i in range(points)] + [c_ne]
    near = [(e_west, (own,), e_sw, e_nw)] + [(own, (), e_south, e_north)] * points
    near += [(e_east, (own,), e_se, e_ne)]
    near[1] = (own, (e_west,), e_south, e_north)
    near[points] = (own, (e_east,), e_south, e_north)
    image = [
        (field[i] + field[i + 2])
        + across_sum(field[i + 1], lows[i], highs[i])
        - (weight[i] * field[i + 1] + spread_image(weight[i], *near[i]))
        for i in range(points + 2)
    ]
    edge = stride * (points - 1)

    def ring_image(tile, step, here, west, east, west_lane, east_lane, c_west, c_east):
        rim_weight = turn(tile, -4)
        spread = rim_weight * here + (here - own)
        spread = spread + jnp.where(lane == west_lane, here - west, jnp.where(lane == east_lane, here - east, 0.0))
        return (
            jnp.where(lane == west_lane, c_west, turn(tile, stride))
            + jnp.where(lane == east_lane, c_east, turn(tile, -stride))
            + (turn(tile, step) + turn(rim, -step))
            - (rim_weight * tile + spread)
        )

    ring_south = ring_image(from_south, 1, e_south, e_sw, e_se, across - 1, edge - 1, c_sw, c_se)
    ring_north = ring_image(from_north, -1, e_north, e_nw, e_ne, 0, edge, c_nw, c_ne)
    inside = lane & (stride - 1)
    is_south, is_north = inside == stride - 1, inside == 0
    ring = jnp.where(is_south, ring_south, jnp.where(is_north, ring_north, 0.0))
    ring_field = jnp.where(is_south, from_south, from_north)
    second = jnp.dot(
        inverse_ref[:, :padded],
        jnp.concatenate(image + [ring], axis=1),
        precision=HIGHEST,
        preferred_element_type=F32,
    )
    second = [second[:, i * across : (i + 1) * across] for i in range(points + 3)]
    ring = ring_field - second.pop()
    second = [field[i + 1] - tile for i, tile in enumerate(second)]

    names = ("image", "change", "residual")
    pairs = {}
    sides = {name: [] for name in names}
    left = []

    def collect(key, value):
        pairs.setdefault(key, []).append(fold(value))

    for i in range(points):
        tile = second[i + 1]
        second_ref[i] = tile
        again = (
            (second[i] + second[i + 2])
            + across_sum(tile, turn(ring, 1 - stride * i), turn(ring, -1 - stride * i))
            - weight[i + 1] * tile
        )
        residual = residual_ref[i]
        result = residual - image[i + 1]
        change = result - again
        left.append(fold(again + (result - 4.0 * tile)))
        heavy = weight[i + 1]
        collect("qq", result * result)
        collect("rq", residual * result)
        collect("qd", result * change)
        collect("dd", change * change)
        collect("rd", residual * change)
        collect("ww", heavy * heavy)
        sides.setdefault("weight", []).append(fold(heavy))
        for name, value in zip(names, (result, change, residual)):
            sides[name].append(fold(value))
            collect("w" + name, heavy * value)
    pairs = {key: add_all(value) for key, value in pairs.items()}
    lane = iota(pairs["qq"].shape, 1)
    out = [pairs[key] for key in ("qq", "rq", "qd", "dd", "rd")]
    for name in names + ("weight",):
        every = add_all(sides[name])
        out += [
            pairs["ww"] if name == "weight" else pairs["w" + name],
            sides[name][0],
            sides[name][-1],
            jnp.where(lane == 0, every, 0.0),
            jnp.where(lane == across - 1, every, 0.0),
        ]
    out.append(add_all(left))
    row = scalars_row(out, across)
    message_ref[...] = jnp.zeros(message_ref.shape, F32)
    message_ref[:, 0, :] = jnp.broadcast_to(row, (blocks, across))


def final_kernel(
    levels,
    tiles,
    groups,
    swap,
    received_ref,
    steps_ref,
    coarse_ref,
    smooth_ref,
    second_ref,
    *refs,
):
    if swap:
        *part_refs, field_ref, state_ref, scratch_ref = refs
    else:
        field_ref, state_ref = refs
    points, padded, across = smooth_ref.shape
    blocks = tiles * groups
    rows = by_block(received_ref[:, 0, :])
    rows = [rows[j : j + 1, :] for j in range(26)]
    steps, last = load_steps(steps_ref, tiles, groups)
    coarse = coarse_solve(steps, last, rows[25], groups)
    jumps = [coarse - near for near in around(coarse, groups)]

    def against(part):
        return add_all([rows[part] * coarse] + [rows[part + 1 + j] * jumps[j] for j in range(4)])

    j_w, j_e, j_s, j_n = jumps
    x_face, y_face = float(levels * across), float(levels * points)
    weighted = add_all([rows[21 + j] * jumps[j] for j in range(4)])
    square = (
        coarse * (rows[20] * coarse + 2.0 * weighted)
        + x_face * (j_w * j_w + j_e * j_e)
        + y_face * (j_s * j_s + j_n * j_n)
        + (2.0 * levels) * ((j_w + j_e) * (j_s + j_n))
    )
    lane = iota(coarse.shape, 1)
    tile, group = lax.axis_index("tile"), lax.axis_index("grp")
    parts = [
        rows[0],
        rows[1],
        rows[2] + against(5),
        rows[3] + 2.0 * against(10) + square,
        rows[4] + against(15),
    ]
    parts = [jnp.where(lane < blocks, part, 0.0) for part in parts]
    parts += [jnp.zeros_like(coarse)] * 3
    sums = jnp.sum(jnp.concatenate(parts, axis=0), axis=1, keepdims=True)
    qq, rq, qv, vv, rv = [sums[j : j + 1, :] for j in range(5)]
    alpha = rq / qq
    beta = qv / qq
    kappa = (rv - alpha * qv) / (vv - beta * qv)
    scale = alpha - kappa * beta
    constant = scale * coarse_ref[...] + kappa * coarse
    others = points if swap else 1
    parts = [jnp.where(lane == (tile ^ k) * groups + group, constant, 0.0) for k in range(others)]
    parts += [jnp.zeros_like(coarse)] * (-others % 8)
    shifts = jnp.sum(jnp.concatenate(parts, axis=0), axis=1, keepdims=True)
    shifts = [shifts[k : k + 1, :] for k in range(others)]
    result = [scale * smooth_ref[i] + (kappa * second_ref[i] + shifts[0]) for i in range(points)]
    store_columns(field_ref, result, levels)
    if swap:
        for k, part_ref in enumerate(part_refs):
            scratch_ref[tile ^ k] = scale * part_ref[0] + (kappa * part_ref[1] + shifts[k])
        result = swap_groups([scratch_ref[s] for s in range(points)])
        store_columns(state_ref, result, levels)
    else:
        for i in range(points):
            state_ref[i] = result[i]


def per_device(
    forcing_vector,
    shift_weights,
    layer_link_factor,
    previous_kelvin_field,
    longwave_opacity,
    shortwave_opacity,
):
    tiles, groups = lax.axis_size("tile"), lax.axis_size("grp")
    levels, points, across = forcing_vector.shape
    padded = -(-levels // 8) * 8
    blocks = tiles * groups
    lanes = max(across, blocks)
    width = across // tiles
    swap = tiles == points
    flat = (levels * points, across)

    def to_tiles(value):
        return lax.all_to_all(value, "tile", split_axis=0, concat_axis=0, tiled=True)

    def gather(value):
        return lax.all_to_all(value, ("tile", "grp"), split_axis=0, concat_axis=0, tiled=True)

    def part(kernel, *settings):
        return lambda *refs: kernel(*settings, *refs)

    kelvin = previous_kelvin_field
    if swap:
        (kelvin,) = call(
            part(pack_kernel, levels), [(points, padded, across)], kelvin.reshape(flat)
        )
        kelvin = to_tiles(kelvin)
    else:
        kelvin = kelvin.reshape(levels, points, tiles, width).transpose(2, 1, 0, 3)
        kelvin = to_tiles(kelvin).transpose(1, 2, 0, 3).reshape(points, levels, across)
        kelvin = jnp.pad(kelvin, ((0, 0), (0, padded - levels), (0, 0)))

    vectors = (layer_link_factor, longwave_opacity, shortwave_opacity)
    rows = jnp.stack([jnp.pad(v, (0, across - v.shape[0])) for v in vectors])
    rows = jnp.pad(rows, ((0, 8 - len(vectors)), (0, 0)))
    inverse, matrix, absorbed = call(
        part(tables_kernel, levels), [(padded, across)] * 3, rows
    )
    global_row = lax.axis_index("grp") * across + jnp.arange(across)
    latitude = ((global_row.astype(F32) + 0.5) / (across * groups) - 0.5) * (math.pi / 2)
    cosine = jnp.cos(latitude - 0.4)[None, :]

    forcing = forcing_vector.reshape(flat)
    weights = shift_weights.reshape(flat)
    field = (points, padded, across)
    message = (blocks, MESSAGE_ROWS, across)
    residual, smooth, message = call(
        part(smooth_kernel, levels, tiles, groups, swap),
        [field, field, message],
        kelvin,
        forcing,
        weights,
        inverse,
        matrix,
        absorbed,
        cosine,
    )
    tile, side = (padded, across), (3, padded, across)
    (rim,) = call(part(rim_kernel, levels), [tile], smooth, weights)
    inner, outer, *packed = call(
        part(side_kernel, levels, swap), [side, side] + [field] * swap, smooth, weights, rim
    )
    received = gather(message)

    def inner_pairs(size):
        return [(i, i ^ 1) for i in range(size) if i ^ 1 < size]

    def outer_pairs(size, around):
        pairs = [(i, (i + 1) % size) for i in range(1, size, 2) if around or i + 1 < size]
        return pairs + [(j, i) for i, j in pairs]

    inner = lax.ppermute(inner, "tile", inner_pairs(tiles))
    outer = lax.ppermute(outer, "tile", outer_pairs(tiles, True))
    low = lax.ppermute(rim, "grp", inner_pairs(groups))
    high = lax.ppermute(rim, "grp", outer_pairs(groups, False))
    steps, coarse = call(
        part(coarse_kernel, levels, points, tiles, groups),
        [(saved_rows(tiles, groups), lanes), (1, lanes)],
        received,
    )
    second, message = call(
        part(second_kernel, levels, tiles, groups),
        [field, (blocks, LAST_ROWS, across)],
        received,
        inner,
        outer,
        low,
        high,
        rim,
        smooth,
        residual,
        weights,
        inverse,
        coarse,
    )
    received = gather(message)
    parts = []
    if swap:
        parts = list(
            call(send_kernel, [(2, padded, across)] * tiles, packed[0], second, scratch=[field])
        )
        for k in range(1, tiles):
            parts[k] = lax.ppermute(parts[k], "tile", [(i, i ^ k) for i in range(tiles)])
    solution_field, state = call(
        part(final_kernel, levels, tiles, groups, swap),
        [flat, flat if swap else field],
        received,
        steps,
        coarse,
        smooth,
        second,
        *parts,
        scratch=[field] * swap,
    )
    if not swap:
        state = state[:, :levels].reshape(points, levels, tiles, width).transpose(2, 1, 0, 3)
        state = to_tiles(state).transpose(2, 1, 0, 3)
    shape = (levels, points, across)
    return solution_field.reshape(shape), state.reshape(shape)


def solution(mesh):
    return jax.shard_map(
        per_device,
        mesh=mesh,
        in_specs=(
            P(None, "tile", "grp"),
            P(None, "tile", "grp"),
            P(),
            P(None, None, ("tile", "grp")),
            P(),
            P(),
        ),
        out_specs=(P(None, "tile", "grp"), P(None, None, ("tile", "grp"))),
        check_vma=False,
    )
```

```python
import math

import jax
import jax.numpy as jnp
from jax import lax
from jax.experimental import pallas as pl
from jax.experimental.pallas import tpu as pltpu
from jax.sharding import PartitionSpec as P

F32 = jnp.float32
HIGHEST = lax.Precision.HIGHEST
MESSAGE_ROWS = 4
LAST_ROWS = 8
VMEM = pl.BlockSpec(memory_space=pltpu.VMEM)
HBM = pl.BlockSpec(memory_space=pltpu.HBM)


def iota(shape, dim):
    return lax.broadcasted_iota(jnp.int32, shape, dim)


def turn(value, shift, axis=1):
    shift = shift % value.shape[axis]
    return pltpu.roll(value, shift, axis) if shift else value


def total(value):
    return jnp.sum(value, axis=(0, 1), keepdims=True)


def call(kernel, outs, *args, scratch=(), copies=0):
    return pl.pallas_call(
        kernel,
        out_shape=[jax.ShapeDtypeStruct(shape, F32) for shape in outs],
        in_specs=[HBM if copies else VMEM] * len(args),
        out_specs=[VMEM] * len(outs),
        scratch_shapes=[pltpu.VMEM(shape, F32) for shape in scratch]
        + [pltpu.SemaphoreType.DMA((copies,))] * bool(copies),
        compiler_params=pltpu.CompilerParams(vmem_limit_bytes=32 * 1024 * 1024),
    )(*args)


def load_columns(ref, points, levels, padded):
    tiles = []
    for i in range(points):
        tile = ref[pl.ds(i, levels, stride=points), :]
        if padded > levels:
            tile = jnp.concatenate([tile, jnp.zeros((padded - levels, tile.shape[1]), F32)], axis=0)
        tiles.append(tile)
    return tiles


def store_columns(ref, tiles, levels):
    for i, tile in enumerate(tiles):
        ref[pl.ds(i, levels, stride=len(tiles)), :] = tile[:levels]


def swap_groups(tiles):
    count, lanes = len(tiles), tiles[0].shape[1]
    width = lanes // count
    group = iota(tiles[0].shape, 1) // width
    tiles = list(tiles)
    step = count // 2
    while step:
        low = (group & step) == 0
        for j in range(count):
            if j & step == 0:
                a, b = tiles[j], tiles[j + step]
                tiles[j] = jnp.where(low, a, turn(b, step * width))
                tiles[j + step] = jnp.where(low, turn(a, -step * width), b)
        step //= 2
    return tiles


def pack_kernel(levels, x_ref, *out_refs):
    *out_refs, packed_ref = out_refs
    points, padded, _ = packed_ref.shape
    for s, tile in enumerate(swap_groups(load_columns(x_ref, points, levels, padded))):
        packed_ref[s] = tile
    tile = lax.axis_index("tile")
    for k, out_ref in enumerate(out_refs):
        out_ref[...] = packed_ref[tile ^ k]


def tables_kernel(levels, *refs):
    *vector_refs, inverse_ref, matrix_ref, absorbed_ref = refs[:6]
    *buffer_refs, sems = refs[6:]
    copies = [
        pltpu.make_async_copy(vector_ref, buffer_ref, sems.at[n])
        for n, (vector_ref, buffer_ref) in enumerate(zip(vector_refs, buffer_refs))
    ]
    for copy in copies:
        copy.start()
    for copy in copies:
        copy.wait()
    shape = inverse_ref.shape
    sub, lane = iota(shape, 0), iota(shape, 1)

    def column(row, mask):
        return jnp.broadcast_to(jnp.sum(jnp.where(mask, row, 0.0), axis=1, keepdims=True), shape)

    link, thermal, solar = [
        jnp.concatenate([ref[...], jnp.zeros((1, shape[1] - ref.shape[1]), F32)], axis=1)
        for ref in buffer_refs
    ]
    lower = column(link, lane == sub - 1)
    upper = column(link, lane == sub)
    diagonal = 4.0 + lower + upper
    lower, upper = -lower, -upper
    result = jnp.where(lane == sub, 1.0, 0.0).astype(F32)
    step = 1
    while step < levels:
        inverse = 1.0 / diagonal
        a = -lower * turn(inverse, step, 0)
        c = -upper * turn(inverse, -step, 0)
        diagonal = diagonal + a * turn(upper, step, 0) + c * turn(lower, -step, 0)
        result = result + a * turn(result, step, 0) + c * turn(result, -step, 0)
        lower, upper = a * turn(lower, step, 0), c * turn(upper, -step, 0)
        step *= 2
    valid = (sub < levels) & (lane < levels)
    inverse_ref[...] = jnp.where(valid, result / diagonal, 0.0)

    own = column(thermal, lane == sub)
    top_column = column(thermal, lane < sub)
    bottom_column = column(thermal, lane <= sub)
    top_row = jnp.sum(jnp.where(sub < lane, own, 0.0), axis=0, keepdims=True)
    bottom_row = jnp.sum(jnp.where(sub <= lane, own, 0.0), axis=0, keepdims=True)
    whole = jnp.sum(thermal, axis=1, keepdims=True)
    emitted = 1.0 - jnp.exp(-thermal)

    def decay(mask, gap):
        return jnp.where(mask, jnp.exp(-jnp.where(mask, gap, 0.0)), 0.0)

    below, above = lane < sub, lane > sub
    matrix = decay(below, top_column - bottom_row) - decay(below, bottom_column - bottom_row)
    matrix = matrix + decay(above, top_row - bottom_column) - decay(above, top_row - top_column)
    matrix = (matrix - jnp.where(lane == sub, 2.0, 0.0)) * emitted
    surface = (lane == levels - 1) & (sub < levels)
    matrix = matrix + decay(surface, whole - bottom_column) - decay(surface, whole - top_column)
    matrix_ref[...] = jnp.where(valid, matrix, 0.0)
    entering = column(solar, lane < sub)
    leaving = column(solar, lane <= sub)
    absorbed = 10.0 * (jnp.exp(-entering) - jnp.exp(-leaving))
    absorbed_ref[...] = jnp.where(sub < levels, absorbed, 0.0)


def scalars_row(values, lanes):
    count = len(values)
    padded = -(-count // 8) * 8
    rows = [jnp.sum(value, axis=0, keepdims=True) for value in values]
    rows += [jnp.zeros_like(rows[0])] * (padded - count)
    sums = jnp.sum(jnp.concatenate(rows, axis=0), axis=1, keepdims=True)
    shape = (padded, lanes)
    spread = jnp.where(iota(shape, 0) == iota(shape, 1), sums, 0.0)
    return jnp.sum(spread, axis=0, keepdims=True)


def fold(tile):
    parts = [tile[8 * j : 8 * j + 8] for j in range(tile.shape[0] // 8)]
    while len(parts) > 1:
        parts = [a + b for a, b in zip(parts[::2], parts[1::2])] + parts[len(parts) // 2 * 2 :]
    return parts[0]


def add_all(parts):
    parts = list(parts)
    while len(parts) > 1:
        parts = [a + b for a, b in zip(parts[::2], parts[1::2])] + parts[len(parts) // 2 * 2 :]
    return parts[0]


def dot(matrix, tiles):
    across = tiles[0].shape[1]
    field = jnp.concatenate(tiles, axis=1)
    field = jnp.dot(matrix, field, precision=HIGHEST, preferred_element_type=F32)
    return [field[:, i * across : (i + 1) * across] for i in range(len(tiles))]


def prepare_kernel(
    levels,
    forcing_ref,
    weight_ref,
    inverse_ref,
    matrix_ref,
    absorbed_ref,
    cosine_ref,
    forced_ref,
    weight_out_ref,
    base_ref,
    matrices_ref,
    rows_ref,
    unit_ref,
):
    points, padded, across = forced_ref.shape
    inverse = inverse_ref[:, :padded]
    sun = absorbed_ref[...] * cosine_ref[...]
    forced = [tile + sun for tile in load_columns(forcing_ref, points, levels, padded)]
    for i, tile in enumerate(dot(inverse, forced)):
        forced_ref[i] = forced[i]
        base_ref[i] = tile
    weight = load_columns(weight_ref, points, levels, padded)
    for i, tile in enumerate(weight):
        weight_out_ref[i] = tile
    matrices_ref[0:padded] = matrix_ref[...]
    matrices_ref[padded:] = dot(inverse, [matrix_ref[...]])[0]
    unit_ref[...] = jnp.broadcast_to(
        jnp.sum(inverse_ref[...], axis=1, keepdims=True), unit_ref.shape
    )
    rows_ref[0:8] = add_all([fold(tile) for tile in weight])
    solar = jnp.sum(fold(sun), axis=0, keepdims=True)
    rows_ref[8:16] = jnp.broadcast_to(solar, (8, across))


def smooth_kernel(levels, tiles, groups, swap, *refs):
    *kelvin_refs, forced_ref, weight_ref, base_ref, matrices_ref, rows_ref, unit_ref = refs[: -3 - swap]
    residual_ref, smooth_ref, message_ref = refs[-3 - swap : len(refs) - swap]
    points, padded, across = residual_ref.shape
    if swap:
        scratch_ref = refs[-1]
        tile = lax.axis_index("tile")
        for k, part_ref in enumerate(kelvin_refs):
            scratch_ref[tile ^ k] = part_ref[...]
        kelvin = swap_groups([scratch_ref[i] for i in range(points)])
    else:
        kelvin = [kelvin_refs[0][i] for i in range(points)]
    squares = [tile * tile for tile in kelvin]
    both = dot(matrices_ref[:, :padded], [tile * tile for tile in squares])
    real = iota((padded, across), 0) < levels
    solar, unit = rows_ref[8:9, :], unit_ref[...]
    residual, smooth = [], []
    for i in range(points):
        heat = both[i][:padded]
        mean = (jnp.sum(fold(heat), axis=0, keepdims=True) + solar) * (1.0 / levels)
        residual.append(forced_ref[i] + jnp.where(real, heat - mean, 0.0))
        smooth.append(base_ref[i] + (both[i][padded:] - unit * mean))
        residual_ref[i] = residual[i]
        smooth_ref[i] = smooth[i]
    weight = [weight_ref[i] for i in range(points)]
    folded = [fold(tile) for tile in smooth]
    loss = add_all([fold(a * b) for a, b in zip(smooth, weight)])
    mass = rows_ref[0:8, :]
    every = add_all(folded)
    lane = iota(every.shape, 1)
    scalars = scalars_row(
        [
            add_all([fold(tile) for tile in residual]) - loss,
            folded[0],
            folded[-1],
            jnp.where(lane == 0, every, 0.0),
            jnp.where(lane == across - 1, every, 0.0),
            mass,
        ],
        across,
    )
    lane = iota((padded, across), 1)
    corner = jnp.where((lane == 0) | (lane == across - 1), smooth[0], turn(smooth[-1], 2))
    rows = jnp.concatenate([corner, jnp.zeros((across - padded, across), F32)], axis=0).T
    scalars = turn(scalars, padded)
    message_ref[...] = jnp.zeros(message_ref.shape, F32)
    message_ref[:, 0, :] = jnp.broadcast_to(scalars, (message_ref.shape[0], across))
    corners = (0, 2, across - 1, 1)
    for place, corner in zip(neighbours(tiles, groups)[5:], corners):
        message_ref[pl.ds(place, 1), 0, :] = rows[corner : corner + 1] + scalars


def rim_kernel(smooth_ref, weight_ref, rim_ref):
    points, padded, across = smooth_ref.shape
    stride = across // points
    lane = iota((padded, across), 1)
    rim = jnp.zeros((padded, across), F32)
    for i in range(points):
        place = (lane - stride * i + 2) & (across - 1)
        rim = jnp.where(place < 4, turn(smooth_ref[i], stride * i), rim)
        rim = jnp.where((place == 5) | (place == 6), turn(weight_ref[i], stride * i + 4), rim)
    rim_ref[...] = rim


def side_kernel(swap, smooth_ref, weight_ref, _, inner_ref, outer_ref, *packed_ref):
    points = smooth_ref.shape[0]
    even = lax.rem(lax.axis_index("tile"), 2) == 0
    for j, place in enumerate((0, 1)):
        west, east = smooth_ref[place], smooth_ref[points - 2 + place]
        inner_ref[j] = jnp.where(even, east, west)
        outer_ref[j] = jnp.where(even, west, east)
    west, east = weight_ref[0], weight_ref[points - 1]
    inner_ref[2] = jnp.where(even, east, west)
    outer_ref[2] = jnp.where(even, west, east)
    if swap:
        for s, tile in enumerate(swap_groups([smooth_ref[i] for i in range(points)])):
            packed_ref[0][s] = tile


def send_kernel(smooth_ref, second_ref, *out_refs):
    *out_refs, packed_ref = out_refs
    points = second_ref.shape[0]
    for s, tile in enumerate(swap_groups([second_ref[i] for i in range(points)])):
        packed_ref[s] = tile
    tile = lax.axis_index("tile")
    for k, out_ref in enumerate(out_refs):
        out_ref[0] = smooth_ref[tile ^ k]
        out_ref[1] = packed_ref[tile ^ k]


def neighbours(tiles, groups):
    tile, group = lax.axis_index("tile"), lax.axis_index("grp")
    west, east = lax.rem(tile + tiles - 1, tiles), lax.rem(tile + 1, tiles)
    south, north = jnp.maximum(group - 1, 0), jnp.minimum(group + 1, groups - 1)
    pairs = [(tile, group), (west, group), (east, group), (tile, south), (tile, north)]
    pairs += [(west, south), (east, south), (west, north), (east, north)]
    return [x * groups + y for x, y in pairs]


def small_inverse(block):
    size = len(block)
    block = [list(row) for row in block]
    for k in range(size):
        pivot = 1.0 / block[k][k]
        row = [block[k][j] * pivot for j in range(size)]
        for i in range(size):
            if i != k:
                factor = block[i][k]
                for j in range(size):
                    if j != k:
                        block[i][j] = block[i][j] - factor * row[j]
                block[i][k] = -factor * pivot
        for j in range(size):
            block[k][j] = row[j]
        block[k][k] = pivot
    return block


def product(a, b):
    size = range(len(a))
    return [[add_all([a[i][k] * b[k][j] for k in size]) for j in size] for i in size]


def apply(a, v):
    size = range(len(a))
    return [add_all([a[i][k] * v[k] for k in size]) for i in size]


def flip(a):
    return [list(row) for row in zip(*a)]


def turn_block(a, shift):
    return [[turn(value, shift) for value in row] for row in a]


def with_diagonal(block, row_sums, beside):
    size = range(len(block))
    return [
        [
            row_sums[i] - add_all([block[i][k] for k in size if k != i] + beside[i]) if i == j else block[i][j]
            for j in size
        ]
        for i in size
    ]


def coarse_factor(mass, tiles, groups, x_face, y_face):
    zero = jnp.zeros_like(mass)
    size = range(groups)
    diagonal = [[zero - y_face if abs(i - j) == 1 else zero for i in size] for j in size]
    coupling = [[zero - x_face if i == j else zero for i in size] for j in size]
    row_sums = [turn(mass, -j) for j in size]
    diagonal = with_diagonal(diagonal, row_sums, [[zero - 2.0 * x_face]] * groups)
    steps = []
    step = 1
    while step < tiles:
        inverse = small_inverse(diagonal)
        shift = step * groups
        steps.append((inverse, coupling))
        left = product(coupling, turn_block(inverse, shift))
        low = product(left, flip(coupling))
        high = turn_block(product(flip(coupling), product(inverse, coupling)), -shift)
        row_sums = reduce_sums(inverse, coupling, row_sums, shift)
        diagonal = [[diagonal[i][j] - (low[i][j] + high[i][j]) for j in size] for i in size]
        coupling = [[-v for v in row] for row in product(left, turn_block(coupling, shift))]
        step *= 2
        beside = [
            [add_all(coupling[i]), turn(add_all(flip(coupling)[i]), -step * groups)] for i in size
        ]
        diagonal = with_diagonal(diagonal, row_sums, beside)
    last = [[diagonal[i][j] + (coupling[i][j] + coupling[j][i]) for j in size] for i in size]
    last = with_diagonal(last, row_sums, [[]] * groups)
    return steps, small_inverse(last)


def reduce_sums(inverse, coupling, values, shift):
    scaled = apply(inverse, values)
    low = apply(coupling, [turn(v, shift) for v in scaled])
    high = [turn(v, -shift) for v in apply(flip(coupling), scaled)]
    return [v - (a + b) for v, a, b in zip(values, low, high)]


def coarse_solve(steps, last, sums, groups):
    values = [turn(sums, -j) for j in range(groups)]
    shift = groups
    for inverse, coupling in steps:
        values = reduce_sums(inverse, coupling, values, shift)
        shift *= 2
    values = apply(last, values)
    residue = iota(sums.shape, 1) % groups
    result = values[0]
    for j in range(1, groups):
        result = jnp.where(residue == j, turn(values[j], j), result)
    return result


def around(row, groups):
    residue = iota(row.shape, 1) % groups
    south = jnp.where(residue == 0, row, turn(row, 1))
    north = jnp.where(residue == groups - 1, row, turn(row, -1))
    return turn(row, groups), turn(row, -groups), south, north


def by_block(received):
    blocks, lanes = received.shape
    if blocks < lanes:
        received = jnp.concatenate([received] * (lanes // blocks), axis=0)
    return received.T


def save_steps(ref, steps, last):
    rows = [v for inverse, coupling in steps for block in (inverse, coupling) for row in block for v in row]
    rows += [v for row in last for v in row]
    for n, row in enumerate(rows):
        ref[n : n + 1, :] = row


def saved_rows(tiles, groups):
    steps = max(tiles - 1, 0).bit_length()
    return (2 * steps + 1) * groups * groups


def load_steps(ref, tiles, groups):
    place = 0
    blocks = []
    for _ in range(2 * max(tiles - 1, 0).bit_length() + 1):
        block = []
        for _ in range(groups):
            block.append([ref[place + j : place + j + 1, :] for j in range(groups)])
            place += groups
        blocks.append(block)
    return list(zip(blocks[:-1:2], blocks[1::2])), blocks[-1]


def coarse_kernel(levels, points, tiles, groups, received_ref, steps_ref, coarse_ref):
    padded = -(-levels // 8) * 8
    scalars = by_block(received_ref[:, 0, :])
    base, west, east, south, north, mass = [scalars[padded + j : padded + j + 1, :] for j in range(6)]
    residue = iota(base.shape, 1) % groups
    facing_south = jnp.where(residue == 0, south, turn(north, 1))
    facing_north = jnp.where(residue == groups - 1, north, turn(south, -1))
    sums = base + (
        (turn(east, groups) - west)
        + (turn(west, -groups) - east)
        + (facing_south - south)
        + (facing_north - north)
    )
    steps, last = coarse_factor(
        mass, tiles, groups, float(levels * received_ref.shape[2]), float(levels * points)
    )
    coarse = coarse_solve(steps, last, sums, groups)
    save_steps(steps_ref, steps, last)
    coarse_ref[...] = coarse


def second_kernel(
    levels,
    tiles,
    groups,
    received_ref,
    inner_ref,
    outer_ref,
    low_ref,
    high_ref,
    rim_ref,
    smooth_ref,
    residual_ref,
    weight_ref,
    inverse_ref,
    coarse_ref,
    second_ref,
    message_ref,
):
    points, padded, across = smooth_ref.shape
    blocks = tiles * groups
    stride = across // points
    group_index = lax.axis_index("grp")
    even_tile = lax.rem(lax.axis_index("tile"), 2) == 0
    even_group = lax.rem(group_index, 2) == 0
    at_south, at_north = group_index == 0, group_index == groups - 1

    coarse = coarse_ref[...]
    places = neighbours(tiles, groups)
    lane = iota(coarse.shape, 1)
    picked = [jnp.sum(jnp.where(lane == place, coarse, 0.0), axis=1, keepdims=True) for place in places]
    shape = (padded, across)
    real = iota(shape, 0) < levels
    own, e_west, e_east, e_south, e_north, e_sw, e_se, e_nw, e_ne = [
        jnp.where(real, value, 0.0) for value in picked
    ]

    corner_rows = [received_ref[pl.ds(place, 1), 0, :] for place in places[5:]]
    corner_rows = [jnp.where(iota(row.shape, 1) < padded, row, 0.0) for row in corner_rows]
    corners = jnp.concatenate(corner_rows + [jnp.zeros((across - 4, across), F32)], axis=0).T
    c_sw, c_se, c_nw, c_ne = [corners[:padded, j : j + 1] for j in range(4)]

    lane = iota(shape, 1)
    first, final = lane == 0, lane == across - 1

    def across_sum(tile, low, high):
        low = jnp.where(first, jnp.where(at_south, tile, low), turn(tile, 1))
        high = jnp.where(final, jnp.where(at_north, tile, high), turn(tile, -1))
        return low + high

    weight = [weight_ref[i] for i in range(points)]
    from_west = [jnp.where(even_tile, outer_ref[j], inner_ref[j]) for j in range(3)]
    from_east = [jnp.where(even_tile, inner_ref[j], outer_ref[j]) for j in range(3)]
    weight = from_west[2:] + weight + from_east[2:]
    field = from_west[:2] + [smooth_ref[i] for i in range(points)] + from_east[:2]

    def spread_image(tile_weight, here, ends, low, high):
        value = tile_weight * here
        if ends:
            value = value + add_all([here - there for there in ends])
        return value + jnp.where(first, here - low, jnp.where(final, here - high, 0.0))

    rim, low, high = rim_ref[...], low_ref[...], high_ref[...]
    from_south = jnp.where(even_group, high, low)
    from_north = jnp.where(even_group, low, high)
    lows = [c_sw] + [turn(from_south, 1 - stride * i) for i in range(points)] + [c_se]
    highs = [c_nw] + [turn(from_north, -1 - stride * i) for i in range(points)] + [c_ne]
    near = [(e_west, (own,), e_sw, e_nw)] + [(own, (), e_south, e_north)] * points
    near += [(e_east, (own,), e_se, e_ne)]
    near[1] = (own, (e_west,), e_south, e_north)
    near[points] = (own, (e_east,), e_south, e_north)
    image = [
        (field[i] + field[i + 2])
        + across_sum(field[i + 1], lows[i], highs[i])
        - (weight[i] * field[i + 1] + spread_image(weight[i], *near[i]))
        for i in range(points + 2)
    ]
    edge = stride * (points - 1)

    def ring_image(tile, step, here, west, east, west_lane, east_lane, c_west, c_east):
        rim_weight = turn(tile, -4)
        spread = rim_weight * here + (here - own)
        spread = spread + jnp.where(lane == west_lane, here - west, jnp.where(lane == east_lane, here - east, 0.0))
        return (
            jnp.where(lane == west_lane, c_west, turn(tile, stride))
            + jnp.where(lane == east_lane, c_east, turn(tile, -stride))
            + (turn(tile, step) + turn(rim, -step))
            - (rim_weight * tile + spread)
        )

    ring_south = ring_image(from_south, 1, e_south, e_sw, e_se, across - 1, edge - 1, c_sw, c_se)
    ring_north = ring_image(from_north, -1, e_north, e_nw, e_ne, 0, edge, c_nw, c_ne)
    inside = lane & (stride - 1)
    is_south, is_north = inside == stride - 1, inside == 0
    ring = jnp.where(is_south, ring_south, jnp.where(is_north, ring_north, 0.0))
    ring_field = jnp.where(is_south, from_south, from_north)
    second = dot(inverse_ref[:, :padded], image + [ring])
    ring = ring_field - second.pop()
    second = [field[i + 1] - tile for i, tile in enumerate(second)]

    names = ("image", "change", "residual")
    pairs = {}
    sides = {name: [] for name in names}
    left = []

    def collect(key, value):
        pairs.setdefault(key, []).append(fold(value))

    for i in range(points):
        tile = second[i + 1]
        second_ref[i] = tile
        again = (
            (second[i] + second[i + 2])
            + across_sum(tile, turn(ring, 1 - stride * i), turn(ring, -1 - stride * i))
            - weight[i + 1] * tile
        )
        residual = residual_ref[i]
        result = residual - image[i + 1]
        change = result - again
        left.append(fold(again + (result - 4.0 * tile)))
        heavy = weight[i + 1]
        collect("qq", result * result)
        collect("rq", residual * result)
        collect("qd", result * change)
        collect("dd", change * change)
        collect("rd", residual * change)
        collect("ww", heavy * heavy)
        sides.setdefault("weight", []).append(fold(heavy))
        for name, value in zip(names, (result, change, residual)):
            sides[name].append(fold(value))
            collect("w" + name, heavy * value)
    pairs = {key: add_all(value) for key, value in pairs.items()}
    lane = iota(pairs["qq"].shape, 1)
    out = [pairs[key] for key in ("qq", "rq", "qd", "dd", "rd")]
    for name in names + ("weight",):
        every = add_all(sides[name])
        out += [
            pairs["ww"] if name == "weight" else pairs["w" + name],
            sides[name][0],
            sides[name][-1],
            jnp.where(lane == 0, every, 0.0),
            jnp.where(lane == across - 1, every, 0.0),
        ]
    out.append(add_all(left))
    row = scalars_row(out, across)
    message_ref[...] = jnp.zeros(message_ref.shape, F32)
    message_ref[:, 0, :] = jnp.broadcast_to(row, (blocks, across))


def final_kernel(
    levels,
    tiles,
    groups,
    swap,
    received_ref,
    steps_ref,
    coarse_ref,
    smooth_ref,
    second_ref,
    field_ref,
    other_ref,
):
    points, padded, across = smooth_ref.shape
    blocks = tiles * groups
    rows = by_block(received_ref[:, 0, :])
    rows = [rows[j : j + 1, :] for j in range(26)]
    steps, last = load_steps(steps_ref, tiles, groups)
    coarse = coarse_solve(steps, last, rows[25], groups)
    jumps = [coarse - near for near in around(coarse, groups)]

    def against(part):
        return add_all([rows[part] * coarse] + [rows[part + 1 + j] * jumps[j] for j in range(4)])

    j_w, j_e, j_s, j_n = jumps
    x_face, y_face = float(levels * across), float(levels * points)
    weighted = add_all([rows[21 + j] * jumps[j] for j in range(4)])
    square = (
        coarse * (rows[20] * coarse + 2.0 * weighted)
        + x_face * (j_w * j_w + j_e * j_e)
        + y_face * (j_s * j_s + j_n * j_n)
        + (2.0 * levels) * ((j_w + j_e) * (j_s + j_n))
    )
    lane = iota(coarse.shape, 1)
    tile, group = lax.axis_index("tile"), lax.axis_index("grp")
    parts = [
        rows[0],
        rows[1],
        rows[2] + against(5),
        rows[3] + 2.0 * against(10) + square,
        rows[4] + against(15),
    ]
    parts = [jnp.where(lane < blocks, part, 0.0) for part in parts]
    parts += [jnp.zeros_like(coarse)] * 3
    sums = jnp.sum(jnp.concatenate(parts, axis=0), axis=1, keepdims=True)
    qq, rq, qv, vv, rv = [sums[j : j + 1, :] for j in range(5)]
    alpha = rq / qq
    beta = qv / qq
    kappa = (rv - alpha * qv) / (vv - beta * qv)
    scale = alpha - kappa * beta
    constant = scale * coarse_ref[...] + kappa * coarse
    others = tiles if swap else 1
    parts = [jnp.where(lane == (tile ^ k) * groups + group, constant, 0.0) for k in range(others)]
    parts += [jnp.zeros_like(coarse)] * (-others % 8)
    shifts = jnp.sum(jnp.concatenate(parts, axis=0), axis=1, keepdims=True)
    shifts = [shifts[k : k + 1, :] for k in range(others)]
    result = [scale * smooth_ref[i] + (kappa * second_ref[i] + shifts[0]) for i in range(points)]
    store_columns(field_ref, result, levels)
    if swap:
        rows = jnp.concatenate([scale, kappa] + shifts, axis=0)
        rows = jnp.concatenate([rows, jnp.zeros((other_ref.shape[0] - rows.shape[0], 1), F32)], axis=0)
        other_ref[...] = jnp.broadcast_to(rows, other_ref.shape)
    else:
        for i in range(points):
            other_ref[i] = result[i]


def state_kernel(levels, scalars_ref, *refs):
    *part_refs, state_ref, scratch_ref = refs
    tile = lax.axis_index("tile")
    scale, kappa = scalars_ref[0:1, :], scalars_ref[1:2, :]
    for k, part_ref in enumerate(part_refs):
        shift = scalars_ref[2 + k : 3 + k, :]
        scratch_ref[tile ^ k] = scale * part_ref[0] + (kappa * part_ref[1] + shift)
    store_columns(state_ref, swap_groups([scratch_ref[s] for s in range(len(part_refs))]), levels)


def per_device(
    forcing_vector,
    shift_weights,
    layer_link_factor,
    previous_kelvin_field,
    longwave_opacity,
    shortwave_opacity,
):
    tiles, groups = lax.axis_size("tile"), lax.axis_size("grp")
    levels, points, across = forcing_vector.shape
    padded = -(-levels // 8) * 8
    blocks = tiles * groups
    lanes = max(across, blocks)
    width = across // tiles
    swap = tiles == points
    flat = (levels * points, across)

    def to_tiles(value):
        return lax.all_to_all(value, "tile", split_axis=0, concat_axis=0, tiled=True)

    def gather(value):
        return lax.all_to_all(value, ("tile", "grp"), split_axis=0, concat_axis=0, tiled=True)

    def part(kernel, *settings):
        return lambda *refs: kernel(*settings, *refs)

    kelvin = previous_kelvin_field
    if swap:
        kelvin = list(call(
            part(pack_kernel, levels), [(padded, across)] * tiles, kelvin.reshape(flat), scratch=[(points, padded, across)]
        ))
        for k in range(1, tiles):
            kelvin[k] = lax.ppermute(kelvin[k], "tile", [(i, i ^ k) for i in range(tiles)])
    else:
        kelvin = kelvin.reshape(levels, points, tiles, width).transpose(2, 1, 0, 3)
        kelvin = to_tiles(kelvin).transpose(1, 2, 0, 3).reshape(points, levels, across)
        kelvin = [jnp.pad(kelvin, ((0, 0), (0, padded - levels), (0, 0)))]

    vectors = [v[None, :] for v in (layer_link_factor, longwave_opacity, shortwave_opacity)]
    inverse, matrix, absorbed = call(
        part(tables_kernel, levels),
        [(padded, across)] * 3,
        *vectors,
        scratch=[v.shape for v in vectors],
        copies=len(vectors),
    )
    global_row = lax.axis_index("grp") * across + jnp.arange(across)
    latitude = ((global_row.astype(F32) + 0.5) / (across * groups) - 0.5) * (math.pi / 2)
    cosine = jnp.cos(latitude - 0.4)[None, :]

    forcing = forcing_vector.reshape(flat)
    weights = shift_weights.reshape(flat)
    field = (points, padded, across)
    forced, weights, *prepared = call(
        part(prepare_kernel, levels),
        [field, field, field, (2 * padded, across), (16, across), (padded, across)],
        forcing,
        weights,
        inverse,
        matrix,
        absorbed,
        cosine,
    )
    prepared = [forced, weights, *prepared]
    message = (blocks, MESSAGE_ROWS, across)
    residual, smooth, message = call(
        part(smooth_kernel, levels, tiles, groups, swap),
        [field, field, message],
        *kelvin,
        *prepared,
        scratch=[field] * swap,
    )
    tile, side = (padded, across), (3, padded, across)
    (rim,) = call(rim_kernel, [tile], smooth, weights)
    inner, outer, *packed = call(
        part(side_kernel, swap), [side, side] + [field] * swap, smooth, weights, rim
    )
    received = gather(message)

    def inner_pairs(size):
        return [(i, i ^ 1) for i in range(size) if i ^ 1 < size]

    def outer_pairs(size, around):
        pairs = [(i, (i + 1) % size) for i in range(1, size, 2) if around or i + 1 < size]
        return pairs + [(j, i) for i, j in pairs]

    inner = lax.ppermute(inner, "tile", inner_pairs(tiles))
    outer = lax.ppermute(outer, "tile", outer_pairs(tiles, True))
    low = lax.ppermute(rim, "grp", inner_pairs(groups))
    high = lax.ppermute(rim, "grp", outer_pairs(groups, False))
    steps, coarse = call(
        part(coarse_kernel, levels, points, tiles, groups),
        [(saved_rows(tiles, groups), lanes), (1, lanes)],
        received,
    )
    second, message = call(
        part(second_kernel, levels, tiles, groups),
        [field, (blocks, LAST_ROWS, across)],
        received,
        inner,
        outer,
        low,
        high,
        rim,
        smooth,
        residual,
        weights,
        inverse,
        coarse,
    )
    received = gather(message)
    parts = []
    if swap:
        parts = list(
            call(send_kernel, [(2, padded, across)] * tiles, packed[0], second, scratch=[field])
        )
        for k in range(1, tiles):
            parts[k] = lax.ppermute(parts[k], "tile", [(i, i ^ k) for i in range(tiles)])
    solution_field, state = call(
        part(final_kernel, levels, tiles, groups, swap),
        [flat, (-(-(tiles + 2) // 8) * 8, across) if swap else field],
        received,
        steps,
        coarse,
        smooth,
        second,
    )
    if swap:
        (state,) = call(part(state_kernel, levels), [flat], state, *parts, scratch=[field])
    if not swap:
        state = state[:, :levels].reshape(points, levels, tiles, width).transpose(2, 1, 0, 3)
        state = to_tiles(state).transpose(2, 1, 0, 3)
    shape = (levels, points, across)
    return solution_field.reshape(shape), state.reshape(shape)


def solution(mesh):
    return jax.shard_map(
        per_device,
        mesh=mesh,
        in_specs=(
            P(None, "tile", "grp"),
            P(None, "tile", "grp"),
            P(),
            P(None, None, ("tile", "grp")),
            P(),
            P(),
        ),
        out_specs=(P(None, "tile", "grp"), P(None, None, ("tile", "grp"))),
        check_vma=False,
    )
```

```python
import math

import jax
import jax.numpy as jnp
from jax import lax
from jax.experimental import pallas as pl
from jax.experimental.pallas import tpu as pltpu
from jax.sharding import PartitionSpec as P

F32 = jnp.float32
HIGHEST = lax.Precision.HIGHEST
MESSAGE_ROWS = 4
LAST_ROWS = 8
VMEM = pl.BlockSpec(memory_space=pltpu.VMEM)
HBM = pl.BlockSpec(memory_space=pltpu.HBM)


def iota(shape, dim):
    return lax.broadcasted_iota(jnp.int32, shape, dim)


def turn(value, shift, axis=1):
    shift = shift % value.shape[axis]
    return pltpu.roll(value, shift, axis) if shift else value


def total(value):
    return jnp.sum(value, axis=(0, 1), keepdims=True)


def call(kernel, outs, *args, scratch=(), copies=0, sends=False):
    return pl.pallas_call(
        kernel,
        out_shape=[jax.ShapeDtypeStruct(shape, F32) for shape in outs],
        in_specs=[HBM if copies else VMEM] * len(args),
        out_specs=[HBM] * sends + [VMEM] * (len(outs) - sends),
        scratch_shapes=[pltpu.VMEM(shape, F32) for shape in [*scratch, *outs[:sends]]]
        + [pltpu.SemaphoreType.DMA((max(copies, 1),))] * bool(copies or sends),
        compiler_params=pltpu.CompilerParams(vmem_limit_bytes=32 * 1024 * 1024),
    )(*args)


def load_columns(ref, points, levels, padded):
    tiles = []
    for i in range(points):
        tile = ref[pl.ds(i, levels, stride=points), :]
        if padded > levels:
            tile = jnp.concatenate([tile, jnp.zeros((padded - levels, tile.shape[1]), F32)], axis=0)
        tiles.append(tile)
    return tiles


def store_columns(ref, tiles, levels):
    for i, tile in enumerate(tiles):
        ref[pl.ds(i, levels, stride=len(tiles)), :] = tile[:levels]


def swap_groups(tiles):
    count, lanes = len(tiles), tiles[0].shape[1]
    width = lanes // count
    group = iota(tiles[0].shape, 1) // width
    tiles = [turn(tile, i * width) for i, tile in enumerate(tiles)]
    step = 1
    while step < count:
        here = (group & step) == 0
        tiles = [jnp.where(here, tiles[u], tiles[(u + step) % count]) for u in range(count)]
        step *= 2
    return [turn(tiles[-s % count], -s * width) for s in range(count)]


def pack_kernel(levels, x_ref, packed_ref, near_ref):
    points, padded, _ = packed_ref.shape
    for s, tile in enumerate(swap_groups(load_columns(x_ref, points, levels, padded))):
        packed_ref[s] = tile
    other = 1 - (lax.axis_index("tile") & 1)
    for j in range(points // 2):
        near_ref[j] = packed_ref[2 * j + other]


def far_steps(tiles):
    return list(range(tiles - 2, 0, -2))


def relay_kernel(near_ref, packed_ref, *out_refs):
    tile = lax.axis_index("tile")
    for step, out_ref in zip(far_steps(packed_ref.shape[0]), out_refs):
        place = tile ^ step
        out_ref[0], out_ref[1] = packed_ref[place], near_ref[place >> 1]


def tables_kernel(levels, *refs):
    *vector_refs, inverse_ref, matrix_ref, absorbed_ref = refs[:6]
    *buffer_refs, sems = refs[6:]
    copies = [
        pltpu.make_async_copy(vector_ref, buffer_ref, sems.at[n])
        for n, (vector_ref, buffer_ref) in enumerate(zip(vector_refs, buffer_refs))
    ]
    for copy in copies:
        copy.start()
    for copy in copies:
        copy.wait()
    shape = inverse_ref.shape
    sub, lane = iota(shape, 0), iota(shape, 1)

    def column(row, mask):
        return jnp.broadcast_to(jnp.sum(jnp.where(mask, row, 0.0), axis=1, keepdims=True), shape)

    link, thermal, solar = [
        jnp.concatenate([ref[...], jnp.zeros((1, shape[1] - ref.shape[1]), F32)], axis=1)
        for ref in buffer_refs
    ]
    lower = column(link, lane == sub - 1)
    upper = column(link, lane == sub)
    diagonal = 4.0 + lower + upper
    lower, upper = -lower, -upper
    result = jnp.where(lane == sub, 1.0, 0.0).astype(F32)
    step = 1
    while step < levels:
        inverse = 1.0 / diagonal
        a = -lower * turn(inverse, step, 0)
        c = -upper * turn(inverse, -step, 0)
        diagonal = diagonal + a * turn(upper, step, 0) + c * turn(lower, -step, 0)
        result = result + a * turn(result, step, 0) + c * turn(result, -step, 0)
        lower, upper = a * turn(lower, step, 0), c * turn(upper, -step, 0)
        step *= 2
    valid = (sub < levels) & (lane < levels)
    inverse_ref[...] = jnp.where(valid, result / diagonal, 0.0)

    own = column(thermal, lane == sub)
    top_column = column(thermal, lane < sub)
    bottom_column = column(thermal, lane <= sub)
    top_row = jnp.sum(jnp.where(sub < lane, own, 0.0), axis=0, keepdims=True)
    bottom_row = jnp.sum(jnp.where(sub <= lane, own, 0.0), axis=0, keepdims=True)
    whole = jnp.sum(thermal, axis=1, keepdims=True)
    emitted = 1.0 - jnp.exp(-thermal)

    def decay(mask, gap):
        return jnp.where(mask, jnp.exp(-jnp.where(mask, gap, 0.0)), 0.0)

    below, above = lane < sub, lane > sub
    matrix = decay(below, top_column - bottom_row) - decay(below, bottom_column - bottom_row)
    matrix = matrix + decay(above, top_row - bottom_column) - decay(above, top_row - top_column)
    matrix = (matrix - jnp.where(lane == sub, 2.0, 0.0)) * emitted
    surface = (lane == levels - 1) & (sub < levels)
    matrix = matrix + decay(surface, whole - bottom_column) - decay(surface, whole - top_column)
    matrix_ref[...] = jnp.where(valid, matrix, 0.0)
    entering = column(solar, lane < sub)
    leaving = column(solar, lane <= sub)
    absorbed = 10.0 * (jnp.exp(-entering) - jnp.exp(-leaving))
    absorbed_ref[...] = jnp.where(sub < levels, absorbed, 0.0)


def scalars_row(values, lanes):
    count = len(values)
    padded = -(-count // 8) * 8
    rows = [jnp.sum(value, axis=0, keepdims=True) for value in values]
    rows += [jnp.zeros_like(rows[0])] * (padded - count)
    sums = jnp.sum(jnp.concatenate(rows, axis=0), axis=1, keepdims=True)
    shape = (padded, lanes)
    spread = jnp.where(iota(shape, 0) == iota(shape, 1), sums, 0.0)
    return jnp.sum(spread, axis=0, keepdims=True)


def fold(tile):
    parts = [tile[8 * j : 8 * j + 8] for j in range(tile.shape[0] // 8)]
    while len(parts) > 1:
        parts = [a + b for a, b in zip(parts[::2], parts[1::2])] + parts[len(parts) // 2 * 2 :]
    return parts[0]


def add_all(parts):
    parts = list(parts)
    while len(parts) > 1:
        parts = [a + b for a, b in zip(parts[::2], parts[1::2])] + parts[len(parts) // 2 * 2 :]
    return parts[0]


def dot(matrix, tiles):
    across = tiles[0].shape[1]
    field = jnp.concatenate(tiles, axis=1)
    field = jnp.dot(matrix, field, precision=HIGHEST, preferred_element_type=F32)
    return [field[:, i * across : (i + 1) * across] for i in range(len(tiles))]


def prepare_kernel(
    levels,
    forcing_ref,
    weight_ref,
    inverse_ref,
    matrix_ref,
    absorbed_ref,
    cosine_ref,
    forced_ref,
    weight_out_ref,
    base_ref,
    matrices_ref,
    rows_ref,
    unit_ref,
):
    points, padded, across = forced_ref.shape
    inverse = inverse_ref[:, :padded]
    sun = absorbed_ref[...] * cosine_ref[...]
    forced = [tile + sun for tile in load_columns(forcing_ref, points, levels, padded)]
    for i, tile in enumerate(dot(inverse, forced)):
        forced_ref[i] = forced[i]
        base_ref[i] = tile
    weight = load_columns(weight_ref, points, levels, padded)
    for i, tile in enumerate(weight):
        weight_out_ref[i] = tile
    matrices_ref[0:padded] = matrix_ref[...]
    matrices_ref[padded:] = dot(inverse, [matrix_ref[...]])[0]
    unit_ref[...] = jnp.broadcast_to(
        jnp.sum(inverse_ref[...], axis=1, keepdims=True), unit_ref.shape
    )
    rows_ref[0:8] = add_all([fold(tile) for tile in weight])
    solar = jnp.sum(fold(sun), axis=0, keepdims=True)
    rows_ref[8:16] = jnp.broadcast_to(solar, (8, across))


def smooth_kernel(levels, tiles, groups, swap, *refs):
    *refs, message_ref, message_sem = refs
    count = len(refs) - 6 - 2 * swap
    *kelvin_refs, forced_ref, weight_ref, base_ref, matrices_ref, rows_ref, unit_ref = refs[:count]
    sent_ref, residual_ref, smooth_ref, rim_ref, inner_ref, outer_ref, *refs = refs[count:]
    points, padded, across = residual_ref.shape
    if swap:
        state_ref, scratch_ref = refs
        tile = lax.axis_index("tile")
        packed_ref, near_ref, *far_refs = kelvin_refs
        scratch_ref[tile], scratch_ref[tile ^ 1] = packed_ref[tile], near_ref[tile >> 1]
        for step, far_ref in zip(far_steps(points), far_refs):
            scratch_ref[tile ^ step], scratch_ref[tile ^ (step + 1)] = far_ref[0], far_ref[1]
        kelvin = swap_groups([scratch_ref[i] for i in range(points)])
    else:
        kelvin = [kelvin_refs[0][i] for i in range(points)]
    squares = [tile * tile for tile in kelvin]
    both = dot(matrices_ref[:, :padded], [tile * tile for tile in squares])
    real = iota((padded, across), 0) < levels
    solar, unit = rows_ref[8:9, :], unit_ref[...]
    residual, smooth = [], []
    for i in range(points):
        heat = both[i][:padded]
        mean = (jnp.sum(fold(heat), axis=0, keepdims=True) + solar) * (1.0 / levels)
        residual.append(forced_ref[i] + jnp.where(real, heat - mean, 0.0))
        smooth.append(base_ref[i] + (both[i][padded:] - unit * mean))
        residual_ref[i] = residual[i]
        smooth_ref[i] = smooth[i]
    weight = [weight_ref[i] for i in range(points)]
    folded = [fold(tile) for tile in smooth]
    loss = add_all([fold(a * b) for a, b in zip(smooth, weight)])
    mass = rows_ref[0:8, :]
    every = add_all(folded)
    lane = iota(every.shape, 1)
    scalars = scalars_row(
        [
            add_all([fold(tile) for tile in residual]) - loss,
            folded[0],
            folded[-1],
            jnp.where(lane == 0, every, 0.0),
            jnp.where(lane == across - 1, every, 0.0),
            mass,
        ],
        across,
    )
    lane = iota((padded, across), 1)
    corner = jnp.where((lane == 0) | (lane == across - 1), smooth[0], turn(smooth[-1], 2))
    rows = jnp.concatenate([corner, jnp.zeros((across - padded, across), F32)], axis=0).T
    scalars = turn(scalars, padded)
    message_ref[...] = jnp.zeros(message_ref.shape, F32)
    message_ref[:, 0, :] = jnp.broadcast_to(scalars, (message_ref.shape[0], across))
    corners = (0, 2, across - 1, 1)
    for place, corner in zip(neighbours(tiles, groups)[5:], corners):
        message_ref[pl.ds(place, 1), 0, :] = rows[corner : corner + 1] + scalars
    send = pltpu.make_async_copy(message_ref, sent_ref, message_sem.at[0])
    send.start()

    stride = across // points
    rim = jnp.zeros((padded, across), F32)
    for i in range(points):
        place = (lane - stride * i + 2) & (across - 1)
        rim = jnp.where(place < 4, turn(smooth[i], stride * i), rim)
        rim = jnp.where((place == 5) | (place == 6), turn(weight[i], stride * i + 4), rim)
    rim_ref[...] = rim
    even = lax.rem(lax.axis_index("tile"), 2) == 0
    sides = zip((smooth[0], smooth[1], weight[0]), (smooth[-2], smooth[-1], weight[-1]))
    for j, (west, east) in enumerate(sides):
        inner_ref[j] = jnp.where(even, east, west)
        outer_ref[j] = jnp.where(even, west, east)
    if swap:
        for s, tile in enumerate(swap_groups(smooth)):
            state_ref[s] = tile
    send.wait()


def send_kernel(near_ref, smooth_ref, second_ref, *out_refs):
    tile = lax.axis_index("tile")
    for step, out_ref in zip(far_steps(smooth_ref.shape[0]), out_refs):
        place = tile ^ step
        out_ref[0], out_ref[1] = smooth_ref[place], second_ref[place]
        out_ref[2], out_ref[3] = near_ref[place >> 1, 0], near_ref[place >> 1, 1]


def neighbours(tiles, groups):
    tile, group = lax.axis_index("tile"), lax.axis_index("grp")
    west, east = lax.rem(tile + tiles - 1, tiles), lax.rem(tile + 1, tiles)
    south, north = jnp.maximum(group - 1, 0), jnp.minimum(group + 1, groups - 1)
    pairs = [(tile, group), (west, group), (east, group), (tile, south), (tile, north)]
    pairs += [(west, south), (east, south), (west, north), (east, north)]
    return [x * groups + y for x, y in pairs]


def small_inverse(block):
    size = len(block)
    block = [list(row) for row in block]
    for k in range(size):
        pivot = 1.0 / block[k][k]
        row = [block[k][j] * pivot for j in range(size)]
        for i in range(size):
            if i != k:
                factor = block[i][k]
                for j in range(size):
                    if j != k:
                        block[i][j] = block[i][j] - factor * row[j]
                block[i][k] = -factor * pivot
        for j in range(size):
            block[k][j] = row[j]
        block[k][k] = pivot
    return block


def product(a, b):
    size = range(len(a))
    return [[add_all([a[i][k] * b[k][j] for k in size]) for j in size] for i in size]


def apply(a, v):
    size = range(len(a))
    return [add_all([a[i][k] * v[k] for k in size]) for i in size]


def flip(a):
    return [list(row) for row in zip(*a)]


def turn_block(a, shift):
    return [[turn(value, shift) for value in row] for row in a]


def with_diagonal(block, row_sums, beside):
    size = range(len(block))
    return [
        [
            row_sums[i] - add_all([block[i][k] for k in size if k != i] + beside[i]) if i == j else block[i][j]
            for j in size
        ]
        for i in size
    ]


def coarse_factor(mass, tiles, groups, x_face, y_face):
    zero = jnp.zeros_like(mass)
    size = range(groups)
    diagonal = [[zero - y_face if abs(i - j) == 1 else zero for i in size] for j in size]
    coupling = [[zero - x_face if i == j else zero for i in size] for j in size]
    row_sums = [turn(mass, -j) for j in size]
    diagonal = with_diagonal(diagonal, row_sums, [[zero - 2.0 * x_face]] * groups)
    steps = []
    step = 1
    while step < tiles:
        inverse = small_inverse(diagonal)
        shift = step * groups
        steps.append((inverse, coupling))
        left = product(coupling, turn_block(inverse, shift))
        low = product(left, flip(coupling))
        high = turn_block(product(flip(coupling), product(inverse, coupling)), -shift)
        row_sums = reduce_sums(inverse, coupling, row_sums, shift)
        diagonal = [[diagonal[i][j] - (low[i][j] + high[i][j]) for j in size] for i in size]
        coupling = [[-v for v in row] for row in product(left, turn_block(coupling, shift))]
        step *= 2
        beside = [
            [add_all(coupling[i]), turn(add_all(flip(coupling)[i]), -step * groups)] for i in size
        ]
        diagonal = with_diagonal(diagonal, row_sums, beside)
    last = [[diagonal[i][j] + (coupling[i][j] + coupling[j][i]) for j in size] for i in size]
    last = with_diagonal(last, row_sums, [[]] * groups)
    return steps, small_inverse(last)


def reduce_sums(inverse, coupling, values, shift):
    scaled = apply(inverse, values)
    low = apply(coupling, [turn(v, shift) for v in scaled])
    high = [turn(v, -shift) for v in apply(flip(coupling), scaled)]
    return [v - (a + b) for v, a, b in zip(values, low, high)]


def coarse_solve(steps, last, sums, groups):
    values = [turn(sums, -j) for j in range(groups)]
    shift = groups
    for inverse, coupling in steps:
        values = reduce_sums(inverse, coupling, values, shift)
        shift *= 2
    values = apply(last, values)
    residue = iota(sums.shape, 1) % groups
    result = values[0]
    for j in range(1, groups):
        result = jnp.where(residue == j, turn(values[j], j), result)
    return result


def around(row, groups):
    residue = iota(row.shape, 1) % groups
    south = jnp.where(residue == 0, row, turn(row, 1))
    north = jnp.where(residue == groups - 1, row, turn(row, -1))
    return turn(row, groups), turn(row, -groups), south, north


def by_block(received):
    blocks, lanes = received.shape
    if blocks < lanes:
        received = jnp.concatenate([received] * (lanes // blocks), axis=0)
    return received.T


def save_steps(ref, steps, last):
    rows = [v for inverse, coupling in steps for block in (inverse, coupling) for row in block for v in row]
    rows += [v for row in last for v in row]
    for n, row in enumerate(rows):
        ref[n : n + 1, :] = row


def saved_rows(tiles, groups):
    steps = max(tiles - 1, 0).bit_length()
    return (2 * steps + 1) * groups * groups


def load_steps(ref, tiles, groups):
    place = 0
    blocks = []
    for _ in range(2 * max(tiles - 1, 0).bit_length() + 1):
        block = []
        for _ in range(groups):
            block.append([ref[place + j : place + j + 1, :] for j in range(groups)])
            place += groups
        blocks.append(block)
    return list(zip(blocks[:-1:2], blocks[1::2])), blocks[-1]


def coarse_kernel(levels, points, tiles, groups, received_ref, steps_ref, coarse_ref):
    padded = -(-levels // 8) * 8
    scalars = by_block(received_ref[:, 0, :])
    base, west, east, south, north, mass = [scalars[padded + j : padded + j + 1, :] for j in range(6)]
    residue = iota(base.shape, 1) % groups
    facing_south = jnp.where(residue == 0, south, turn(north, 1))
    facing_north = jnp.where(residue == groups - 1, north, turn(south, -1))
    sums = base + (
        (turn(east, groups) - west)
        + (turn(west, -groups) - east)
        + (facing_south - south)
        + (facing_north - north)
    )
    steps, last = coarse_factor(
        mass, tiles, groups, float(levels * received_ref.shape[2]), float(levels * points)
    )
    coarse = coarse_solve(steps, last, sums, groups)
    save_steps(steps_ref, steps, last)
    coarse_ref[...] = coarse


def second_kernel(
    levels,
    tiles,
    groups,
    received_ref,
    inner_ref,
    outer_ref,
    low_ref,
    high_ref,
    rim_ref,
    smooth_ref,
    residual_ref,
    weight_ref,
    inverse_ref,
    coarse_ref,
    *refs,
):
    *refs, message_ref, message_sem = refs
    swap = len(refs) > 2
    if swap:
        packed_smooth_ref, sent_ref, second_ref, packed_ref, near_ref = refs
    else:
        sent_ref, second_ref = refs
    points, padded, across = smooth_ref.shape
    blocks = tiles * groups
    stride = across // points
    group_index = lax.axis_index("grp")
    even_tile = lax.rem(lax.axis_index("tile"), 2) == 0
    even_group = lax.rem(group_index, 2) == 0
    at_south, at_north = group_index == 0, group_index == groups - 1

    coarse = coarse_ref[...]
    places = neighbours(tiles, groups)
    lane = iota(coarse.shape, 1)
    picked = [jnp.sum(jnp.where(lane == place, coarse, 0.0), axis=1, keepdims=True) for place in places]
    shape = (padded, across)
    real = iota(shape, 0) < levels
    own, e_west, e_east, e_south, e_north, e_sw, e_se, e_nw, e_ne = [
        jnp.where(real, value, 0.0) for value in picked
    ]

    corner_rows = [received_ref[pl.ds(place, 1), 0, :] for place in places[5:]]
    corner_rows = [jnp.where(iota(row.shape, 1) < padded, row, 0.0) for row in corner_rows]
    corners = jnp.concatenate(corner_rows + [jnp.zeros((across - 4, across), F32)], axis=0).T
    c_sw, c_se, c_nw, c_ne = [corners[:padded, j : j + 1] for j in range(4)]

    lane = iota(shape, 1)
    first, final = lane == 0, lane == across - 1

    inside = lane & (stride - 1)
    is_south, is_north = inside == stride - 1, inside == 0
    outside = lane == jnp.where(at_south, 0, -1)
    outside = outside | (lane == jnp.where(at_north, across - 1, -1))

    def across_sum(tile, ends):
        ends = jnp.where(outside, tile, ends)
        return jnp.where(first, ends, turn(tile, 1)) + jnp.where(final, ends, turn(tile, -1))

    def tile_ends(south, north):
        both = jnp.where(is_north, turn(south, 1), turn(north, -1))
        return [turn(both, -stride * i) for i in range(points)]

    weight = [weight_ref[i] for i in range(points)]
    from_west = [jnp.where(even_tile, outer_ref[j], inner_ref[j]) for j in range(3)]
    from_east = [jnp.where(even_tile, inner_ref[j], outer_ref[j]) for j in range(3)]
    weight = from_west[2:] + weight + from_east[2:]
    field = from_west[:2] + [smooth_ref[i] for i in range(points)] + from_east[:2]

    rim, low, high = rim_ref[...], low_ref[...], high_ref[...]
    from_south = jnp.where(even_group, high, low)
    from_north = jnp.where(even_group, low, high)
    ends = [jnp.where(first, c_sw, c_nw), *tile_ends(from_south, from_north), jnp.where(first, c_se, c_ne)]

    def steps(here, low, high):
        return jnp.where(first, here - low, jnp.where(final, here - high, 0.0))

    here = [e_west] + [own] * points + [e_east]
    jumps = [steps(e_west, e_sw, e_nw) + (e_west - own)]
    jumps += [steps(own, e_south, e_north)] * points
    jumps += [steps(e_east, e_se, e_ne) + (e_east - own)]
    jumps[1] = jumps[1] + (own - e_west)
    jumps[points] = jumps[points] + (own - e_east)
    image = [
        (field[i] + field[i + 2])
        + across_sum(field[i + 1], ends[i])
        - (weight[i] * (field[i + 1] + here[i]) + jumps[i])
        for i in range(points + 2)
    ]
    edge = stride * (points - 1)

    def ring_image(tile, step, here, west, east, west_lane, east_lane, c_west, c_east):
        rim_weight = turn(tile, -4)
        spread = (here - own) + jnp.where(lane == west_lane, here - west, jnp.where(lane == east_lane, here - east, 0.0))
        return (
            jnp.where(lane == west_lane, c_west, turn(tile, stride))
            + jnp.where(lane == east_lane, c_east, turn(tile, -stride))
            + (turn(tile, step) + turn(rim, -step))
            - (rim_weight * (tile + here) + spread)
        )

    ring_south = ring_image(from_south, 1, e_south, e_sw, e_se, across - 1, edge - 1, c_sw, c_se)
    ring_north = ring_image(from_north, -1, e_north, e_nw, e_ne, 0, edge, c_nw, c_ne)
    ring = jnp.where(is_south, ring_south, jnp.where(is_north, ring_north, 0.0))
    ring_field = jnp.where(is_south, from_south, from_north)
    second = dot(inverse_ref[:, :padded], image + [ring])
    ring = ring_field - second.pop()
    ends = tile_ends(ring, ring)
    second = [field[i + 1] - tile for i, tile in enumerate(second)]

    names = ("image", "change", "residual")
    pairs = {}
    sides = {name: [] for name in names}
    left = []

    def collect(key, value):
        pairs.setdefault(key, []).append(fold(value))

    for i in range(points):
        tile = second[i + 1]
        second_ref[i] = tile
        again = (
            (second[i] + second[i + 2])
            + across_sum(tile, ends[i])
            - weight[i + 1] * tile
        )
        residual = residual_ref[i]
        result = residual - image[i + 1]
        change = result - again
        left.append(fold(again + (result - 4.0 * tile)))
        heavy = weight[i + 1]
        collect("qq", result * result)
        collect("rq", residual * result)
        collect("qd", result * change)
        collect("dd", change * change)
        collect("rd", residual * change)
        collect("ww", heavy * heavy)
        sides.setdefault("weight", []).append(fold(heavy))
        for name, value in zip(names, (result, change, residual)):
            sides[name].append(fold(value))
            collect("w" + name, heavy * value)
    pairs = {key: add_all(value) for key, value in pairs.items()}
    lane = iota(pairs["qq"].shape, 1)
    out = [pairs[key] for key in ("qq", "rq", "qd", "dd", "rd")]
    for name in names + ("weight",):
        every = add_all(sides[name])
        out += [
            pairs["ww"] if name == "weight" else pairs["w" + name],
            sides[name][0],
            sides[name][-1],
            jnp.where(lane == 0, every, 0.0),
            jnp.where(lane == across - 1, every, 0.0),
        ]
    out.append(add_all(left))
    row = scalars_row(out, across)
    message_ref[...] = jnp.zeros(message_ref.shape, F32)
    message_ref[:, 0, :] = jnp.broadcast_to(row, (blocks, across))
    send = pltpu.make_async_copy(message_ref, sent_ref, message_sem.at[0])
    send.start()
    if swap:
        for s, tile in enumerate(swap_groups(second[1 : points + 1])):
            packed_ref[s] = tile
        other = 1 - (lax.axis_index("tile") & 1)
        for j in range(points // 2):
            near_ref[j, 0] = packed_smooth_ref[2 * j + other]
            near_ref[j, 1] = packed_ref[2 * j + other]
    send.wait()


def final_kernel(
    levels,
    tiles,
    groups,
    swap,
    received_ref,
    steps_ref,
    coarse_ref,
    smooth_ref,
    second_ref,
    field_ref,
    other_ref,
):
    points, padded, across = smooth_ref.shape
    blocks = tiles * groups
    rows = by_block(received_ref[:, 0, :])
    rows = [rows[j : j + 1, :] for j in range(26)]
    steps, last = load_steps(steps_ref, tiles, groups)
    coarse = coarse_solve(steps, last, rows[25], groups)
    jumps = [coarse - near for near in around(coarse, groups)]

    def against(part):
        return add_all([rows[part] * coarse] + [rows[part + 1 + j] * jumps[j] for j in range(4)])

    j_w, j_e, j_s, j_n = jumps
    x_face, y_face = float(levels * across), float(levels * points)
    weighted = add_all([rows[21 + j] * jumps[j] for j in range(4)])
    square = (
        coarse * (rows[20] * coarse + 2.0 * weighted)
        + x_face * (j_w * j_w + j_e * j_e)
        + y_face * (j_s * j_s + j_n * j_n)
        + (2.0 * levels) * ((j_w + j_e) * (j_s + j_n))
    )
    lane = iota(coarse.shape, 1)
    tile, group = lax.axis_index("tile"), lax.axis_index("grp")
    parts = [
        rows[0],
        rows[1],
        rows[2] + against(5),
        rows[3] + 2.0 * against(10) + square,
        rows[4] + against(15),
    ]
    parts = [jnp.where(lane < blocks, part, 0.0) for part in parts]
    parts += [jnp.zeros_like(coarse)] * 3
    sums = jnp.sum(jnp.concatenate(parts, axis=0), axis=1, keepdims=True)
    qq, rq, qv, vv, rv = [sums[j : j + 1, :] for j in range(5)]
    alpha = rq / qq
    beta = qv / qq
    kappa = (rv - alpha * qv) / (vv - beta * qv)
    scale = alpha - kappa * beta
    constant = scale * coarse_ref[...] + kappa * coarse
    others = tiles if swap else 1
    parts = [jnp.where(lane == (tile ^ k) * groups + group, constant, 0.0) for k in range(others)]
    parts += [jnp.zeros_like(coarse)] * (-others % 8)
    shifts = jnp.sum(jnp.concatenate(parts, axis=0), axis=1, keepdims=True)
    shifts = [shifts[k : k + 1, :] for k in range(others)]
    result = [scale * smooth_ref[i] + (kappa * second_ref[i] + shifts[0]) for i in range(points)]
    store_columns(field_ref, result, levels)
    if swap:
        rows = jnp.concatenate([scale, kappa] + shifts, axis=0)
        rows = jnp.concatenate([rows, jnp.zeros((other_ref.shape[0] - rows.shape[0], 1), F32)], axis=0)
        other_ref[...] = jnp.broadcast_to(rows, other_ref.shape)
    else:
        for i in range(points):
            other_ref[i] = result[i]


def state_kernel(levels, scalars_ref, *refs):
    smooth_ref, second_ref, near_ref, *part_refs, state_ref, scratch_ref = refs
    tile = lax.axis_index("tile")
    scale, kappa = scalars_ref[0:1, :], scalars_ref[1:2, :]
    pairs = {0: (smooth_ref[tile], second_ref[tile]), 1: (near_ref[tile >> 1, 0], near_ref[tile >> 1, 1])}
    for step, part_ref in zip(far_steps(smooth_ref.shape[0]), part_refs):
        pairs[step] = (part_ref[0], part_ref[1])
        pairs[step + 1] = (part_ref[2], part_ref[3])
    for k, (smooth, second) in pairs.items():
        scratch_ref[tile ^ k] = scale * smooth + (kappa * second + scalars_ref[2 + k : 3 + k, :])
    store_columns(state_ref, swap_groups([scratch_ref[s] for s in range(len(pairs))]), levels)


def per_device(
    forcing_vector,
    shift_weights,
    layer_link_factor,
    previous_kelvin_field,
    longwave_opacity,
    shortwave_opacity,
):
    tiles, groups = lax.axis_size("tile"), lax.axis_size("grp")
    levels, points, across = forcing_vector.shape
    padded = -(-levels // 8) * 8
    blocks = tiles * groups
    lanes = max(across, blocks)
    width = across // tiles
    swap = tiles == points
    flat = (levels * points, across)
    field = (points, padded, across)

    def to_tiles(value):
        return lax.all_to_all(value, "tile", split_axis=0, concat_axis=0, tiled=True)

    def gather(value):
        return lax.all_to_all(value, ("tile", "grp"), split_axis=0, concat_axis=0, tiled=True)

    def part(kernel, *settings):
        return lambda *refs: kernel(*settings, *refs)

    kelvin = previous_kelvin_field
    if swap:
        near = (tiles // 2, padded, across)
        packed, near = call(part(pack_kernel, levels), [field, near], kelvin.reshape(flat))
        near = lax.ppermute(near, "tile", [(i, i ^ 1) for i in range(tiles)])
        far = call(relay_kernel, [(2, padded, across)] * (tiles // 2 - 1), near, packed)
        kelvin = [packed, near] + [
            lax.ppermute(value, "tile", [(i, i ^ step) for i in range(tiles)])
            for step, value in zip(far_steps(tiles), far)
        ]
    else:
        kelvin = kelvin.reshape(levels, points, tiles, width).transpose(2, 1, 0, 3)
        kelvin = to_tiles(kelvin).transpose(1, 2, 0, 3).reshape(points, levels, across)
        kelvin = jnp.pad(kelvin, ((0, 0), (0, padded - levels), (0, 0)))

    vectors = [v[None, :] for v in (layer_link_factor, longwave_opacity, shortwave_opacity)]
    inverse, matrix, absorbed = call(
        part(tables_kernel, levels),
        [(padded, across)] * 3,
        *vectors,
        scratch=[v.shape for v in vectors],
        copies=len(vectors),
    )
    global_row = lax.axis_index("grp") * across + jnp.arange(across)
    latitude = ((global_row.astype(F32) + 0.5) / (across * groups) - 0.5) * (math.pi / 2)
    cosine = jnp.cos(latitude - 0.4)[None, :]

    forcing = forcing_vector.reshape(flat)
    weights = shift_weights.reshape(flat)
    forced, weights, *prepared = call(
        part(prepare_kernel, levels),
        [field, field, field, (2 * padded, across), (16, across), (padded, across)],
        forcing,
        weights,
        inverse,
        matrix,
        absorbed,
        cosine,
    )
    prepared = [forced, weights, *prepared]
    message = (blocks, MESSAGE_ROWS, across)
    tile, side = (padded, across), (3, padded, across)
    message, residual, smooth, rim, inner, outer, *packed = call(
        part(smooth_kernel, levels, tiles, groups, swap),
        [message, field, field, tile, side, side] + [field] * swap,
        *(kelvin if swap else [kelvin]),
        *prepared,
        scratch=[field] * swap,
        sends=True,
    )
    received = gather(message)

    def inner_pairs(size):
        return [(i, i ^ 1) for i in range(size) if i ^ 1 < size]

    def outer_pairs(size, around):
        pairs = [(i, (i + 1) % size) for i in range(1, size, 2) if around or i + 1 < size]
        return pairs + [(j, i) for i, j in pairs]

    inner = lax.ppermute(inner, "tile", inner_pairs(tiles))
    outer = lax.ppermute(outer, "tile", outer_pairs(tiles, True))
    low = lax.ppermute(rim, "grp", inner_pairs(groups))
    high = lax.ppermute(rim, "grp", outer_pairs(groups, False))
    steps, coarse = call(
        part(coarse_kernel, levels, points, tiles, groups),
        [(saved_rows(tiles, groups), lanes), (1, lanes)],
        received,
    )
    near = (tiles // 2, 2, padded, across)
    message, second, *sent = call(
        part(second_kernel, levels, tiles, groups),
        [(blocks, LAST_ROWS, across), field] + [field, near] * swap,
        received,
        inner,
        outer,
        low,
        high,
        rim,
        smooth,
        residual,
        weights,
        inverse,
        coarse,
        *packed,
        sends=True,
    )
    received = gather(message)
    parts = []
    if swap:
        near = lax.ppermute(sent[1], "tile", inner_pairs(tiles))
        parts = [packed[0], sent[0], near]
        far = call(send_kernel, [(4, padded, across)] * (tiles // 2 - 1), near, packed[0], sent[0])
        for step, value in zip(far_steps(tiles), far):
            parts.append(lax.ppermute(value, "tile", [(i, i ^ step) for i in range(tiles)]))
    solution_field, state = call(
        part(final_kernel, levels, tiles, groups, swap),
        [flat, (-(-(tiles + 2) // 8) * 8, across) if swap else field],
        received,
        steps,
        coarse,
        smooth,
        second,
    )
    if swap:
        (state,) = call(part(state_kernel, levels), [flat], state, *parts, scratch=[field])
    if not swap:
        state = state[:, :levels].reshape(points, levels, tiles, width).transpose(2, 1, 0, 3)
        state = to_tiles(state).transpose(2, 1, 0, 3)
    shape = (levels, points, across)
    return solution_field.reshape(shape), state.reshape(shape)


def solution(mesh):
    return jax.shard_map(
        per_device,
        mesh=mesh,
        in_specs=(
            P(None, "tile", "grp"),
            P(None, "tile", "grp"),
            P(),
            P(None, None, ("tile", "grp")),
            P(),
            P(),
        ),
        out_specs=(P(None, "tile", "grp"), P(None, None, ("tile", "grp"))),
        check_vma=False,
    )
```

```python
import math

import jax
import jax.numpy as jnp
from jax import lax
from jax.experimental import pallas as pl
from jax.experimental.pallas import tpu as pltpu
from jax.sharding import PartitionSpec as P

F32 = jnp.float32
HIGHEST = lax.Precision.HIGHEST
MESSAGE_ROWS = 4
LAST_ROWS = 8
VMEM = pl.BlockSpec(memory_space=pltpu.VMEM)
HBM = pl.BlockSpec(memory_space=pltpu.HBM)


def iota(shape, dim):
    return lax.broadcasted_iota(jnp.int32, shape, dim)


def turn(value, shift, axis=1):
    shift = shift % value.shape[axis]
    return pltpu.roll(value, shift, axis) if shift else value


def total(value):
    return jnp.sum(value, axis=(0, 1), keepdims=True)


def call(kernel, outs, *args, scratch=(), copies=0, sends=False):
    return pl.pallas_call(
        kernel,
        out_shape=[jax.ShapeDtypeStruct(shape, F32) for shape in outs],
        in_specs=[HBM if copies else VMEM] * len(args),
        out_specs=[HBM] * sends + [VMEM] * (len(outs) - sends),
        scratch_shapes=[pltpu.VMEM(shape, F32) for shape in [*scratch, *outs[:sends]]]
        + [pltpu.SemaphoreType.DMA((max(copies, 1),))] * bool(copies or sends),
        compiler_params=pltpu.CompilerParams(vmem_limit_bytes=32 * 1024 * 1024),
    )(*args)


def load_columns(ref, points, levels, padded):
    tiles = []
    for i in range(points):
        tile = ref[pl.ds(i, levels, stride=points), :]
        if padded > levels:
            tile = jnp.concatenate([tile, jnp.zeros((padded - levels, tile.shape[1]), F32)], axis=0)
        tiles.append(tile)
    return tiles


def store_columns(ref, tiles, levels):
    for i, tile in enumerate(tiles):
        ref[pl.ds(i, levels, stride=len(tiles)), :] = tile[:levels]


def swap_groups(tiles):
    count, lanes = len(tiles), tiles[0].shape[1]
    width = lanes // count
    group = iota(tiles[0].shape, 1) // width
    tiles = [turn(tile, i * width) for i, tile in enumerate(tiles)]
    step = 1
    while step < count:
        here = (group & step) == 0
        tiles = [jnp.where(here, tiles[u], tiles[(u + step) % count]) for u in range(count)]
        step *= 2
    return [turn(tiles[-s % count], -s * width) for s in range(count)]


def pack_kernel(levels, x_ref, packed_ref, near_ref):
    points, padded, _ = packed_ref.shape
    for s, tile in enumerate(swap_groups(load_columns(x_ref, points, levels, padded))):
        packed_ref[s] = tile
    other = 1 - (lax.axis_index("tile") & 1)
    for j in range(points // 2):
        near_ref[j] = packed_ref[2 * j + other]


def far_steps(tiles):
    return list(range(tiles - 2, 0, -2))


def relay_kernel(near_ref, packed_ref, *out_refs):
    tile = lax.axis_index("tile")
    for step, out_ref in zip(far_steps(packed_ref.shape[0]), out_refs):
        place = tile ^ step
        out_ref[0], out_ref[1] = packed_ref[place], near_ref[place >> 1]


def tables_kernel(levels, *refs):
    *vector_refs, inverse_ref, matrix_ref, absorbed_ref = refs[:6]
    *buffer_refs, sems = refs[6:]
    copies = [
        pltpu.make_async_copy(vector_ref, buffer_ref, sems.at[n])
        for n, (vector_ref, buffer_ref) in enumerate(zip(vector_refs, buffer_refs))
    ]
    for copy in copies:
        copy.start()
    for copy in copies:
        copy.wait()
    shape = inverse_ref.shape
    sub, lane = iota(shape, 0), iota(shape, 1)

    def column(row, mask):
        return jnp.broadcast_to(jnp.sum(jnp.where(mask, row, 0.0), axis=1, keepdims=True), shape)

    link, thermal, solar = [
        jnp.concatenate([ref[...], jnp.zeros((1, shape[1] - ref.shape[1]), F32)], axis=1)
        for ref in buffer_refs
    ]
    lower = column(link, lane == sub - 1)
    upper = column(link, lane == sub)
    diagonal = 4.0 + lower + upper
    lower, upper = -lower, -upper
    result = jnp.where(lane == sub, 1.0, 0.0).astype(F32)
    step = 1
    while step < levels:
        inverse = 1.0 / diagonal
        a = -lower * turn(inverse, step, 0)
        c = -upper * turn(inverse, -step, 0)
        diagonal = diagonal + a * turn(upper, step, 0) + c * turn(lower, -step, 0)
        result = result + a * turn(result, step, 0) + c * turn(result, -step, 0)
        lower, upper = a * turn(lower, step, 0), c * turn(upper, -step, 0)
        step *= 2
    valid = (sub < levels) & (lane < levels)
    inverse_ref[...] = jnp.where(valid, result / diagonal, 0.0)

    own = column(thermal, lane == sub)
    top_column = column(thermal, lane < sub)
    bottom_column = column(thermal, lane <= sub)
    top_row = jnp.sum(jnp.where(sub < lane, own, 0.0), axis=0, keepdims=True)
    bottom_row = jnp.sum(jnp.where(sub <= lane, own, 0.0), axis=0, keepdims=True)
    whole = jnp.sum(thermal, axis=1, keepdims=True)
    emitted = 1.0 - jnp.exp(-thermal)

    def decay(mask, gap):
        return jnp.where(mask, jnp.exp(-jnp.where(mask, gap, 0.0)), 0.0)

    below, above = lane < sub, lane > sub
    matrix = decay(below, top_column - bottom_row) - decay(below, bottom_column - bottom_row)
    matrix = matrix + decay(above, top_row - bottom_column) - decay(above, top_row - top_column)
    matrix = (matrix - jnp.where(lane == sub, 2.0, 0.0)) * emitted
    surface = (lane == levels - 1) & (sub < levels)
    matrix = matrix + decay(surface, whole - bottom_column) - decay(surface, whole - top_column)
    matrix_ref[...] = jnp.where(valid, matrix, 0.0)
    entering = column(solar, lane < sub)
    leaving = column(solar, lane <= sub)
    absorbed = 10.0 * (jnp.exp(-entering) - jnp.exp(-leaving))
    absorbed_ref[...] = jnp.where(sub < levels, absorbed, 0.0)


def scalars_row(values, lanes):
    count = len(values)
    padded = -(-count // 8) * 8
    rows = [jnp.sum(value, axis=0, keepdims=True) for value in values]
    rows += [jnp.zeros_like(rows[0])] * (padded - count)
    sums = jnp.sum(jnp.concatenate(rows, axis=0), axis=1, keepdims=True)
    shape = (padded, lanes)
    spread = jnp.where(iota(shape, 0) == iota(shape, 1), sums, 0.0)
    return jnp.sum(spread, axis=0, keepdims=True)


def fold(tile):
    parts = [tile[8 * j : 8 * j + 8] for j in range(tile.shape[0] // 8)]
    while len(parts) > 1:
        parts = [a + b for a, b in zip(parts[::2], parts[1::2])] + parts[len(parts) // 2 * 2 :]
    return parts[0]


def add_all(parts):
    parts = list(parts)
    while len(parts) > 1:
        parts = [a + b for a, b in zip(parts[::2], parts[1::2])] + parts[len(parts) // 2 * 2 :]
    return parts[0]


def dot(matrix, tiles):
    across = tiles[0].shape[1]
    field = jnp.concatenate(tiles, axis=1)
    field = jnp.dot(matrix, field, precision=HIGHEST, preferred_element_type=F32)
    return [field[:, i * across : (i + 1) * across] for i in range(len(tiles))]


def prepare_kernel(
    levels,
    forcing_ref,
    weight_ref,
    inverse_ref,
    matrix_ref,
    absorbed_ref,
    cosine_ref,
    forced_ref,
    weight_out_ref,
    base_ref,
    matrices_ref,
    rows_ref,
    unit_ref,
):
    points, padded, across = forced_ref.shape
    inverse = inverse_ref[:, :padded]
    sun = absorbed_ref[...] * cosine_ref[...]
    forced = [tile + sun for tile in load_columns(forcing_ref, points, levels, padded)]
    for i, tile in enumerate(dot(inverse, forced)):
        forced_ref[i] = forced[i]
        base_ref[i] = tile
    weight = load_columns(weight_ref, points, levels, padded)
    for i, tile in enumerate(weight):
        weight_out_ref[i] = tile
    matrices_ref[0:padded] = matrix_ref[...]
    matrices_ref[padded:] = dot(inverse, [matrix_ref[...]])[0]
    unit_ref[...] = jnp.broadcast_to(
        jnp.sum(inverse_ref[...], axis=1, keepdims=True), unit_ref.shape
    )
    rows_ref[0:8] = add_all([fold(tile) for tile in weight])
    solar = jnp.sum(fold(sun), axis=0, keepdims=True)
    rows_ref[8:16] = jnp.broadcast_to(solar, (8, across))


def smooth_kernel(levels, tiles, groups, swap, *refs):
    *refs, message_ref, message_sem = refs
    count = len(refs) - 6 - 2 * swap
    *kelvin_refs, forced_ref, weight_ref, base_ref, matrices_ref, rows_ref, unit_ref = refs[:count]
    sent_ref, residual_ref, smooth_ref, rim_ref, inner_ref, outer_ref, *refs = refs[count:]
    points, padded, across = residual_ref.shape
    if swap:
        state_ref, scratch_ref = refs
        tile = lax.axis_index("tile")
        packed_ref, near_ref, *far_refs = kelvin_refs
        scratch_ref[tile], scratch_ref[tile ^ 1] = packed_ref[tile], near_ref[tile >> 1]
        for step, far_ref in zip(far_steps(points), far_refs):
            scratch_ref[tile ^ step], scratch_ref[tile ^ (step + 1)] = far_ref[0], far_ref[1]
        kelvin = swap_groups([scratch_ref[i] for i in range(points)])
    else:
        kelvin = [kelvin_refs[0][i] for i in range(points)]
    squares = [tile * tile for tile in kelvin]
    both = dot(matrices_ref[:, :padded], [tile * tile for tile in squares])
    real = iota((padded, across), 0) < levels
    solar, unit = rows_ref[8:9, :], unit_ref[...]
    residual, smooth = [], []
    for i in range(points):
        heat = both[i][:padded]
        mean = (jnp.sum(fold(heat), axis=0, keepdims=True) + solar) * (1.0 / levels)
        residual.append(forced_ref[i] + jnp.where(real, heat - mean, 0.0))
        smooth.append(base_ref[i] + (both[i][padded:] - unit * mean))
        residual_ref[i] = residual[i]
        smooth_ref[i] = smooth[i]
    weight = [weight_ref[i] for i in range(points)]
    folded = [fold(tile) for tile in smooth]
    loss = add_all([fold(a * b) for a, b in zip(smooth, weight)])
    mass = rows_ref[0:8, :]
    every = add_all(folded)
    lane = iota(every.shape, 1)
    scalars = scalars_row(
        [
            add_all([fold(tile) for tile in residual]) - loss,
            folded[0],
            folded[-1],
            jnp.where(lane == 0, every, 0.0),
            jnp.where(lane == across - 1, every, 0.0),
            mass,
        ],
        across,
    )
    lane = iota((padded, across), 1)
    corner = jnp.where((lane == 0) | (lane == across - 1), smooth[0], turn(smooth[-1], 2))
    rows = jnp.concatenate([corner, jnp.zeros((across - padded, across), F32)], axis=0).T
    scalars = turn(scalars, padded)
    message_ref[...] = jnp.zeros(message_ref.shape, F32)
    message_ref[:, 0, :] = jnp.broadcast_to(scalars, (message_ref.shape[0], across))
    corners = (0, 2, across - 1, 1)
    for place, corner in zip(neighbours(tiles, groups)[5:], corners):
        message_ref[pl.ds(place, 1), 0, :] = rows[corner : corner + 1] + scalars
    send = pltpu.make_async_copy(message_ref, sent_ref, message_sem.at[0])
    send.start()

    stride = across // points
    rim = jnp.zeros((padded, across), F32)
    for i in range(points):
        place = (lane - stride * i + 2) & (across - 1)
        rim = jnp.where(place < 4, turn(smooth[i], stride * i), rim)
        rim = jnp.where((place == 5) | (place == 6), turn(weight[i], stride * i + 4), rim)
    rim_ref[...] = rim
    even = lax.rem(lax.axis_index("tile"), 2) == 0
    sides = zip((smooth[0], smooth[1], weight[0]), (smooth[-2], smooth[-1], weight[-1]))
    for j, (west, east) in enumerate(sides):
        inner_ref[j] = jnp.where(even, east, west)
        outer_ref[j] = jnp.where(even, west, east)
    if swap:
        for s, tile in enumerate(swap_groups(smooth)):
            state_ref[s] = tile
    send.wait()


def send_kernel(near_ref, smooth_ref, second_ref, *out_refs):
    tile = lax.axis_index("tile")
    for step, out_ref in zip(far_steps(smooth_ref.shape[0]), out_refs):
        place = tile ^ step
        out_ref[0], out_ref[1] = smooth_ref[place], second_ref[place]
        out_ref[2], out_ref[3] = near_ref[place >> 1, 0], near_ref[place >> 1, 1]


def neighbours(tiles, groups):
    tile, group = lax.axis_index("tile"), lax.axis_index("grp")
    west, east = lax.rem(tile + tiles - 1, tiles), lax.rem(tile + 1, tiles)
    south, north = jnp.maximum(group - 1, 0), jnp.minimum(group + 1, groups - 1)
    pairs = [(tile, group), (west, group), (east, group), (tile, south), (tile, north)]
    pairs += [(west, south), (east, south), (west, north), (east, north)]
    return [x * groups + y for x, y in pairs]


def small_inverse(block):
    size = len(block)
    block = [list(row) for row in block]
    for k in range(size):
        pivot = 1.0 / block[k][k]
        row = [block[k][j] * pivot for j in range(size)]
        for i in range(size):
            if i != k:
                factor = block[i][k]
                for j in range(size):
                    if j != k:
                        block[i][j] = block[i][j] - factor * row[j]
                block[i][k] = -factor * pivot
        for j in range(size):
            block[k][j] = row[j]
        block[k][k] = pivot
    return block


def product(a, b):
    size = range(len(a))
    return [[add_all([a[i][k] * b[k][j] for k in size]) for j in size] for i in size]


def apply(a, v):
    size = range(len(a))
    return [add_all([a[i][k] * v[k] for k in size]) for i in size]


def flip(a):
    return [list(row) for row in zip(*a)]


def turn_block(a, shift):
    return [[turn(value, shift) for value in row] for row in a]


def with_diagonal(block, row_sums, beside):
    size = range(len(block))
    return [
        [
            row_sums[i] - add_all([block[i][k] for k in size if k != i] + beside[i]) if i == j else block[i][j]
            for j in size
        ]
        for i in size
    ]


def coarse_factor(mass, tiles, groups, x_face, y_face):
    zero = jnp.zeros_like(mass)
    size = range(groups)
    diagonal = [[zero - y_face if abs(i - j) == 1 else zero for i in size] for j in size]
    coupling = [[zero - x_face if i == j else zero for i in size] for j in size]
    row_sums = [turn(mass, -j) for j in size]
    diagonal = with_diagonal(diagonal, row_sums, [[zero - 2.0 * x_face]] * groups)
    steps = []
    step = 1
    while step < tiles:
        inverse = small_inverse(diagonal)
        shift = step * groups
        steps.append((inverse, coupling))
        left = product(coupling, turn_block(inverse, shift))
        low = product(left, flip(coupling))
        high = turn_block(product(flip(coupling), product(inverse, coupling)), -shift)
        row_sums = reduce_sums(inverse, coupling, row_sums, shift)
        diagonal = [[diagonal[i][j] - (low[i][j] + high[i][j]) for j in size] for i in size]
        coupling = [[-v for v in row] for row in product(left, turn_block(coupling, shift))]
        step *= 2
        beside = [
            [add_all(coupling[i]), turn(add_all(flip(coupling)[i]), -step * groups)] for i in size
        ]
        diagonal = with_diagonal(diagonal, row_sums, beside)
    last = [[diagonal[i][j] + (coupling[i][j] + coupling[j][i]) for j in size] for i in size]
    last = with_diagonal(last, row_sums, [[]] * groups)
    return steps, small_inverse(last)


def reduce_sums(inverse, coupling, values, shift):
    scaled = apply(inverse, values)
    low = apply(coupling, [turn(v, shift) for v in scaled])
    high = [turn(v, -shift) for v in apply(flip(coupling), scaled)]
    return [v - (a + b) for v, a, b in zip(values, low, high)]


def coarse_solve(steps, last, sums, groups):
    values = [turn(sums, -j) for j in range(groups)]
    shift = groups
    for inverse, coupling in steps:
        values = reduce_sums(inverse, coupling, values, shift)
        shift *= 2
    values = apply(last, values)
    residue = iota(sums.shape, 1) % groups
    result = values[0]
    for j in range(1, groups):
        result = jnp.where(residue == j, turn(values[j], j), result)
    return result


def around(row, groups):
    residue = iota(row.shape, 1) % groups
    south = jnp.where(residue == 0, row, turn(row, 1))
    north = jnp.where(residue == groups - 1, row, turn(row, -1))
    return turn(row, groups), turn(row, -groups), south, north


def by_block(received):
    blocks, lanes = received.shape
    if blocks < lanes:
        received = jnp.concatenate([received] * (lanes // blocks), axis=0)
    return received.T


def save_steps(ref, steps, last):
    rows = [v for inverse, coupling in steps for block in (inverse, coupling) for row in block for v in row]
    rows += [v for row in last for v in row]
    for n, row in enumerate(rows):
        ref[n : n + 1, :] = row


def saved_rows(tiles, groups):
    steps = max(tiles - 1, 0).bit_length()
    return (2 * steps + 1) * groups * groups


def load_steps(ref, tiles, groups):
    place = 0
    blocks = []
    for _ in range(2 * max(tiles - 1, 0).bit_length() + 1):
        block = []
        for _ in range(groups):
            block.append([ref[place + j : place + j + 1, :] for j in range(groups)])
            place += groups
        blocks.append(block)
    return list(zip(blocks[:-1:2], blocks[1::2])), blocks[-1]


def coarse_kernel(levels, points, tiles, groups, received_ref, steps_ref, coarse_ref):
    padded = -(-levels // 8) * 8
    scalars = by_block(received_ref[:, 0, :])
    base, west, east, south, north, mass = [scalars[padded + j : padded + j + 1, :] for j in range(6)]
    residue = iota(base.shape, 1) % groups
    facing_south = jnp.where(residue == 0, south, turn(north, 1))
    facing_north = jnp.where(residue == groups - 1, north, turn(south, -1))
    sums = base + (
        (turn(east, groups) - west)
        + (turn(west, -groups) - east)
        + (facing_south - south)
        + (facing_north - north)
    )
    steps, last = coarse_factor(
        mass, tiles, groups, float(levels * received_ref.shape[2]), float(levels * points)
    )
    coarse = coarse_solve(steps, last, sums, groups)
    save_steps(steps_ref, steps, last)
    coarse_ref[...] = coarse


def beyond(groups, lane, across, none=-1):
    group = lax.axis_index("grp")
    south = jnp.where(group == 0, 0, none)
    north = jnp.where(group == groups - 1, across - 1, none)
    return (lane == south) | (lane == north)


def inside_kernel(
    levels,
    tiles,
    groups,
    received_ref,
    coarse_ref,
    inner_ref,
    outer_ref,
    smooth_ref,
    weight_ref,
    inverse_ref,
    image_ref,
    second_ref,
    values_ref,
    corners_ref,
):
    points, padded, across = smooth_ref.shape
    coarse = coarse_ref[...]
    places = neighbours(tiles, groups)
    lane = iota(coarse.shape, 1)
    picked = [jnp.sum(jnp.where(lane == place, coarse, 0.0), axis=1, keepdims=True) for place in places]
    for j, value in enumerate(picked):
        values_ref[j : j + 1, :] = jnp.broadcast_to(value, (1, across))
    shape = (padded, across)
    real = iota(shape, 0) < levels
    own, e_west, e_east, e_south, e_north, e_sw, e_se, e_nw, e_ne = [
        jnp.where(real, value, 0.0) for value in picked
    ]

    corner_rows = [received_ref[pl.ds(place, 1), 0, :] for place in places[5:]]
    corner_rows = [jnp.where(iota(row.shape, 1) < padded, row, 0.0) for row in corner_rows]
    corners = jnp.concatenate(corner_rows + [jnp.zeros((across - 4, across), F32)], axis=0).T
    c_sw, c_se, c_nw, c_ne = [corners[:padded, j : j + 1] for j in range(4)]

    for j, corner in enumerate((c_sw, c_se, c_nw, c_ne)):
        corners_ref[j] = jnp.broadcast_to(corner, shape)

    lane = iota(shape, 1)
    first, final = lane == 0, lane == across - 1

    outside = beyond(groups, lane, across)

    def across_sum(tile, ends):
        ends = jnp.where(outside, tile, ends)
        return jnp.where(first, ends, turn(tile, 1)) + jnp.where(final, ends, turn(tile, -1))

    even_tile = lax.rem(lax.axis_index("tile"), 2) == 0
    weight = [weight_ref[i] for i in range(points)]
    from_west = [jnp.where(even_tile, outer_ref[j], inner_ref[j]) for j in range(3)]
    from_east = [jnp.where(even_tile, inner_ref[j], outer_ref[j]) for j in range(3)]
    weight = from_west[2:] + weight + from_east[2:]
    field = from_west[:2] + [smooth_ref[i] for i in range(points)] + from_east[:2]

    ends = [jnp.where(first, c_sw, c_nw), *[jnp.zeros(shape, F32)] * points, jnp.where(first, c_se, c_ne)]

    def steps(here, low, high):
        return jnp.where(first, here - low, jnp.where(final, here - high, 0.0))

    here = [e_west] + [own] * points + [e_east]
    jumps = [steps(e_west, e_sw, e_nw) + (e_west - own)]
    jumps += [steps(own, e_south, e_north)] * points
    jumps += [steps(e_east, e_se, e_ne) + (e_east - own)]
    jumps[1] = jumps[1] + (own - e_west)
    jumps[points] = jumps[points] + (own - e_east)
    image = [
        (field[i] + field[i + 2])
        + across_sum(field[i + 1], ends[i])
        - (weight[i] * (field[i + 1] + here[i]) + jumps[i])
        for i in range(points + 2)
    ]
    smoothed = dot(inverse_ref[:, :padded], image)
    for i in range(points + 2):
        image_ref[i] = image[i]
        second_ref[i] = field[i + 1] - smoothed[i]


def second_kernel(
    levels,
    groups,
    low_ref,
    high_ref,
    rim_ref,
    residual_ref,
    weight_ref,
    inverse_ref,
    image_ref,
    second_ref_in,
    values_ref,
    corners_ref,
    *refs,
):
    *refs, message_ref, message_sem = refs
    swap = len(refs) > 2
    if swap:
        packed_smooth_ref, sent_ref, second_ref, packed_ref, near_ref = refs
    else:
        sent_ref, second_ref = refs
    points, padded, across = residual_ref.shape
    blocks = message_ref.shape[0]
    stride = across // points
    even_group = lax.rem(lax.axis_index("grp"), 2) == 0

    shape = (padded, across)
    real = iota(shape, 0) < levels
    values = [values_ref[j : j + 1, :] for j in range(9)]
    own, e_west, e_east, e_south, e_north, e_sw, e_se, e_nw, e_ne = [
        jnp.where(real, value, 0.0) for value in values
    ]
    c_sw, c_se, c_nw, c_ne = [corners_ref[j] for j in range(4)]
    weight = [weight_ref[i] for i in range(points)]
    lane = iota(shape, 1)
    first, final = lane == 0, lane == across - 1
    outside = beyond(groups, lane, across)
    inside = lane & (stride - 1)
    is_south, is_north = inside == stride - 1, inside == 0
    rim, low, high = rim_ref[...], low_ref[...], high_ref[...]
    from_south = jnp.where(even_group, high, low)
    from_north = jnp.where(even_group, low, high)
    outer = beyond(groups, jnp.where(is_north, 0, jnp.where(is_south, across - 1, 1)), across)
    both = jnp.where(is_north, turn(from_south, 1), turn(from_north, -1))
    both = jnp.where((is_north | is_south) & jnp.logical_not(outer), both, 0.0)
    edge = stride * (points - 1)

    def ring_image(tile, step, here, west, east, west_lane, east_lane, c_west, c_east):
        rim_weight = turn(tile, -4)
        spread = (here - own) + jnp.where(lane == west_lane, here - west, jnp.where(lane == east_lane, here - east, 0.0))
        return (
            jnp.where(lane == west_lane, c_west, turn(tile, stride))
            + jnp.where(lane == east_lane, c_east, turn(tile, -stride))
            + (turn(tile, step) + turn(rim, -step))
            - (rim_weight * (tile + here) + spread)
        )

    ring_south = ring_image(from_south, 1, e_south, e_sw, e_se, across - 1, edge - 1, c_sw, c_se)
    ring_north = ring_image(from_north, -1, e_north, e_nw, e_ne, 0, edge, c_nw, c_ne)
    ring = jnp.where(is_south, ring_south, jnp.where(is_north, ring_north, 0.0))
    ring_field = jnp.where(is_south, from_south, from_north)
    ring, smoothed = dot(inverse_ref[:, :padded], [ring, both])
    ring = ring_field - ring
    second, image = [second_ref_in[0]], [None]
    ends = first | final
    for i in range(1, points + 1):
        shift = -stride * (i - 1)
        image.append(jnp.where(ends, image_ref[i] + turn(both, shift), image_ref[i]))
        second.append(jnp.where(ends, second_ref_in[i] - turn(smoothed, shift), second_ref_in[i]))
    second.append(second_ref_in[points + 1])
    both = jnp.where(is_north, turn(ring, 1), turn(ring, -1))

    names = ("image", "change", "residual")
    pairs = {}
    sides = {name: [] for name in names}
    left = []

    def collect(key, value):
        pairs.setdefault(key, []).append(fold(value))

    for i in range(points):
        tile = second[i + 1]
        second_ref[i] = tile
        ends = jnp.where(outside, tile, turn(both, -stride * i))
        again = (
            (second[i] + second[i + 2])
            + (jnp.where(first, ends, turn(tile, 1)) + jnp.where(final, ends, turn(tile, -1)))
            - weight[i] * tile
        )
        residual = residual_ref[i]
        result = residual - image[i + 1]
        change = result - again
        left.append(fold(again + (result - 4.0 * tile)))
        heavy = weight[i]
        collect("qq", result * result)
        collect("rq", residual * result)
        collect("qd", result * change)
        collect("dd", change * change)
        collect("rd", residual * change)
        collect("ww", heavy * heavy)
        sides.setdefault("weight", []).append(fold(heavy))
        for name, value in zip(names, (result, change, residual)):
            sides[name].append(fold(value))
            collect("w" + name, heavy * value)
    pairs = {key: add_all(value) for key, value in pairs.items()}
    lane = iota(pairs["qq"].shape, 1)
    out = [pairs[key] for key in ("qq", "rq", "qd", "dd", "rd")]
    for name in names + ("weight",):
        every = add_all(sides[name])
        out += [
            pairs["ww"] if name == "weight" else pairs["w" + name],
            sides[name][0],
            sides[name][-1],
            jnp.where(lane == 0, every, 0.0),
            jnp.where(lane == across - 1, every, 0.0),
        ]
    out.append(add_all(left))
    row = scalars_row(out, across)
    message_ref[...] = jnp.zeros(message_ref.shape, F32)
    message_ref[:, 0, :] = jnp.broadcast_to(row, (blocks, across))
    send = pltpu.make_async_copy(message_ref, sent_ref, message_sem.at[0])
    send.start()
    if swap:
        for s, tile in enumerate(swap_groups(second[1 : points + 1])):
            packed_ref[s] = tile
        other = 1 - (lax.axis_index("tile") & 1)
        for j in range(points // 2):
            near_ref[j, 0] = packed_smooth_ref[2 * j + other]
            near_ref[j, 1] = packed_ref[2 * j + other]
    send.wait()


def final_kernel(
    levels,
    tiles,
    groups,
    swap,
    received_ref,
    steps_ref,
    coarse_ref,
    smooth_ref,
    second_ref,
    field_ref,
    other_ref,
):
    points, padded, across = smooth_ref.shape
    blocks = tiles * groups
    rows = by_block(received_ref[:, 0, :])
    rows = [rows[j : j + 1, :] for j in range(26)]
    steps, last = load_steps(steps_ref, tiles, groups)
    coarse = coarse_solve(steps, last, rows[25], groups)
    jumps = [coarse - near for near in around(coarse, groups)]

    def against(part):
        return add_all([rows[part] * coarse] + [rows[part + 1 + j] * jumps[j] for j in range(4)])

    j_w, j_e, j_s, j_n = jumps
    x_face, y_face = float(levels * across), float(levels * points)
    weighted = add_all([rows[21 + j] * jumps[j] for j in range(4)])
    square = (
        coarse * (rows[20] * coarse + 2.0 * weighted)
        + x_face * (j_w * j_w + j_e * j_e)
        + y_face * (j_s * j_s + j_n * j_n)
        + (2.0 * levels) * ((j_w + j_e) * (j_s + j_n))
    )
    lane = iota(coarse.shape, 1)
    tile, group = lax.axis_index("tile"), lax.axis_index("grp")
    parts = [
        rows[0],
        rows[1],
        rows[2] + against(5),
        rows[3] + 2.0 * against(10) + square,
        rows[4] + against(15),
    ]
    parts = [jnp.where(lane < blocks, part, 0.0) for part in parts]
    parts += [jnp.zeros_like(coarse)] * 3
    sums = jnp.sum(jnp.concatenate(parts, axis=0), axis=1, keepdims=True)
    qq, rq, qv, vv, rv = [sums[j : j + 1, :] for j in range(5)]
    alpha = rq / qq
    beta = qv / qq
    kappa = (rv - alpha * qv) / (vv - beta * qv)
    scale = alpha - kappa * beta
    constant = scale * coarse_ref[...] + kappa * coarse
    others = tiles if swap else 1
    parts = [jnp.where(lane == (tile ^ k) * groups + group, constant, 0.0) for k in range(others)]
    parts += [jnp.zeros_like(coarse)] * (-others % 8)
    shifts = jnp.sum(jnp.concatenate(parts, axis=0), axis=1, keepdims=True)
    shifts = [shifts[k : k + 1, :] for k in range(others)]
    result = [scale * smooth_ref[i] + (kappa * second_ref[i] + shifts[0]) for i in range(points)]
    store_columns(field_ref, result, levels)
    if swap:
        rows = jnp.concatenate([scale, kappa] + shifts, axis=0)
        rows = jnp.concatenate([rows, jnp.zeros((other_ref.shape[0] - rows.shape[0], 1), F32)], axis=0)
        other_ref[...] = jnp.broadcast_to(rows, other_ref.shape)
    else:
        for i in range(points):
            other_ref[i] = result[i]


def state_kernel(levels, scalars_ref, *refs):
    smooth_ref, second_ref, near_ref, *part_refs, state_ref, scratch_ref = refs
    tile = lax.axis_index("tile")
    scale, kappa = scalars_ref[0:1, :], scalars_ref[1:2, :]
    pairs = {0: (smooth_ref[tile], second_ref[tile]), 1: (near_ref[tile >> 1, 0], near_ref[tile >> 1, 1])}
    for step, part_ref in zip(far_steps(smooth_ref.shape[0]), part_refs):
        pairs[step] = (part_ref[0], part_ref[1])
        pairs[step + 1] = (part_ref[2], part_ref[3])
    for k, (smooth, second) in pairs.items():
        scratch_ref[tile ^ k] = scale * smooth + (kappa * second + scalars_ref[2 + k : 3 + k, :])
    store_columns(state_ref, swap_groups([scratch_ref[s] for s in range(len(pairs))]), levels)


def per_device(
    forcing_vector,
    shift_weights,
    layer_link_factor,
    previous_kelvin_field,
    longwave_opacity,
    shortwave_opacity,
):
    tiles, groups = lax.axis_size("tile"), lax.axis_size("grp")
    levels, points, across = forcing_vector.shape
    padded = -(-levels // 8) * 8
    blocks = tiles * groups
    lanes = max(across, blocks)
    width = across // tiles
    swap = tiles == points
    flat = (levels * points, across)
    field = (points, padded, across)

    def to_tiles(value):
        return lax.all_to_all(value, "tile", split_axis=0, concat_axis=0, tiled=True)

    def gather(value):
        return lax.all_to_all(value, ("tile", "grp"), split_axis=0, concat_axis=0, tiled=True)

    def part(kernel, *settings):
        return lambda *refs: kernel(*settings, *refs)

    kelvin = previous_kelvin_field
    if swap:
        near = (tiles // 2, padded, across)
        packed, near = call(part(pack_kernel, levels), [field, near], kelvin.reshape(flat))
        near = lax.ppermute(near, "tile", [(i, i ^ 1) for i in range(tiles)])
        far = call(relay_kernel, [(2, padded, across)] * (tiles // 2 - 1), near, packed)
        kelvin = [packed, near] + [
            lax.ppermute(value, "tile", [(i, i ^ step) for i in range(tiles)])
            for step, value in zip(far_steps(tiles), far)
        ]
    else:
        kelvin = kelvin.reshape(levels, points, tiles, width).transpose(2, 1, 0, 3)
        kelvin = to_tiles(kelvin).transpose(1, 2, 0, 3).reshape(points, levels, across)
        kelvin = jnp.pad(kelvin, ((0, 0), (0, padded - levels), (0, 0)))

    vectors = [v[None, :] for v in (layer_link_factor, longwave_opacity, shortwave_opacity)]
    inverse, matrix, absorbed = call(
        part(tables_kernel, levels),
        [(padded, across)] * 3,
        *vectors,
        scratch=[v.shape for v in vectors],
        copies=len(vectors),
    )
    global_row = lax.axis_index("grp") * across + jnp.arange(across)
    latitude = ((global_row.astype(F32) + 0.5) / (across * groups) - 0.5) * (math.pi / 2)
    cosine = jnp.cos(latitude - 0.4)[None, :]

    forcing = forcing_vector.reshape(flat)
    weights = shift_weights.reshape(flat)
    forced, weights, *prepared = call(
        part(prepare_kernel, levels),
        [field, field, field, (2 * padded, across), (16, across), (padded, across)],
        forcing,
        weights,
        inverse,
        matrix,
        absorbed,
        cosine,
    )
    prepared = [forced, weights, *prepared]
    message = (blocks, MESSAGE_ROWS, across)
    tile, side = (padded, across), (3, padded, across)
    message, residual, smooth, rim, inner, outer, *packed = call(
        part(smooth_kernel, levels, tiles, groups, swap),
        [message, field, field, tile, side, side] + [field] * swap,
        *(kelvin if swap else [kelvin]),
        *prepared,
        scratch=[field] * swap,
        sends=True,
    )
    received = gather(message)

    def inner_pairs(size):
        return [(i, i ^ 1) for i in range(size) if i ^ 1 < size]

    def outer_pairs(size, around):
        pairs = [(i, (i + 1) % size) for i in range(1, size, 2) if around or i + 1 < size]
        return pairs + [(j, i) for i, j in pairs]

    inner = lax.ppermute(inner, "tile", inner_pairs(tiles))
    outer = lax.ppermute(outer, "tile", outer_pairs(tiles, True))
    low = lax.ppermute(rim, "grp", inner_pairs(groups))
    high = lax.ppermute(rim, "grp", outer_pairs(groups, False))
    wide = (points + 2, padded, across)
    steps, coarse = call(
        part(coarse_kernel, levels, points, tiles, groups),
        [(saved_rows(tiles, groups), lanes), (1, lanes)],
        received,
    )
    image, second, values, corners = call(
        part(inside_kernel, levels, tiles, groups),
        [wide, wide, (16, across), (4, padded, across)],
        received,
        coarse,
        inner,
        outer,
        smooth,
        weights,
        inverse,
    )
    near = (tiles // 2, 2, padded, across)
    message, second, *sent = call(
        part(second_kernel, levels, groups),
        [(blocks, LAST_ROWS, across), field] + [field, near] * swap,
        low,
        high,
        rim,
        residual,
        weights,
        inverse,
        image,
        second,
        values,
        corners,
        *packed,
        sends=True,
    )
    received = gather(message)
    parts = []
    if swap:
        near = lax.ppermute(sent[1], "tile", inner_pairs(tiles))
        parts = [packed[0], sent[0], near]
        far = call(send_kernel, [(4, padded, across)] * (tiles // 2 - 1), near, packed[0], sent[0])
        for step, value in zip(far_steps(tiles), far):
            parts.append(lax.ppermute(value, "tile", [(i, i ^ step) for i in range(tiles)]))
    solution_field, state = call(
        part(final_kernel, levels, tiles, groups, swap),
        [flat, (-(-(tiles + 2) // 8) * 8, across) if swap else field],
        received,
        steps,
        coarse,
        smooth,
        second,
    )
    if swap:
        (state,) = call(part(state_kernel, levels), [flat], state, *parts, scratch=[field])
    if not swap:
        state = state[:, :levels].reshape(points, levels, tiles, width).transpose(2, 1, 0, 3)
        state = to_tiles(state).transpose(2, 1, 0, 3)
    shape = (levels, points, across)
    return solution_field.reshape(shape), state.reshape(shape)


def solution(mesh):
    return jax.shard_map(
        per_device,
        mesh=mesh,
        in_specs=(
            P(None, "tile", "grp"),
            P(None, "tile", "grp"),
            P(),
            P(None, None, ("tile", "grp")),
            P(),
            P(),
        ),
        out_specs=(P(None, "tile", "grp"), P(None, None, ("tile", "grp"))),
        check_vma=False,
    )
```

```python
import math

import jax
import jax.numpy as jnp
from jax import lax
from jax.experimental import pallas as pl
from jax.experimental.pallas import tpu as pltpu
from jax.sharding import PartitionSpec as P

F32 = jnp.float32
HIGHEST = lax.Precision.HIGHEST
MESSAGE_ROWS = 4
LAST_ROWS = 8
VMEM = pl.BlockSpec(memory_space=pltpu.VMEM)
HBM = pl.BlockSpec(memory_space=pltpu.HBM)


def iota(shape, dim):
    return lax.broadcasted_iota(jnp.int32, shape, dim)


def turn(value, shift, axis=1):
    shift = shift % value.shape[axis]
    return pltpu.roll(value, shift, axis) if shift else value


def total(value):
    return jnp.sum(value, axis=(0, 1), keepdims=True)


def call(kernel, outs, *args, scratch=(), copies=0, sends=False):
    return pl.pallas_call(
        kernel,
        out_shape=[jax.ShapeDtypeStruct(shape, F32) for shape in outs],
        in_specs=[HBM if copies else VMEM] * len(args),
        out_specs=[HBM] * sends + [VMEM] * (len(outs) - sends),
        scratch_shapes=[pltpu.VMEM(shape, F32) for shape in [*scratch, *outs[:sends]]]
        + [pltpu.SemaphoreType.DMA((max(copies, 1),))] * bool(copies or sends),
        compiler_params=pltpu.CompilerParams(vmem_limit_bytes=32 * 1024 * 1024),
    )(*args)


def load_columns(ref, points, levels, padded):
    tiles = []
    for i in range(points):
        tile = ref[pl.ds(i, levels, stride=points), :]
        if padded > levels:
            tile = jnp.concatenate([tile, jnp.zeros((padded - levels, tile.shape[1]), F32)], axis=0)
        tiles.append(tile)
    return tiles


def store_columns(ref, tiles, levels):
    for i, tile in enumerate(tiles):
        ref[pl.ds(i, levels, stride=len(tiles)), :] = tile[:levels]


def swap_groups(tiles):
    count, lanes = len(tiles), tiles[0].shape[1]
    width = lanes // count
    group = iota(tiles[0].shape, 1) // width
    tiles = [turn(tile, i * width) for i, tile in enumerate(tiles)]
    step = 1
    while step < count:
        here = (group & step) == 0
        tiles = [jnp.where(here, tiles[u], tiles[(u + step) % count]) for u in range(count)]
        step *= 2
    return [turn(tiles[-s % count], -s * width) for s in range(count)]


def pack_kernel(levels, x_ref, packed_ref, near_ref):
    points, padded, _ = packed_ref.shape
    for s, tile in enumerate(swap_groups(load_columns(x_ref, points, levels, padded))):
        packed_ref[s] = tile
    other = 1 - (lax.axis_index("tile") & 1)
    for j in range(points // 2):
        near_ref[j] = packed_ref[2 * j + other]


def far_steps(tiles):
    return list(range(tiles - 2, 0, -2))


def relay_kernel(near_ref, packed_ref, *out_refs):
    tile = lax.axis_index("tile")
    for step, out_ref in zip(far_steps(packed_ref.shape[0]), out_refs):
        place = tile ^ step
        out_ref[0], out_ref[1] = packed_ref[place], near_ref[place >> 1]


def tables_kernel(levels, *refs):
    *vector_refs, inverse_ref, matrix_ref, absorbed_ref = refs[:6]
    *buffer_refs, sems = refs[6:]
    copies = [
        pltpu.make_async_copy(vector_ref, buffer_ref, sems.at[n])
        for n, (vector_ref, buffer_ref) in enumerate(zip(vector_refs, buffer_refs))
    ]
    for copy in copies:
        copy.start()
    for copy in copies:
        copy.wait()
    shape = inverse_ref.shape
    sub, lane = iota(shape, 0), iota(shape, 1)

    def column(row, mask):
        return jnp.broadcast_to(jnp.sum(jnp.where(mask, row, 0.0), axis=1, keepdims=True), shape)

    link, thermal, solar = [
        jnp.concatenate([ref[...], jnp.zeros((1, shape[1] - ref.shape[1]), F32)], axis=1)
        for ref in buffer_refs
    ]
    lower = column(link, lane == sub - 1)
    upper = column(link, lane == sub)
    diagonal = 4.0 + lower + upper
    lower, upper = -lower, -upper
    result = jnp.where(lane == sub, 1.0, 0.0).astype(F32)
    step = 1
    while step < levels:
        inverse = 1.0 / diagonal
        a = -lower * turn(inverse, step, 0)
        c = -upper * turn(inverse, -step, 0)
        diagonal = diagonal + a * turn(upper, step, 0) + c * turn(lower, -step, 0)
        result = result + a * turn(result, step, 0) + c * turn(result, -step, 0)
        lower, upper = a * turn(lower, step, 0), c * turn(upper, -step, 0)
        step *= 2
    valid = (sub < levels) & (lane < levels)
    inverse_ref[...] = jnp.where(valid, result / diagonal, 0.0)

    own = column(thermal, lane == sub)
    top_column = column(thermal, lane < sub)
    bottom_column = column(thermal, lane <= sub)
    top_row = jnp.sum(jnp.where(sub < lane, own, 0.0), axis=0, keepdims=True)
    bottom_row = jnp.sum(jnp.where(sub <= lane, own, 0.0), axis=0, keepdims=True)
    whole = jnp.sum(thermal, axis=1, keepdims=True)
    emitted = 1.0 - jnp.exp(-thermal)

    def decay(mask, gap):
        return jnp.where(mask, jnp.exp(-jnp.where(mask, gap, 0.0)), 0.0)

    below, above = lane < sub, lane > sub
    matrix = decay(below, top_column - bottom_row) - decay(below, bottom_column - bottom_row)
    matrix = matrix + decay(above, top_row - bottom_column) - decay(above, top_row - top_column)
    matrix = (matrix - jnp.where(lane == sub, 2.0, 0.0)) * emitted
    surface = (lane == levels - 1) & (sub < levels)
    matrix = matrix + decay(surface, whole - bottom_column) - decay(surface, whole - top_column)
    matrix_ref[...] = jnp.where(valid, matrix, 0.0)
    entering = column(solar, lane < sub)
    leaving = column(solar, lane <= sub)
    absorbed = 10.0 * (jnp.exp(-entering) - jnp.exp(-leaving))
    absorbed_ref[...] = jnp.where(sub < levels, absorbed, 0.0)


def scalars_row(values, lanes):
    count = len(values)
    padded = -(-count // 8) * 8
    rows = [jnp.sum(value, axis=0, keepdims=True) for value in values]
    rows += [jnp.zeros_like(rows[0])] * (padded - count)
    sums = jnp.sum(jnp.concatenate(rows, axis=0), axis=1, keepdims=True)
    shape = (padded, lanes)
    spread = jnp.where(iota(shape, 0) == iota(shape, 1), sums, 0.0)
    return jnp.sum(spread, axis=0, keepdims=True)


def fold(tile):
    parts = [tile[8 * j : 8 * j + 8] for j in range(tile.shape[0] // 8)]
    while len(parts) > 1:
        parts = [a + b for a, b in zip(parts[::2], parts[1::2])] + parts[len(parts) // 2 * 2 :]
    return parts[0]


def add_all(parts):
    parts = list(parts)
    while len(parts) > 1:
        parts = [a + b for a, b in zip(parts[::2], parts[1::2])] + parts[len(parts) // 2 * 2 :]
    return parts[0]


def dot(matrix, tiles):
    across = tiles[0].shape[1]
    field = jnp.concatenate(tiles, axis=1)
    field = jnp.dot(matrix, field, precision=HIGHEST, preferred_element_type=F32)
    return [field[:, i * across : (i + 1) * across] for i in range(len(tiles))]


def prepare_kernel(
    levels,
    forcing_ref,
    weight_ref,
    inverse_ref,
    matrix_ref,
    absorbed_ref,
    cosine_ref,
    forced_ref,
    weight_out_ref,
    base_ref,
    matrices_ref,
    rows_ref,
    unit_ref,
):
    points, padded, across = forced_ref.shape
    inverse = inverse_ref[:, :padded]
    sun = absorbed_ref[...] * cosine_ref[...]
    forcing = load_columns(forcing_ref, points, levels, padded)
    rows_ref[16:24] = add_all([fold(tile) for tile in forcing])
    forced = [tile + sun for tile in forcing]
    for i, tile in enumerate(dot(inverse, forced)):
        forced_ref[i] = forced[i]
        base_ref[i] = tile
    weight = load_columns(weight_ref, points, levels, padded)
    for i, tile in enumerate(weight):
        weight_out_ref[i] = tile
    matrices_ref[0:padded] = matrix_ref[...]
    matrices_ref[padded : 2 * padded] = dot(inverse, [matrix_ref[...]])[0]
    heated = jnp.sum(fold(matrix_ref[...]), axis=0, keepdims=True)
    matrices_ref[2 * padded :] = jnp.broadcast_to(heated, (8, across))
    unit_ref[...] = jnp.broadcast_to(
        jnp.sum(inverse_ref[...], axis=1, keepdims=True), unit_ref.shape
    )
    rows_ref[0:8] = add_all([fold(tile) for tile in weight])
    solar = jnp.sum(fold(sun), axis=0, keepdims=True)
    rows_ref[8:16] = jnp.broadcast_to(solar, (8, across))


def smooth_kernel(levels, tiles, groups, swap, *refs):
    *refs, message_ref, message_sem = refs
    count = len(refs) - 6 - 2 * swap
    *kelvin_refs, forced_ref, weight_ref, base_ref, matrices_ref, rows_ref, unit_ref = refs[:count]
    sent_ref, residual_ref, smooth_ref, rim_ref, inner_ref, outer_ref, *refs = refs[count:]
    points, padded, across = residual_ref.shape
    if swap:
        state_ref, scratch_ref = refs
        tile = lax.axis_index("tile")
        packed_ref, near_ref, *far_refs = kelvin_refs
        scratch_ref[tile], scratch_ref[tile ^ 1] = packed_ref[tile], near_ref[tile >> 1]
        for step, far_ref in zip(far_steps(points), far_refs):
            scratch_ref[tile ^ step], scratch_ref[tile ^ (step + 1)] = far_ref[0], far_ref[1]
        kelvin = swap_groups([scratch_ref[i] for i in range(points)])
    else:
        kelvin = [kelvin_refs[0][i] for i in range(points)]
    squares = [tile * tile for tile in kelvin]
    emission = [tile * tile for tile in squares]
    both = dot(matrices_ref[padded:, :padded], emission)
    solar, unit = rows_ref[8:9, :], unit_ref[...]
    means = [(tile[padded : padded + 1] + solar) * (1.0 / levels) for tile in both]
    smooth = [base_ref[i] + (both[i][:padded] - unit * means[i]) for i in range(points)]
    for i in range(points):
        smooth_ref[i] = smooth[i]
    weight = [weight_ref[i] for i in range(points)]
    folded = [fold(tile) for tile in smooth]
    loss = add_all([fold(a * b) for a, b in zip(smooth, weight)])
    mass = rows_ref[0:8, :]
    every = add_all(folded)
    lane = iota(every.shape, 1)
    scalars = scalars_row(
        [
            rows_ref[16:24, :] - loss,
            folded[0],
            folded[-1],
            jnp.where(lane == 0, every, 0.0),
            jnp.where(lane == across - 1, every, 0.0),
            mass,
        ],
        across,
    )
    lane = iota((padded, across), 1)
    corner = jnp.where((lane == 0) | (lane == across - 1), smooth[0], turn(smooth[-1], 2))
    rows = jnp.concatenate([corner, jnp.zeros((across - padded, across), F32)], axis=0).T
    scalars = turn(scalars, padded)
    message_ref[...] = jnp.zeros(message_ref.shape, F32)
    message_ref[:, 0, :] = jnp.broadcast_to(scalars, (message_ref.shape[0], across))
    corners = (0, 2, across - 1, 1)
    for place, corner in zip(neighbours(tiles, groups)[5:], corners):
        message_ref[pl.ds(place, 1), 0, :] = rows[corner : corner + 1] + scalars
    send = pltpu.make_async_copy(message_ref, sent_ref, message_sem.at[0])
    send.start()

    heat = dot(matrices_ref[:padded, :padded], emission)
    real = iota((padded, across), 0) < levels
    for i in range(points):
        residual_ref[i] = forced_ref[i] + jnp.where(real, heat[i] - means[i], 0.0)
    stride = across // points
    rim = jnp.zeros((padded, across), F32)
    for i in range(points):
        place = (lane - stride * i + 2) & (across - 1)
        rim = jnp.where(place < 4, turn(smooth[i], stride * i), rim)
        rim = jnp.where((place == 5) | (place == 6), turn(weight[i], stride * i + 4), rim)
    rim_ref[...] = rim
    even = lax.rem(lax.axis_index("tile"), 2) == 0
    sides = zip((smooth[0], smooth[1], weight[0]), (smooth[-2], smooth[-1], weight[-1]))
    for j, (west, east) in enumerate(sides):
        inner_ref[j] = jnp.where(even, east, west)
        outer_ref[j] = jnp.where(even, west, east)
    if swap:
        for s, tile in enumerate(swap_groups(smooth)):
            state_ref[s] = tile
    send.wait()


def send_kernel(near_ref, smooth_ref, second_ref, *out_refs):
    tile = lax.axis_index("tile")
    for step, out_ref in zip(far_steps(smooth_ref.shape[0]), out_refs):
        place = tile ^ step
        out_ref[0], out_ref[1] = smooth_ref[place], second_ref[place]
        out_ref[2], out_ref[3] = near_ref[place >> 1, 0], near_ref[place >> 1, 1]


def neighbours(tiles, groups):
    tile, group = lax.axis_index("tile"), lax.axis_index("grp")
    west, east = lax.rem(tile + tiles - 1, tiles), lax.rem(tile + 1, tiles)
    south, north = jnp.maximum(group - 1, 0), jnp.minimum(group + 1, groups - 1)
    pairs = [(tile, group), (west, group), (east, group), (tile, south), (tile, north)]
    pairs += [(west, south), (east, south), (west, north), (east, north)]
    return [x * groups + y for x, y in pairs]


def small_inverse(block):
    size = len(block)
    block = [list(row) for row in block]
    for k in range(size):
        pivot = 1.0 / block[k][k]
        row = [block[k][j] * pivot for j in range(size)]
        for i in range(size):
            if i != k:
                factor = block[i][k]
                for j in range(size):
                    if j != k:
                        block[i][j] = block[i][j] - factor * row[j]
                block[i][k] = -factor * pivot
        for j in range(size):
            block[k][j] = row[j]
        block[k][k] = pivot
    return block


def product(a, b):
    size = range(len(a))
    return [[add_all([a[i][k] * b[k][j] for k in size]) for j in size] for i in size]


def apply(a, v):
    size = range(len(a))
    return [add_all([a[i][k] * v[k] for k in size]) for i in size]


def flip(a):
    return [list(row) for row in zip(*a)]


def turn_block(a, shift):
    return [[turn(value, shift) for value in row] for row in a]


def with_diagonal(block, row_sums, beside):
    size = range(len(block))
    return [
        [
            row_sums[i] - add_all([block[i][k] for k in size if k != i] + beside[i]) if i == j else block[i][j]
            for j in size
        ]
        for i in size
    ]


def coarse_factor(mass, tiles, groups, x_face, y_face):
    zero = jnp.zeros_like(mass)
    size = range(groups)
    diagonal = [[zero - y_face if abs(i - j) == 1 else zero for i in size] for j in size]
    coupling = [[zero - x_face if i == j else zero for i in size] for j in size]
    row_sums = [turn(mass, -j) for j in size]
    diagonal = with_diagonal(diagonal, row_sums, [[zero - 2.0 * x_face]] * groups)
    steps = []
    step = 1
    while step < tiles:
        inverse = small_inverse(diagonal)
        shift = step * groups
        steps.append((inverse, coupling))
        left = product(coupling, turn_block(inverse, shift))
        low = product(left, flip(coupling))
        high = turn_block(product(flip(coupling), product(inverse, coupling)), -shift)
        row_sums = reduce_sums(inverse, coupling, row_sums, shift)
        diagonal = [[diagonal[i][j] - (low[i][j] + high[i][j]) for j in size] for i in size]
        coupling = [[-v for v in row] for row in product(left, turn_block(coupling, shift))]
        step *= 2
        beside = [
            [add_all(coupling[i]), turn(add_all(flip(coupling)[i]), -step * groups)] for i in size
        ]
        diagonal = with_diagonal(diagonal, row_sums, beside)
    last = [[diagonal[i][j] + (coupling[i][j] + coupling[j][i]) for j in size] for i in size]
    last = with_diagonal(last, row_sums, [[]] * groups)
    return steps, small_inverse(last)


def reduce_sums(inverse, coupling, values, shift):
    scaled = apply(inverse, values)
    low = apply(coupling, [turn(v, shift) for v in scaled])
    high = [turn(v, -shift) for v in apply(flip(coupling), scaled)]
    return [v - (a + b) for v, a, b in zip(values, low, high)]


def coarse_solve(steps, last, sums, groups):
    values = [turn(sums, -j) for j in range(groups)]
    shift = groups
    for inverse, coupling in steps:
        values = reduce_sums(inverse, coupling, values, shift)
        shift *= 2
    values = apply(last, values)
    residue = iota(sums.shape, 1) % groups
    result = values[0]
    for j in range(1, groups):
        result = jnp.where(residue == j, turn(values[j], j), result)
    return result


def around(row, groups):
    residue = iota(row.shape, 1) % groups
    south = jnp.where(residue == 0, row, turn(row, 1))
    north = jnp.where(residue == groups - 1, row, turn(row, -1))
    return turn(row, groups), turn(row, -groups), south, north


def by_block(received):
    blocks, lanes = received.shape
    if blocks < lanes:
        received = jnp.concatenate([received] * (lanes // blocks), axis=0)
    return received.T


def save_steps(ref, steps, last):
    rows = [v for inverse, coupling in steps for block in (inverse, coupling) for row in block for v in row]
    rows += [v for row in last for v in row]
    for n, row in enumerate(rows):
        ref[n : n + 1, :] = row


def saved_rows(tiles, groups):
    steps = max(tiles - 1, 0).bit_length()
    return (2 * steps + 1) * groups * groups


def load_steps(ref, tiles, groups):
    place = 0
    blocks = []
    for _ in range(2 * max(tiles - 1, 0).bit_length() + 1):
        block = []
        for _ in range(groups):
            block.append([ref[place + j : place + j + 1, :] for j in range(groups)])
            place += groups
        blocks.append(block)
    return list(zip(blocks[:-1:2], blocks[1::2])), blocks[-1]


def coarse_kernel(levels, points, tiles, groups, received_ref, steps_ref, coarse_ref):
    padded = -(-levels // 8) * 8
    scalars = by_block(received_ref[:, 0, :])
    base, west, east, south, north, mass = [scalars[padded + j : padded + j + 1, :] for j in range(6)]
    residue = iota(base.shape, 1) % groups
    facing_south = jnp.where(residue == 0, south, turn(north, 1))
    facing_north = jnp.where(residue == groups - 1, north, turn(south, -1))
    sums = base + (
        (turn(east, groups) - west)
        + (turn(west, -groups) - east)
        + (facing_south - south)
        + (facing_north - north)
    )
    steps, last = coarse_factor(
        mass, tiles, groups, float(levels * received_ref.shape[2]), float(levels * points)
    )
    coarse = coarse_solve(steps, last, sums, groups)
    save_steps(steps_ref, steps, last)
    coarse_ref[...] = coarse


def beyond(groups, lane, across, none=-1):
    group = lax.axis_index("grp")
    south = jnp.where(group == 0, 0, none)
    north = jnp.where(group == groups - 1, across - 1, none)
    return (lane == south) | (lane == north)


def inside_kernel(
    levels,
    tiles,
    groups,
    received_ref,
    coarse_ref,
    inner_ref,
    outer_ref,
    smooth_ref,
    weight_ref,
    inverse_ref,
    image_ref,
    second_ref,
    values_ref,
    corners_ref,
):
    points, padded, across = smooth_ref.shape
    coarse = coarse_ref[...]
    places = neighbours(tiles, groups)
    lane = iota(coarse.shape, 1)
    picked = [jnp.sum(jnp.where(lane == place, coarse, 0.0), axis=1, keepdims=True) for place in places]
    for j, value in enumerate(picked):
        values_ref[j : j + 1, :] = jnp.broadcast_to(value, (1, across))
    shape = (padded, across)
    real = iota(shape, 0) < levels
    own, e_west, e_east, e_south, e_north, e_sw, e_se, e_nw, e_ne = [
        jnp.where(real, value, 0.0) for value in picked
    ]

    corner_rows = [received_ref[pl.ds(place, 1), 0, :] for place in places[5:]]
    corner_rows = [jnp.where(iota(row.shape, 1) < padded, row, 0.0) for row in corner_rows]
    corners = jnp.concatenate(corner_rows + [jnp.zeros((across - 4, across), F32)], axis=0).T
    c_sw, c_se, c_nw, c_ne = [corners[:padded, j : j + 1] for j in range(4)]

    for j, corner in enumerate((c_sw, c_se, c_nw, c_ne)):
        corners_ref[j] = jnp.broadcast_to(corner, shape)

    lane = iota(shape, 1)
    first, final = lane == 0, lane == across - 1

    outside = beyond(groups, lane, across)

    def across_sum(tile, ends):
        ends = jnp.where(outside, tile, ends)
        return jnp.where(first, ends, turn(tile, 1)) + jnp.where(final, ends, turn(tile, -1))

    even_tile = lax.rem(lax.axis_index("tile"), 2) == 0
    weight = [weight_ref[i] for i in range(points)]
    from_west = [jnp.where(even_tile, outer_ref[j], inner_ref[j]) for j in range(3)]
    from_east = [jnp.where(even_tile, inner_ref[j], outer_ref[j]) for j in range(3)]
    weight = from_west[2:] + weight + from_east[2:]
    field = from_west[:2] + [smooth_ref[i] for i in range(points)] + from_east[:2]

    ends = [jnp.where(first, c_sw, c_nw), *[jnp.zeros(shape, F32)] * points, jnp.where(first, c_se, c_ne)]

    def steps(here, low, high):
        return jnp.where(first, here - low, jnp.where(final, here - high, 0.0))

    here = [e_west] + [own] * points + [e_east]
    jumps = [steps(e_west, e_sw, e_nw) + (e_west - own)]
    jumps += [steps(own, e_south, e_north)] * points
    jumps += [steps(e_east, e_se, e_ne) + (e_east - own)]
    jumps[1] = jumps[1] + (own - e_west)
    jumps[points] = jumps[points] + (own - e_east)
    image = [
        (field[i] + field[i + 2])
        + across_sum(field[i + 1], ends[i])
        - (weight[i] * (field[i + 1] + here[i]) + jumps[i])
        for i in range(points + 2)
    ]
    smoothed = dot(inverse_ref[:, :padded], image)
    for i in range(points + 2):
        image_ref[i] = image[i]
        second_ref[i] = field[i + 1] - smoothed[i]


def second_kernel(
    levels,
    groups,
    low_ref,
    high_ref,
    rim_ref,
    residual_ref,
    weight_ref,
    inverse_ref,
    image_ref,
    second_ref_in,
    values_ref,
    corners_ref,
    *refs,
):
    *refs, message_ref, message_sem = refs
    swap = len(refs) > 2
    if swap:
        packed_smooth_ref, sent_ref, second_ref, packed_ref, near_ref = refs
    else:
        sent_ref, second_ref = refs
    points, padded, across = residual_ref.shape
    blocks = message_ref.shape[0]
    stride = across // points
    even_group = lax.rem(lax.axis_index("grp"), 2) == 0

    shape = (padded, across)
    real = iota(shape, 0) < levels
    values = [values_ref[j : j + 1, :] for j in range(9)]
    own, e_west, e_east, e_south, e_north, e_sw, e_se, e_nw, e_ne = [
        jnp.where(real, value, 0.0) for value in values
    ]
    c_sw, c_se, c_nw, c_ne = [corners_ref[j] for j in range(4)]
    weight = [weight_ref[i] for i in range(points)]
    lane = iota(shape, 1)
    first, final = lane == 0, lane == across - 1
    outside = beyond(groups, lane, across)
    inside = lane & (stride - 1)
    is_south, is_north = inside == stride - 1, inside == 0
    rim, low, high = rim_ref[...], low_ref[...], high_ref[...]
    from_south = jnp.where(even_group, high, low)
    from_north = jnp.where(even_group, low, high)
    outer = beyond(groups, jnp.where(is_north, 0, jnp.where(is_south, across - 1, 1)), across)
    both = jnp.where(is_north, turn(from_south, 1), turn(from_north, -1))
    both = jnp.where((is_north | is_south) & jnp.logical_not(outer), both, 0.0)
    edge = stride * (points - 1)

    def ring_image(tile, step, here, west, east, west_lane, east_lane, c_west, c_east):
        rim_weight = turn(tile, -4)
        spread = (here - own) + jnp.where(lane == west_lane, here - west, jnp.where(lane == east_lane, here - east, 0.0))
        return (
            jnp.where(lane == west_lane, c_west, turn(tile, stride))
            + jnp.where(lane == east_lane, c_east, turn(tile, -stride))
            + (turn(tile, step) + turn(rim, -step))
            - (rim_weight * (tile + here) + spread)
        )

    ring_south = ring_image(from_south, 1, e_south, e_sw, e_se, across - 1, edge - 1, c_sw, c_se)
    ring_north = ring_image(from_north, -1, e_north, e_nw, e_ne, 0, edge, c_nw, c_ne)
    ring = jnp.where(is_south, ring_south, jnp.where(is_north, ring_north, 0.0))
    ring_field = jnp.where(is_south, from_south, from_north)
    ring, smoothed = dot(inverse_ref[:, :padded], [ring, both])
    ring = ring_field - ring
    second, image = [second_ref_in[0]], [None]
    ends = first | final
    for i in range(1, points + 1):
        shift = -stride * (i - 1)
        image.append(jnp.where(ends, image_ref[i] + turn(both, shift), image_ref[i]))
        second.append(jnp.where(ends, second_ref_in[i] - turn(smoothed, shift), second_ref_in[i]))
    second.append(second_ref_in[points + 1])
    both = jnp.where(is_north, turn(ring, 1), turn(ring, -1))

    names = ("image", "change", "residual")
    pairs = {}
    sides = {name: [] for name in names}
    left = []

    def collect(key, value):
        pairs.setdefault(key, []).append(fold(value))

    for i in range(points):
        tile = second[i + 1]
        second_ref[i] = tile
        ends = jnp.where(outside, tile, turn(both, -stride * i))
        again = (
            (second[i] + second[i + 2])
            + (jnp.where(first, ends, turn(tile, 1)) + jnp.where(final, ends, turn(tile, -1)))
            - weight[i] * tile
        )
        residual = residual_ref[i]
        result = residual - image[i + 1]
        change = result - again
        left.append(fold(again + (result - 4.0 * tile)))
        heavy = weight[i]
        collect("qq", result * result)
        collect("rq", residual * result)
        collect("qd", result * change)
        collect("dd", change * change)
        collect("rd", residual * change)
        collect("ww", heavy * heavy)
        sides.setdefault("weight", []).append(fold(heavy))
        for name, value in zip(names, (result, change, residual)):
            sides[name].append(fold(value))
            collect("w" + name, heavy * value)
    pairs = {key: add_all(value) for key, value in pairs.items()}
    lane = iota(pairs["qq"].shape, 1)
    out = [pairs[key] for key in ("qq", "rq", "qd", "dd", "rd")]
    for name in names + ("weight",):
        every = add_all(sides[name])
        out += [
            pairs["ww"] if name == "weight" else pairs["w" + name],
            sides[name][0],
            sides[name][-1],
            jnp.where(lane == 0, every, 0.0),
            jnp.where(lane == across - 1, every, 0.0),
        ]
    out.append(add_all(left))
    row = scalars_row(out, across)
    message_ref[...] = jnp.zeros(message_ref.shape, F32)
    message_ref[:, 0, :] = jnp.broadcast_to(row, (blocks, across))
    send = pltpu.make_async_copy(message_ref, sent_ref, message_sem.at[0])
    send.start()
    if swap:
        for s, tile in enumerate(swap_groups(second[1 : points + 1])):
            packed_ref[s] = tile
        other = 1 - (lax.axis_index("tile") & 1)
        for j in range(points // 2):
            near_ref[j, 0] = packed_smooth_ref[2 * j + other]
            near_ref[j, 1] = packed_ref[2 * j + other]
    send.wait()


def final_kernel(
    levels,
    tiles,
    groups,
    swap,
    received_ref,
    steps_ref,
    coarse_ref,
    smooth_ref,
    second_ref,
    field_ref,
    other_ref,
):
    points, padded, across = smooth_ref.shape
    blocks = tiles * groups
    rows = by_block(received_ref[:, 0, :])
    rows = [rows[j : j + 1, :] for j in range(26)]
    steps, last = load_steps(steps_ref, tiles, groups)
    coarse = coarse_solve(steps, last, rows[25], groups)
    jumps = [coarse - near for near in around(coarse, groups)]

    def against(part):
        return add_all([rows[part] * coarse] + [rows[part + 1 + j] * jumps[j] for j in range(4)])

    j_w, j_e, j_s, j_n = jumps
    x_face, y_face = float(levels * across), float(levels * points)
    weighted = add_all([rows[21 + j] * jumps[j] for j in range(4)])
    square = (
        coarse * (rows[20] * coarse + 2.0 * weighted)
        + x_face * (j_w * j_w + j_e * j_e)
        + y_face * (j_s * j_s + j_n * j_n)
        + (2.0 * levels) * ((j_w + j_e) * (j_s + j_n))
    )
    lane = iota(coarse.shape, 1)
    tile, group = lax.axis_index("tile"), lax.axis_index("grp")
    parts = [
        rows[0],
        rows[1],
        rows[2] + against(5),
        rows[3] + 2.0 * against(10) + square,
        rows[4] + against(15),
    ]
    parts = [jnp.where(lane < blocks, part, 0.0) for part in parts]
    parts += [jnp.zeros_like(coarse)] * 3
    sums = jnp.sum(jnp.concatenate(parts, axis=0), axis=1, keepdims=True)
    qq, rq, qv, vv, rv = [sums[j : j + 1, :] for j in range(5)]
    alpha = rq / qq
    beta = qv / qq
    kappa = (rv - alpha * qv) / (vv - beta * qv)
    scale = alpha - kappa * beta
    constant = scale * coarse_ref[...] + kappa * coarse
    others = tiles if swap else 1
    parts = [jnp.where(lane == (tile ^ k) * groups + group, constant, 0.0) for k in range(others)]
    parts += [jnp.zeros_like(coarse)] * (-others % 8)
    shifts = jnp.sum(jnp.concatenate(parts, axis=0), axis=1, keepdims=True)
    shifts = [shifts[k : k + 1, :] for k in range(others)]
    result = [scale * smooth_ref[i] + (kappa * second_ref[i] + shifts[0]) for i in range(points)]
    store_columns(field_ref, result, levels)
    if swap:
        rows = jnp.concatenate([scale, kappa] + shifts, axis=0)
        rows = jnp.concatenate([rows, jnp.zeros((other_ref.shape[0] - rows.shape[0], 1), F32)], axis=0)
        other_ref[...] = jnp.broadcast_to(rows, other_ref.shape)
    else:
        for i in range(points):
            other_ref[i] = result[i]


def state_kernel(levels, scalars_ref, *refs):
    smooth_ref, second_ref, near_ref, *part_refs, state_ref, scratch_ref = refs
    tile = lax.axis_index("tile")
    scale, kappa = scalars_ref[0:1, :], scalars_ref[1:2, :]
    pairs = {0: (smooth_ref[tile], second_ref[tile]), 1: (near_ref[tile >> 1, 0], near_ref[tile >> 1, 1])}
    for step, part_ref in zip(far_steps(smooth_ref.shape[0]), part_refs):
        pairs[step] = (part_ref[0], part_ref[1])
        pairs[step + 1] = (part_ref[2], part_ref[3])
    for k, (smooth, second) in pairs.items():
        scratch_ref[tile ^ k] = scale * smooth + (kappa * second + scalars_ref[2 + k : 3 + k, :])
    store_columns(state_ref, swap_groups([scratch_ref[s] for s in range(len(pairs))]), levels)


def per_device(
    forcing_vector,
    shift_weights,
    layer_link_factor,
    previous_kelvin_field,
    longwave_opacity,
    shortwave_opacity,
):
    tiles, groups = lax.axis_size("tile"), lax.axis_size("grp")
    levels, points, across = forcing_vector.shape
    padded = -(-levels // 8) * 8
    blocks = tiles * groups
    lanes = max(across, blocks)
    width = across // tiles
    swap = tiles == points
    flat = (levels * points, across)
    field = (points, padded, across)

    def to_tiles(value):
        return lax.all_to_all(value, "tile", split_axis=0, concat_axis=0, tiled=True)

    def gather(value):
        return lax.all_to_all(value, ("tile", "grp"), split_axis=0, concat_axis=0, tiled=True)

    def part(kernel, *settings):
        return lambda *refs: kernel(*settings, *refs)

    kelvin = previous_kelvin_field
    if swap:
        near = (tiles // 2, padded, across)
        packed, near = call(part(pack_kernel, levels), [field, near], kelvin.reshape(flat))
        near = lax.ppermute(near, "tile", [(i, i ^ 1) for i in range(tiles)])
        far = call(relay_kernel, [(2, padded, across)] * (tiles // 2 - 1), near, packed)
        kelvin = [packed, near] + [
            lax.ppermute(value, "tile", [(i, i ^ step) for i in range(tiles)])
            for step, value in zip(far_steps(tiles), far)
        ]
    else:
        kelvin = kelvin.reshape(levels, points, tiles, width).transpose(2, 1, 0, 3)
        kelvin = to_tiles(kelvin).transpose(1, 2, 0, 3).reshape(points, levels, across)
        kelvin = jnp.pad(kelvin, ((0, 0), (0, padded - levels), (0, 0)))

    vectors = [v[None, :] for v in (layer_link_factor, longwave_opacity, shortwave_opacity)]
    inverse, matrix, absorbed = call(
        part(tables_kernel, levels),
        [(padded, across)] * 3,
        *vectors,
        scratch=[v.shape for v in vectors],
        copies=len(vectors),
    )
    global_row = lax.axis_index("grp") * across + jnp.arange(across)
    latitude = ((global_row.astype(F32) + 0.5) / (across * groups) - 0.5) * (math.pi / 2)
    cosine = jnp.cos(latitude - 0.4)[None, :]

    forcing = forcing_vector.reshape(flat)
    weights = shift_weights.reshape(flat)
    forced, weights, *prepared = call(
        part(prepare_kernel, levels),
        [field, field, field, (2 * padded + 8, across), (24, across), (padded, across)],
        forcing,
        weights,
        inverse,
        matrix,
        absorbed,
        cosine,
    )
    prepared = [forced, weights, *prepared]
    message = (blocks, MESSAGE_ROWS, across)
    tile, side = (padded, across), (3, padded, across)
    message, residual, smooth, rim, inner, outer, *packed = call(
        part(smooth_kernel, levels, tiles, groups, swap),
        [message, field, field, tile, side, side] + [field] * swap,
        *(kelvin if swap else [kelvin]),
        *prepared,
        scratch=[field] * swap,
        sends=True,
    )
    received = gather(message)

    def inner_pairs(size):
        return [(i, i ^ 1) for i in range(size) if i ^ 1 < size]

    def outer_pairs(size, around):
        pairs = [(i, (i + 1) % size) for i in range(1, size, 2) if around or i + 1 < size]
        return pairs + [(j, i) for i, j in pairs]

    inner = lax.ppermute(inner, "tile", inner_pairs(tiles))
    outer = lax.ppermute(outer, "tile", outer_pairs(tiles, True))
    low = lax.ppermute(rim, "grp", inner_pairs(groups))
    high = lax.ppermute(rim, "grp", outer_pairs(groups, False))
    wide = (points + 2, padded, across)
    steps, coarse = call(
        part(coarse_kernel, levels, points, tiles, groups),
        [(saved_rows(tiles, groups), lanes), (1, lanes)],
        received,
    )
    image, second, values, corners = call(
        part(inside_kernel, levels, tiles, groups),
        [wide, wide, (16, across), (4, padded, across)],
        received,
        coarse,
        inner,
        outer,
        smooth,
        weights,
        inverse,
    )
    near = (tiles // 2, 2, padded, across)
    message, second, *sent = call(
        part(second_kernel, levels, groups),
        [(blocks, LAST_ROWS, across), field] + [field, near] * swap,
        low,
        high,
        rim,
        residual,
        weights,
        inverse,
        image,
        second,
        values,
        corners,
        *packed,
        sends=True,
    )
    received = gather(message)
    parts = []
    if swap:
        near = lax.ppermute(sent[1], "tile", inner_pairs(tiles))
        parts = [packed[0], sent[0], near]
        far = call(send_kernel, [(4, padded, across)] * (tiles // 2 - 1), near, packed[0], sent[0])
        for step, value in zip(far_steps(tiles), far):
            parts.append(lax.ppermute(value, "tile", [(i, i ^ step) for i in range(tiles)]))
    solution_field, state = call(
        part(final_kernel, levels, tiles, groups, swap),
        [flat, (-(-(tiles + 2) // 8) * 8, across) if swap else field],
        received,
        steps,
        coarse,
        smooth,
        second,
    )
    if swap:
        (state,) = call(part(state_kernel, levels), [flat], state, *parts, scratch=[field])
    if not swap:
        state = state[:, :levels].reshape(points, levels, tiles, width).transpose(2, 1, 0, 3)
        state = to_tiles(state).transpose(2, 1, 0, 3)
    shape = (levels, points, across)
    return solution_field.reshape(shape), state.reshape(shape)


def solution(mesh):
    return jax.shard_map(
        per_device,
        mesh=mesh,
        in_specs=(
            P(None, "tile", "grp"),
            P(None, "tile", "grp"),
            P(),
            P(None, None, ("tile", "grp")),
            P(),
            P(),
        ),
        out_specs=(P(None, "tile", "grp"), P(None, None, ("tile", "grp"))),
        check_vma=False,
    )
```

```python
import math

import jax
import jax.numpy as jnp
from jax import lax
from jax.experimental import pallas as pl
from jax.experimental.pallas import tpu as pltpu
from jax.sharding import PartitionSpec as P

F32 = jnp.float32
HIGHEST = lax.Precision.HIGHEST
MESSAGE_ROWS = 4
LAST_ROWS = 8
VMEM = pl.BlockSpec(memory_space=pltpu.VMEM)
HBM = pl.BlockSpec(memory_space=pltpu.HBM)


def iota(shape, dim):
    return lax.broadcasted_iota(jnp.int32, shape, dim)


def turn(value, shift, axis=1):
    shift = shift % value.shape[axis]
    return pltpu.roll(value, shift, axis) if shift else value


def total(value):
    return jnp.sum(value, axis=(0, 1), keepdims=True)


def call(kernel, outs, *args, scratch=(), copies=0, sends=False):
    return pl.pallas_call(
        kernel,
        out_shape=[jax.ShapeDtypeStruct(shape, F32) for shape in outs],
        in_specs=[HBM if copies else VMEM] * len(args),
        out_specs=[HBM] * sends + [VMEM] * (len(outs) - sends),
        scratch_shapes=[pltpu.VMEM(shape, F32) for shape in [*scratch, *outs[:sends]]]
        + [pltpu.SemaphoreType.DMA((max(copies, 1),))] * bool(copies or sends),
        compiler_params=pltpu.CompilerParams(vmem_limit_bytes=32 * 1024 * 1024),
    )(*args)


def load_columns(ref, points, levels, padded):
    tiles = []
    whole = levels // 8 * 8
    for i in range(points):
        parts = [ref[pl.ds(i, whole, stride=points), :]]
        if padded > levels:
            last = ref[pl.ds((levels - 8) * points + i, 8, stride=points), :]
            parts += [last[8 - (levels - whole) :], jnp.zeros((padded - levels, last.shape[1]), F32)]
        tiles.append(jnp.concatenate(parts, axis=0))
    return tiles


def store_columns(ref, tiles, levels):
    points, whole = len(tiles), levels // 8 * 8
    for i, tile in enumerate(tiles):
        ref[pl.ds(i, whole, stride=points), :] = tile[:whole]
        if whole < levels:
            ref[pl.ds((levels - 8) * points + i, 8, stride=points), :] = tile[levels - 8 : levels]


def swap_groups(tiles):
    count, lanes = len(tiles), tiles[0].shape[1]
    width = lanes // count
    group = iota(tiles[0].shape, 1) // width
    tiles = [turn(tile, i * width) for i, tile in enumerate(tiles)]
    step = 1
    while step < count:
        here = (group & step) == 0
        tiles = [jnp.where(here, tiles[u], tiles[(u + step) % count]) for u in range(count)]
        step *= 2
    return [turn(tiles[-s % count], -s * width) for s in range(count)]


def pack_kernel(levels, x_ref, packed_ref, near_ref):
    points, padded, _ = packed_ref.shape
    for s, tile in enumerate(swap_groups(load_columns(x_ref, points, levels, padded))):
        packed_ref[s] = tile
    other = 1 - (lax.axis_index("tile") & 1)
    for j in range(points // 2):
        near_ref[j] = packed_ref[2 * j + other]


def far_steps(tiles):
    return list(range(tiles - 2, 0, -2))


def relay_kernel(near_ref, packed_ref, *out_refs):
    tile = lax.axis_index("tile")
    for step, out_ref in zip(far_steps(packed_ref.shape[0]), out_refs):
        place = tile ^ step
        out_ref[0], out_ref[1] = packed_ref[place], near_ref[place >> 1]


def tables_kernel(levels, *refs):
    *vector_refs, inverse_ref, matrix_ref, absorbed_ref = refs[:6]
    *buffer_refs, sems = refs[6:]
    copies = [
        pltpu.make_async_copy(vector_ref, buffer_ref, sems.at[n])
        for n, (vector_ref, buffer_ref) in enumerate(zip(vector_refs, buffer_refs))
    ]
    for copy in copies:
        copy.start()
    for copy in copies:
        copy.wait()
    shape = inverse_ref.shape
    sub, lane = iota(shape, 0), iota(shape, 1)

    def column(row, mask):
        return jnp.broadcast_to(jnp.sum(jnp.where(mask, row, 0.0), axis=1, keepdims=True), shape)

    link, thermal, solar = [
        jnp.concatenate([ref[...], jnp.zeros((1, shape[1] - ref.shape[1]), F32)], axis=1)
        for ref in buffer_refs
    ]
    lower = column(link, lane == sub - 1)
    upper = column(link, lane == sub)
    diagonal = 4.0 + lower + upper
    lower, upper = -lower, -upper
    result = jnp.where(lane == sub, 1.0, 0.0).astype(F32)
    step = 1
    while step < levels:
        inverse = 1.0 / diagonal
        a = -lower * turn(inverse, step, 0)
        c = -upper * turn(inverse, -step, 0)
        diagonal = diagonal + a * turn(upper, step, 0) + c * turn(lower, -step, 0)
        result = result + a * turn(result, step, 0) + c * turn(result, -step, 0)
        lower, upper = a * turn(lower, step, 0), c * turn(upper, -step, 0)
        step *= 2
    valid = (sub < levels) & (lane < levels)
    inverse_ref[...] = jnp.where(valid, result / diagonal, 0.0)

    own = column(thermal, lane == sub)
    top_column = column(thermal, lane < sub)
    bottom_column = column(thermal, lane <= sub)
    top_row = jnp.sum(jnp.where(sub < lane, own, 0.0), axis=0, keepdims=True)
    bottom_row = jnp.sum(jnp.where(sub <= lane, own, 0.0), axis=0, keepdims=True)
    whole = jnp.sum(thermal, axis=1, keepdims=True)
    emitted = 1.0 - jnp.exp(-thermal)

    def decay(mask, gap):
        return jnp.where(mask, jnp.exp(-jnp.where(mask, gap, 0.0)), 0.0)

    below, above = lane < sub, lane > sub
    matrix = decay(below, top_column - bottom_row) - decay(below, bottom_column - bottom_row)
    matrix = matrix + decay(above, top_row - bottom_column) - decay(above, top_row - top_column)
    matrix = (matrix - jnp.where(lane == sub, 2.0, 0.0)) * emitted
    surface = (lane == levels - 1) & (sub < levels)
    matrix = matrix + decay(surface, whole - bottom_column) - decay(surface, whole - top_column)
    matrix_ref[...] = jnp.where(valid, matrix, 0.0)
    entering = column(solar, lane < sub)
    leaving = column(solar, lane <= sub)
    absorbed = 10.0 * (jnp.exp(-entering) - jnp.exp(-leaving))
    absorbed_ref[...] = jnp.where(sub < levels, absorbed, 0.0)


def scalars_row(values, lanes):
    count = len(values)
    padded = -(-count // 8) * 8
    rows = [jnp.sum(value, axis=0, keepdims=True) for value in values]
    rows += [jnp.zeros_like(rows[0])] * (padded - count)
    sums = jnp.sum(jnp.concatenate(rows, axis=0), axis=1, keepdims=True)
    shape = (padded, lanes)
    spread = jnp.where(iota(shape, 0) == iota(shape, 1), sums, 0.0)
    return jnp.sum(spread, axis=0, keepdims=True)


def fold(tile):
    parts = [tile[8 * j : 8 * j + 8] for j in range(tile.shape[0] // 8)]
    while len(parts) > 1:
        parts = [a + b for a, b in zip(parts[::2], parts[1::2])] + parts[len(parts) // 2 * 2 :]
    return parts[0]


def add_all(parts):
    parts = list(parts)
    while len(parts) > 1:
        parts = [a + b for a, b in zip(parts[::2], parts[1::2])] + parts[len(parts) // 2 * 2 :]
    return parts[0]


def dot(matrix, tiles):
    across = tiles[0].shape[1]
    field = jnp.concatenate(tiles, axis=1)
    field = jnp.dot(matrix, field, precision=HIGHEST, preferred_element_type=F32)
    return [field[:, i * across : (i + 1) * across] for i in range(len(tiles))]


def prepare_kernel(
    levels,
    forcing_ref,
    weight_ref,
    inverse_ref,
    matrix_ref,
    absorbed_ref,
    cosine_ref,
    forced_ref,
    weight_out_ref,
    base_ref,
    matrices_ref,
    rows_ref,
    unit_ref,
):
    points, padded, across = forced_ref.shape
    inverse = inverse_ref[:, :padded]
    sun = absorbed_ref[...] * cosine_ref[...]
    forcing = load_columns(forcing_ref, points, levels, padded)
    rows_ref[16:24] = add_all([fold(tile) for tile in forcing])
    forced = [tile + sun for tile in forcing]
    for i, tile in enumerate(dot(inverse, forced)):
        forced_ref[i] = forced[i]
        base_ref[i] = tile
    weight = load_columns(weight_ref, points, levels, padded)
    for i, tile in enumerate(weight):
        weight_out_ref[i] = tile
    matrices_ref[0:padded] = matrix_ref[...]
    matrices_ref[padded : 2 * padded] = dot(inverse, [matrix_ref[...]])[0]
    heated = jnp.sum(fold(matrix_ref[...]), axis=0, keepdims=True)
    matrices_ref[2 * padded :] = jnp.broadcast_to(heated, (8, across))
    unit_ref[...] = jnp.broadcast_to(
        jnp.sum(inverse_ref[...], axis=1, keepdims=True), unit_ref.shape
    )
    rows_ref[0:8] = add_all([fold(tile) for tile in weight])
    solar = jnp.sum(fold(sun), axis=0, keepdims=True)
    rows_ref[8:16] = jnp.broadcast_to(solar, (8, across))


def smooth_kernel(levels, tiles, groups, swap, *refs):
    *refs, message_ref, message_sem = refs
    count = len(refs) - 6 - 2 * swap
    *kelvin_refs, forced_ref, weight_ref, base_ref, matrices_ref, rows_ref, unit_ref = refs[:count]
    sent_ref, residual_ref, smooth_ref, rim_ref, inner_ref, outer_ref, *refs = refs[count:]
    points, padded, across = residual_ref.shape
    if swap:
        state_ref, scratch_ref = refs
        tile = lax.axis_index("tile")
        packed_ref, near_ref, *far_refs = kelvin_refs
        scratch_ref[tile], scratch_ref[tile ^ 1] = packed_ref[tile], near_ref[tile >> 1]
        for step, far_ref in zip(far_steps(points), far_refs):
            scratch_ref[tile ^ step], scratch_ref[tile ^ (step + 1)] = far_ref[0], far_ref[1]
        kelvin = swap_groups([scratch_ref[i] for i in range(points)])
    else:
        kelvin = [kelvin_refs[0][i] for i in range(points)]
    squares = [tile * tile for tile in kelvin]
    emission = [tile * tile for tile in squares]
    both = dot(matrices_ref[padded:, :padded], emission)
    solar, unit = rows_ref[8:9, :], unit_ref[...]
    means = [(tile[padded : padded + 1] + solar) * (1.0 / levels) for tile in both]
    smooth = [base_ref[i] + (both[i][:padded] - unit * means[i]) for i in range(points)]
    for i in range(points):
        smooth_ref[i] = smooth[i]
    weight = [weight_ref[i] for i in range(points)]
    folded = [fold(tile) for tile in smooth]
    loss = add_all([fold(a * b) for a, b in zip(smooth, weight)])
    mass = rows_ref[0:8, :]
    every = add_all(folded)
    lane = iota(every.shape, 1)
    scalars = scalars_row(
        [
            rows_ref[16:24, :] - loss,
            folded[0],
            folded[-1],
            jnp.where(lane == 0, every, 0.0),
            jnp.where(lane == across - 1, every, 0.0),
            mass,
        ],
        across,
    )
    lane = iota((padded, across), 1)
    corner = jnp.where((lane == 0) | (lane == across - 1), smooth[0], turn(smooth[-1], 2))
    rows = jnp.concatenate([corner, jnp.zeros((across - padded, across), F32)], axis=0).T
    scalars = turn(scalars, padded)
    message_ref[...] = jnp.zeros(message_ref.shape, F32)
    message_ref[:, 0, :] = jnp.broadcast_to(scalars, (message_ref.shape[0], across))
    corners = (0, 2, across - 1, 1)
    for place, corner in zip(neighbours(tiles, groups)[5:], corners):
        message_ref[pl.ds(place, 1), 0, :] = rows[corner : corner + 1] + scalars
    send = pltpu.make_async_copy(message_ref, sent_ref, message_sem.at[0])
    send.start()

    heat = dot(matrices_ref[:padded, :padded], emission)
    real = iota((padded, across), 0) < levels
    for i in range(points):
        residual_ref[i] = forced_ref[i] + jnp.where(real, heat[i] - means[i], 0.0)
    stride = across // points
    rim = jnp.zeros((padded, across), F32)
    for i in range(points):
        place = (lane - stride * i + 2) & (across - 1)
        rim = jnp.where(place < 4, turn(smooth[i], stride * i), rim)
        rim = jnp.where((place == 5) | (place == 6), turn(weight[i], stride * i + 4), rim)
    rim_ref[...] = rim
    even = lax.rem(lax.axis_index("tile"), 2) == 0
    sides = zip((smooth[0], smooth[1], weight[0]), (smooth[-2], smooth[-1], weight[-1]))
    for j, (west, east) in enumerate(sides):
        inner_ref[j] = jnp.where(even, east, west)
        outer_ref[j] = jnp.where(even, west, east)
    if swap:
        for s, tile in enumerate(swap_groups(smooth)):
            state_ref[s] = tile
    send.wait()


def send_kernel(near_ref, smooth_ref, second_ref, *out_refs):
    tile = lax.axis_index("tile")
    for step, out_ref in zip(far_steps(smooth_ref.shape[0]), out_refs):
        place = tile ^ step
        out_ref[0], out_ref[1] = smooth_ref[place], second_ref[place]
        out_ref[2], out_ref[3] = near_ref[place >> 1, 0], near_ref[place >> 1, 1]


def neighbours(tiles, groups):
    tile, group = lax.axis_index("tile"), lax.axis_index("grp")
    west, east = lax.rem(tile + tiles - 1, tiles), lax.rem(tile + 1, tiles)
    south, north = jnp.maximum(group - 1, 0), jnp.minimum(group + 1, groups - 1)
    pairs = [(tile, group), (west, group), (east, group), (tile, south), (tile, north)]
    pairs += [(west, south), (east, south), (west, north), (east, north)]
    return [x * groups + y for x, y in pairs]


def small_inverse(block):
    size = len(block)
    block = [list(row) for row in block]
    for k in range(size):
        pivot = 1.0 / block[k][k]
        row = [block[k][j] * pivot for j in range(size)]
        for i in range(size):
            if i != k:
                factor = block[i][k]
                for j in range(size):
                    if j != k:
                        block[i][j] = block[i][j] - factor * row[j]
                block[i][k] = -factor * pivot
        for j in range(size):
            block[k][j] = row[j]
        block[k][k] = pivot
    return block


def product(a, b):
    size = range(len(a))
    return [[add_all([a[i][k] * b[k][j] for k in size]) for j in size] for i in size]


def apply(a, v):
    size = range(len(a))
    return [add_all([a[i][k] * v[k] for k in size]) for i in size]


def flip(a):
    return [list(row) for row in zip(*a)]


def turn_block(a, shift):
    return [[turn(value, shift) for value in row] for row in a]


def with_diagonal(block, row_sums, beside):
    size = range(len(block))
    return [
        [
            row_sums[i] - add_all([block[i][k] for k in size if k != i] + beside[i]) if i == j else block[i][j]
            for j in size
        ]
        for i in size
    ]


def coarse_factor(mass, tiles, groups, x_face, y_face):
    zero = jnp.zeros_like(mass)
    size = range(groups)
    diagonal = [[zero - y_face if abs(i - j) == 1 else zero for i in size] for j in size]
    coupling = [[zero - x_face if i == j else zero for i in size] for j in size]
    row_sums = [turn(mass, -j) for j in size]
    diagonal = with_diagonal(diagonal, row_sums, [[zero - 2.0 * x_face]] * groups)
    steps = []
    step = 1
    while step < tiles:
        inverse = small_inverse(diagonal)
        shift = step * groups
        steps.append((inverse, coupling))
        left = product(coupling, turn_block(inverse, shift))
        low = product(left, flip(coupling))
        high = turn_block(product(flip(coupling), product(inverse, coupling)), -shift)
        row_sums = reduce_sums(inverse, coupling, row_sums, shift)
        diagonal = [[diagonal[i][j] - (low[i][j] + high[i][j]) for j in size] for i in size]
        coupling = [[-v for v in row] for row in product(left, turn_block(coupling, shift))]
        step *= 2
        beside = [
            [add_all(coupling[i]), turn(add_all(flip(coupling)[i]), -step * groups)] for i in size
        ]
        diagonal = with_diagonal(diagonal, row_sums, beside)
    last = [[diagonal[i][j] + (coupling[i][j] + coupling[j][i]) for j in size] for i in size]
    last = with_diagonal(last, row_sums, [[]] * groups)
    return steps, small_inverse(last)


def reduce_sums(inverse, coupling, values, shift):
    scaled = apply(inverse, values)
    low = apply(coupling, [turn(v, shift) for v in scaled])
    high = [turn(v, -shift) for v in apply(flip(coupling), scaled)]
    return [v - (a + b) for v, a, b in zip(values, low, high)]


def coarse_solve(steps, last, sums, groups):
    values = [turn(sums, -j) for j in range(groups)]
    shift = groups
    for inverse, coupling in steps:
        values = reduce_sums(inverse, coupling, values, shift)
        shift *= 2
    values = apply(last, values)
    residue = iota(sums.shape, 1) % groups
    result = values[0]
    for j in range(1, groups):
        result = jnp.where(residue == j, turn(values[j], j), result)
    return result


def around(row, groups):
    residue = iota(row.shape, 1) % groups
    south = jnp.where(residue == 0, row, turn(row, 1))
    north = jnp.where(residue == groups - 1, row, turn(row, -1))
    return turn(row, groups), turn(row, -groups), south, north


def by_block(received):
    blocks, lanes = received.shape
    if blocks < lanes:
        received = jnp.concatenate([received] * (lanes // blocks), axis=0)
    return received.T


def save_steps(ref, steps, last):
    rows = [v for inverse, coupling in steps for block in (inverse, coupling) for row in block for v in row]
    rows += [v for row in last for v in row]
    for n, row in enumerate(rows):
        ref[n : n + 1, :] = row


def saved_rows(tiles, groups):
    steps = max(tiles - 1, 0).bit_length()
    return (2 * steps + 1) * groups * groups


def load_steps(ref, tiles, groups):
    place = 0
    blocks = []
    for _ in range(2 * max(tiles - 1, 0).bit_length() + 1):
        block = []
        for _ in range(groups):
            block.append([ref[place + j : place + j + 1, :] for j in range(groups)])
            place += groups
        blocks.append(block)
    return list(zip(blocks[:-1:2], blocks[1::2])), blocks[-1]


def coarse_kernel(levels, points, tiles, groups, received_ref, steps_ref, coarse_ref):
    padded = -(-levels // 8) * 8
    scalars = by_block(received_ref[:, 0, :])
    base, west, east, south, north, mass = [scalars[padded + j : padded + j + 1, :] for j in range(6)]
    residue = iota(base.shape, 1) % groups
    facing_south = jnp.where(residue == 0, south, turn(north, 1))
    facing_north = jnp.where(residue == groups - 1, north, turn(south, -1))
    sums = base + (
        (turn(east, groups) - west)
        + (turn(west, -groups) - east)
        + (facing_south - south)
        + (facing_north - north)
    )
    steps, last = coarse_factor(
        mass, tiles, groups, float(levels * received_ref.shape[2]), float(levels * points)
    )
    coarse = coarse_solve(steps, last, sums, groups)
    save_steps(steps_ref, steps, last)
    coarse_ref[...] = coarse


def beyond(groups, lane, across, none=-1):
    group = lax.axis_index("grp")
    south = jnp.where(group == 0, 0, none)
    north = jnp.where(group == groups - 1, across - 1, none)
    return (lane == south) | (lane == north)


def inside_kernel(
    levels,
    tiles,
    groups,
    received_ref,
    coarse_ref,
    inner_ref,
    outer_ref,
    smooth_ref,
    weight_ref,
    inverse_ref,
    image_ref,
    second_ref,
    values_ref,
    corners_ref,
):
    points, padded, across = smooth_ref.shape
    coarse = coarse_ref[...]
    places = neighbours(tiles, groups)
    lane = iota(coarse.shape, 1)
    picked = [jnp.sum(jnp.where(lane == place, coarse, 0.0), axis=1, keepdims=True) for place in places]
    for j, value in enumerate(picked):
        values_ref[j : j + 1, :] = jnp.broadcast_to(value, (1, across))
    shape = (padded, across)
    real = iota(shape, 0) < levels
    own, e_west, e_east, e_south, e_north, e_sw, e_se, e_nw, e_ne = [
        jnp.where(real, value, 0.0) for value in picked
    ]

    corner_rows = [received_ref[pl.ds(place, 1), 0, :] for place in places[5:]]
    corner_rows = [jnp.where(iota(row.shape, 1) < padded, row, 0.0) for row in corner_rows]
    corners = jnp.concatenate(corner_rows + [jnp.zeros((across - 4, across), F32)], axis=0).T
    c_sw, c_se, c_nw, c_ne = [corners[:padded, j : j + 1] for j in range(4)]

    for j, corner in enumerate((c_sw, c_se, c_nw, c_ne)):
        corners_ref[j] = jnp.broadcast_to(corner, shape)

    lane = iota(shape, 1)
    first, final = lane == 0, lane == across - 1

    outside = beyond(groups, lane, across)

    def across_sum(tile, ends):
        ends = jnp.where(outside, tile, ends)
        return jnp.where(first, ends, turn(tile, 1)) + jnp.where(final, ends, turn(tile, -1))

    even_tile = lax.rem(lax.axis_index("tile"), 2) == 0
    weight = [weight_ref[i] for i in range(points)]
    from_west = [jnp.where(even_tile, outer_ref[j], inner_ref[j]) for j in range(3)]
    from_east = [jnp.where(even_tile, inner_ref[j], outer_ref[j]) for j in range(3)]
    weight = from_west[2:] + weight + from_east[2:]
    field = from_west[:2] + [smooth_ref[i] for i in range(points)] + from_east[:2]

    ends = [jnp.where(first, c_sw, c_nw), *[jnp.zeros(shape, F32)] * points, jnp.where(first, c_se, c_ne)]

    def steps(here, low, high):
        return jnp.where(first, here - low, jnp.where(final, here - high, 0.0))

    here = [e_west] + [own] * points + [e_east]
    jumps = [steps(e_west, e_sw, e_nw) + (e_west - own)]
    jumps += [steps(own, e_south, e_north)] * points
    jumps += [steps(e_east, e_se, e_ne) + (e_east - own)]
    jumps[1] = jumps[1] + (own - e_west)
    jumps[points] = jumps[points] + (own - e_east)
    image = [
        (field[i] + field[i + 2])
        + across_sum(field[i + 1], ends[i])
        - (weight[i] * (field[i + 1] + here[i]) + jumps[i])
        for i in range(points + 2)
    ]
    smoothed = dot(inverse_ref[:, :padded], image)
    for i in range(points + 2):
        image_ref[i] = image[i]
        second_ref[i] = field[i + 1] - smoothed[i]


def second_kernel(
    levels,
    groups,
    low_ref,
    high_ref,
    rim_ref,
    residual_ref,
    weight_ref,
    inverse_ref,
    image_ref,
    second_ref_in,
    values_ref,
    corners_ref,
    *refs,
):
    *refs, message_ref, message_sem = refs
    swap = len(refs) > 2
    if swap:
        packed_smooth_ref, sent_ref, second_ref, packed_ref, near_ref = refs
    else:
        sent_ref, second_ref = refs
    points, padded, across = residual_ref.shape
    blocks = message_ref.shape[0]
    stride = across // points
    even_group = lax.rem(lax.axis_index("grp"), 2) == 0

    shape = (padded, across)
    real = iota(shape, 0) < levels
    values = [values_ref[j : j + 1, :] for j in range(9)]
    own, e_west, e_east, e_south, e_north, e_sw, e_se, e_nw, e_ne = [
        jnp.where(real, value, 0.0) for value in values
    ]
    c_sw, c_se, c_nw, c_ne = [corners_ref[j] for j in range(4)]
    weight = [weight_ref[i] for i in range(points)]
    lane = iota(shape, 1)
    first, final = lane == 0, lane == across - 1
    outside = beyond(groups, lane, across)
    inside = lane & (stride - 1)
    is_south, is_north = inside == stride - 1, inside == 0
    rim, low, high = rim_ref[...], low_ref[...], high_ref[...]
    from_south = jnp.where(even_group, high, low)
    from_north = jnp.where(even_group, low, high)
    outer = beyond(groups, jnp.where(is_north, 0, jnp.where(is_south, across - 1, 1)), across)
    both = jnp.where(is_north, turn(from_south, 1), turn(from_north, -1))
    both = jnp.where((is_north | is_south) & jnp.logical_not(outer), both, 0.0)
    edge = stride * (points - 1)

    def ring_image(tile, step, here, west, east, west_lane, east_lane, c_west, c_east):
        rim_weight = turn(tile, -4)
        spread = (here - own) + jnp.where(lane == west_lane, here - west, jnp.where(lane == east_lane, here - east, 0.0))
        return (
            jnp.where(lane == west_lane, c_west, turn(tile, stride))
            + jnp.where(lane == east_lane, c_east, turn(tile, -stride))
            + (turn(tile, step) + turn(rim, -step))
            - (rim_weight * (tile + here) + spread)
        )

    ring_south = ring_image(from_south, 1, e_south, e_sw, e_se, across - 1, edge - 1, c_sw, c_se)
    ring_north = ring_image(from_north, -1, e_north, e_nw, e_ne, 0, edge, c_nw, c_ne)
    ring = jnp.where(is_south, ring_south, jnp.where(is_north, ring_north, 0.0))
    ring_field = jnp.where(is_south, from_south, from_north)
    ring, smoothed = dot(inverse_ref[:, :padded], [ring, both])
    ring = ring_field - ring
    second, image = [second_ref_in[0]], [None]
    ends = first | final
    for i in range(1, points + 1):
        shift = -stride * (i - 1)
        image.append(jnp.where(ends, image_ref[i] + turn(both, shift), image_ref[i]))
        second.append(jnp.where(ends, second_ref_in[i] - turn(smoothed, shift), second_ref_in[i]))
    second.append(second_ref_in[points + 1])
    both = jnp.where(is_north, turn(ring, 1), turn(ring, -1))

    names = ("image", "change", "residual")
    pairs = {}
    sides = {name: [] for name in names}
    left = []

    def collect(key, value):
        pairs.setdefault(key, []).append(fold(value))

    for i in range(points):
        tile = second[i + 1]
        second_ref[i] = tile
        ends = jnp.where(outside, tile, turn(both, -stride * i))
        again = (
            (second[i] + second[i + 2])
            + (jnp.where(first, ends, turn(tile, 1)) + jnp.where(final, ends, turn(tile, -1)))
            - weight[i] * tile
        )
        residual = residual_ref[i]
        result = residual - image[i + 1]
        change = result - again
        left.append(fold(again + (result - 4.0 * tile)))
        heavy = weight[i]
        collect("qq", result * result)
        collect("rq", residual * result)
        collect("qd", result * change)
        collect("dd", change * change)
        collect("rd", residual * change)
        collect("ww", heavy * heavy)
        sides.setdefault("weight", []).append(fold(heavy))
        for name, value in zip(names, (result, change, residual)):
            sides[name].append(fold(value))
            collect("w" + name, heavy * value)
    pairs = {key: add_all(value) for key, value in pairs.items()}
    lane = iota(pairs["qq"].shape, 1)
    out = [pairs[key] for key in ("qq", "rq", "qd", "dd", "rd")]
    for name in names + ("weight",):
        every = add_all(sides[name])
        out += [
            pairs["ww"] if name == "weight" else pairs["w" + name],
            sides[name][0],
            sides[name][-1],
            jnp.where(lane == 0, every, 0.0),
            jnp.where(lane == across - 1, every, 0.0),
        ]
    out.append(add_all(left))
    row = scalars_row(out, across)
    message_ref[...] = jnp.zeros(message_ref.shape, F32)
    message_ref[:, 0, :] = jnp.broadcast_to(row, (blocks, across))
    send = pltpu.make_async_copy(message_ref, sent_ref, message_sem.at[0])
    send.start()
    if swap:
        for s, tile in enumerate(swap_groups(second[1 : points + 1])):
            packed_ref[s] = tile
        other = 1 - (lax.axis_index("tile") & 1)
        for j in range(points // 2):
            near_ref[j, 0] = packed_smooth_ref[2 * j + other]
            near_ref[j, 1] = packed_ref[2 * j + other]
    send.wait()


def final_kernel(
    levels,
    tiles,
    groups,
    swap,
    received_ref,
    steps_ref,
    coarse_ref,
    smooth_ref,
    second_ref,
    field_ref,
    other_ref,
):
    points, padded, across = smooth_ref.shape
    blocks = tiles * groups
    rows = by_block(received_ref[:, 0, :])
    rows = [rows[j : j + 1, :] for j in range(26)]
    steps, last = load_steps(steps_ref, tiles, groups)
    coarse = coarse_solve(steps, last, rows[25], groups)
    jumps = [coarse - near for near in around(coarse, groups)]

    def against(part):
        return add_all([rows[part] * coarse] + [rows[part + 1 + j] * jumps[j] for j in range(4)])

    j_w, j_e, j_s, j_n = jumps
    x_face, y_face = float(levels * across), float(levels * points)
    weighted = add_all([rows[21 + j] * jumps[j] for j in range(4)])
    square = (
        coarse * (rows[20] * coarse + 2.0 * weighted)
        + x_face * (j_w * j_w + j_e * j_e)
        + y_face * (j_s * j_s + j_n * j_n)
        + (2.0 * levels) * ((j_w + j_e) * (j_s + j_n))
    )
    lane = iota(coarse.shape, 1)
    tile, group = lax.axis_index("tile"), lax.axis_index("grp")
    parts = [
        rows[0],
        rows[1],
        rows[2] + against(5),
        rows[3] + 2.0 * against(10) + square,
        rows[4] + against(15),
    ]
    parts = [jnp.where(lane < blocks, part, 0.0) for part in parts]
    parts += [jnp.zeros_like(coarse)] * 3
    sums = jnp.sum(jnp.concatenate(parts, axis=0), axis=1, keepdims=True)
    qq, rq, qv, vv, rv = [sums[j : j + 1, :] for j in range(5)]
    alpha = rq / qq
    beta = qv / qq
    kappa = (rv - alpha * qv) / (vv - beta * qv)
    scale = alpha - kappa * beta
    constant = scale * coarse_ref[...] + kappa * coarse
    others = tiles if swap else 1
    parts = [jnp.where(lane == (tile ^ k) * groups + group, constant, 0.0) for k in range(others)]
    parts += [jnp.zeros_like(coarse)] * (-others % 8)
    shifts = jnp.sum(jnp.concatenate(parts, axis=0), axis=1, keepdims=True)
    shifts = [shifts[k : k + 1, :] for k in range(others)]
    result = [scale * smooth_ref[i] + (kappa * second_ref[i] + shifts[0]) for i in range(points)]
    store_columns(field_ref, result, levels)
    if swap:
        rows = jnp.concatenate([scale, kappa] + shifts, axis=0)
        rows = jnp.concatenate([rows, jnp.zeros((other_ref.shape[0] - rows.shape[0], 1), F32)], axis=0)
        other_ref[...] = jnp.broadcast_to(rows, other_ref.shape)
    else:
        for i in range(points):
            other_ref[i] = result[i]


def state_kernel(levels, scalars_ref, *refs):
    smooth_ref, second_ref, near_ref, *part_refs, state_ref, scratch_ref = refs
    tile = lax.axis_index("tile")
    scale, kappa = scalars_ref[0:1, :], scalars_ref[1:2, :]
    pairs = {0: (smooth_ref[tile], second_ref[tile]), 1: (near_ref[tile >> 1, 0], near_ref[tile >> 1, 1])}
    for step, part_ref in zip(far_steps(smooth_ref.shape[0]), part_refs):
        pairs[step] = (part_ref[0], part_ref[1])
        pairs[step + 1] = (part_ref[2], part_ref[3])
    for k, (smooth, second) in pairs.items():
        scratch_ref[tile ^ k] = scale * smooth + (kappa * second + scalars_ref[2 + k : 3 + k, :])
    store_columns(state_ref, swap_groups([scratch_ref[s] for s in range(len(pairs))]), levels)


def per_device(
    forcing_vector,
    shift_weights,
    layer_link_factor,
    previous_kelvin_field,
    longwave_opacity,
    shortwave_opacity,
):
    tiles, groups = lax.axis_size("tile"), lax.axis_size("grp")
    levels, points, across = forcing_vector.shape
    padded = -(-levels // 8) * 8
    blocks = tiles * groups
    lanes = max(across, blocks)
    width = across // tiles
    swap = tiles == points
    flat = (levels * points, across)
    field = (points, padded, across)

    def to_tiles(value):
        return lax.all_to_all(value, "tile", split_axis=0, concat_axis=0, tiled=True)

    def gather(value):
        return lax.all_to_all(value, ("tile", "grp"), split_axis=0, concat_axis=0, tiled=True)

    def part(kernel, *settings):
        return lambda *refs: kernel(*settings, *refs)

    kelvin = previous_kelvin_field
    if swap:
        near = (tiles // 2, padded, across)
        packed, near = call(part(pack_kernel, levels), [field, near], kelvin.reshape(flat))
        near = lax.ppermute(near, "tile", [(i, i ^ 1) for i in range(tiles)])
        far = call(relay_kernel, [(2, padded, across)] * (tiles // 2 - 1), near, packed)
        kelvin = [packed, near] + [
            lax.ppermute(value, "tile", [(i, i ^ step) for i in range(tiles)])
            for step, value in zip(far_steps(tiles), far)
        ]
    else:
        kelvin = kelvin.reshape(levels, points, tiles, width).transpose(2, 1, 0, 3)
        kelvin = to_tiles(kelvin).transpose(1, 2, 0, 3).reshape(points, levels, across)
        kelvin = jnp.pad(kelvin, ((0, 0), (0, padded - levels), (0, 0)))

    vectors = [v[None, :] for v in (layer_link_factor, longwave_opacity, shortwave_opacity)]
    inverse, matrix, absorbed = call(
        part(tables_kernel, levels),
        [(padded, across)] * 3,
        *vectors,
        scratch=[v.shape for v in vectors],
        copies=len(vectors),
    )
    global_row = lax.axis_index("grp") * across + jnp.arange(across)
    latitude = ((global_row.astype(F32) + 0.5) / (across * groups) - 0.5) * (math.pi / 2)
    cosine = jnp.cos(latitude - 0.4)[None, :]

    forcing = forcing_vector.reshape(flat)
    weights = shift_weights.reshape(flat)
    forced, weights, *prepared = call(
        part(prepare_kernel, levels),
        [field, field, field, (2 * padded + 8, across), (24, across), (padded, across)],
        forcing,
        weights,
        inverse,
        matrix,
        absorbed,
        cosine,
    )
    prepared = [forced, weights, *prepared]
    message = (blocks, MESSAGE_ROWS, across)
    tile, side = (padded, across), (3, padded, across)
    message, residual, smooth, rim, inner, outer, *packed = call(
        part(smooth_kernel, levels, tiles, groups, swap),
        [message, field, field, tile, side, side] + [field] * swap,
        *(kelvin if swap else [kelvin]),
        *prepared,
        scratch=[field] * swap,
        sends=True,
    )
    received = gather(message)

    def inner_pairs(size):
        return [(i, i ^ 1) for i in range(size) if i ^ 1 < size]

    def outer_pairs(size, around):
        pairs = [(i, (i + 1) % size) for i in range(1, size, 2) if around or i + 1 < size]
        return pairs + [(j, i) for i, j in pairs]

    inner = lax.ppermute(inner, "tile", inner_pairs(tiles))
    outer = lax.ppermute(outer, "tile", outer_pairs(tiles, True))
    low = lax.ppermute(rim, "grp", inner_pairs(groups))
    high = lax.ppermute(rim, "grp", outer_pairs(groups, False))
    wide = (points + 2, padded, across)
    steps, coarse = call(
        part(coarse_kernel, levels, points, tiles, groups),
        [(saved_rows(tiles, groups), lanes), (1, lanes)],
        received,
    )
    image, second, values, corners = call(
        part(inside_kernel, levels, tiles, groups),
        [wide, wide, (16, across), (4, padded, across)],
        received,
        coarse,
        inner,
        outer,
        smooth,
        weights,
        inverse,
    )
    near = (tiles // 2, 2, padded, across)
    message, second, *sent = call(
        part(second_kernel, levels, groups),
        [(blocks, LAST_ROWS, across), field] + [field, near] * swap,
        low,
        high,
        rim,
        residual,
        weights,
        inverse,
        image,
        second,
        values,
        corners,
        *packed,
        sends=True,
    )
    received = gather(message)
    parts = []
    if swap:
        near = lax.ppermute(sent[1], "tile", inner_pairs(tiles))
        parts = [packed[0], sent[0], near]
        far = call(send_kernel, [(4, padded, across)] * (tiles // 2 - 1), near, packed[0], sent[0])
        for step, value in zip(far_steps(tiles), far):
            parts.append(lax.ppermute(value, "tile", [(i, i ^ step) for i in range(tiles)]))
    solution_field, state = call(
        part(final_kernel, levels, tiles, groups, swap),
        [flat, (-(-(tiles + 2) // 8) * 8, across) if swap else field],
        received,
        steps,
        coarse,
        smooth,
        second,
    )
    if swap:
        (state,) = call(part(state_kernel, levels), [flat], state, *parts, scratch=[field])
    if not swap:
        state = state[:, :levels].reshape(points, levels, tiles, width).transpose(2, 1, 0, 3)
        state = to_tiles(state).transpose(1, 2, 0, 3)
    shape = (levels, points, across)
    return solution_field.reshape(shape), state.reshape(shape)


def solution(mesh):
    return jax.shard_map(
        per_device,
        mesh=mesh,
        in_specs=(
            P(None, "tile", "grp"),
            P(None, "tile", "grp"),
            P(),
            P(None, None, ("tile", "grp")),
            P(),
            P(),
        ),
        out_specs=(P(None, "tile", "grp"), P(None, None, ("tile", "grp"))),
        check_vma=False,
    )
```

```python
import math

import jax
import jax.numpy as jnp
from jax import lax
from jax.experimental import pallas as pl
from jax.experimental.pallas import tpu as pltpu
from jax.sharding import PartitionSpec as P

F32 = jnp.float32
HIGHEST = lax.Precision.HIGHEST
MESSAGE_ROWS = 4
LAST_ROWS = 8
VMEM = pl.BlockSpec(memory_space=pltpu.VMEM)
HBM = pl.BlockSpec(memory_space=pltpu.HBM)


def iota(shape, dim):
    return lax.broadcasted_iota(jnp.int32, shape, dim)


def turn(value, shift, axis=1):
    shift = shift % value.shape[axis]
    return pltpu.roll(value, shift, axis) if shift else value


def total(value):
    return jnp.sum(value, axis=(0, 1), keepdims=True)


def call(kernel, outs, *args, scratch=(), copies=0, sends=False):
    return pl.pallas_call(
        kernel,
        out_shape=[jax.ShapeDtypeStruct(shape, F32) for shape in outs],
        in_specs=[HBM if copies else VMEM] * len(args),
        out_specs=[HBM] * sends + [VMEM] * (len(outs) - sends),
        scratch_shapes=[pltpu.VMEM(shape, F32) for shape in [*scratch, *outs[:sends]]]
        + [pltpu.SemaphoreType.DMA((max(copies, 1),))] * bool(copies or sends),
        compiler_params=pltpu.CompilerParams(vmem_limit_bytes=32 * 1024 * 1024),
    )(*args)


def load_columns(ref, points, levels, padded):
    tiles = []
    whole = levels // 8 * 8
    for i in range(points):
        parts = [ref[pl.ds(i, whole, stride=points), :]]
        if padded > levels:
            last = ref[pl.ds((levels - 8) * points + i, 8, stride=points), :]
            parts += [last[8 - (levels - whole) :], jnp.zeros((padded - levels, last.shape[1]), F32)]
        tiles.append(jnp.concatenate(parts, axis=0))
    return tiles


def store_columns(ref, tiles, levels):
    points, whole = len(tiles), levels // 8 * 8
    for i, tile in enumerate(tiles):
        ref[pl.ds(i, whole, stride=points), :] = tile[:whole]
        if whole < levels:
            ref[pl.ds((levels - 8) * points + i, 8, stride=points), :] = tile[levels - 8 : levels]


def swap_groups(tiles):
    count, lanes = len(tiles), tiles[0].shape[1]
    width = lanes // count
    group = iota(tiles[0].shape, 1) // width
    tiles = [turn(tile, i * width) for i, tile in enumerate(tiles)]
    step = 1
    while step < count:
        here = (group & step) == 0
        tiles = [jnp.where(here, tiles[u], tiles[(u + step) % count]) for u in range(count)]
        step *= 2
    return [turn(tiles[-s % count], -s * width) for s in range(count)]


def pack_kernel(levels, x_ref, packed_ref, near_ref):
    points, padded, _ = packed_ref.shape
    for s, tile in enumerate(swap_groups(load_columns(x_ref, points, levels, padded))):
        packed_ref[s] = tile
    other = 1 - (lax.axis_index("tile") & 1)
    for j in range(points // 2):
        near_ref[j] = packed_ref[2 * j + other]


def far_steps(tiles):
    return list(range(tiles - 2, 0, -2))


def relay_kernel(near_ref, packed_ref, *out_refs):
    tile = lax.axis_index("tile")
    for step, out_ref in zip(far_steps(packed_ref.shape[0]), out_refs):
        place = tile ^ step
        out_ref[0], out_ref[1] = packed_ref[place], near_ref[place >> 1]


def tables_kernel(levels, *refs):
    *vector_refs, inverse_ref, matrix_ref, absorbed_ref = refs[:6]
    *buffer_refs, sems = refs[6:]
    copies = [
        pltpu.make_async_copy(vector_ref, buffer_ref, sems.at[n])
        for n, (vector_ref, buffer_ref) in enumerate(zip(vector_refs, buffer_refs))
    ]
    for copy in copies:
        copy.start()
    for copy in copies:
        copy.wait()
    shape = inverse_ref.shape
    sub, lane = iota(shape, 0), iota(shape, 1)

    def column(row, mask):
        return jnp.broadcast_to(jnp.sum(jnp.where(mask, row, 0.0), axis=1, keepdims=True), shape)

    link, thermal, solar = [
        jnp.concatenate([ref[...], jnp.zeros((1, shape[1] - ref.shape[1]), F32)], axis=1)
        for ref in buffer_refs
    ]
    lower = column(link, lane == sub - 1)
    upper = column(link, lane == sub)
    diagonal = 4.0 + lower + upper
    lower, upper = -lower, -upper
    result = jnp.where(lane == sub, 1.0, 0.0).astype(F32)
    step = 1
    while step < levels:
        inverse = 1.0 / diagonal
        a = -lower * turn(inverse, step, 0)
        c = -upper * turn(inverse, -step, 0)
        diagonal = diagonal + a * turn(upper, step, 0) + c * turn(lower, -step, 0)
        result = result + a * turn(result, step, 0) + c * turn(result, -step, 0)
        lower, upper = a * turn(lower, step, 0), c * turn(upper, -step, 0)
        step *= 2
    valid = (sub < levels) & (lane < levels)
    inverse_ref[...] = jnp.where(valid, result / diagonal, 0.0)

    own = column(thermal, lane == sub)
    top_column = column(thermal, lane < sub)
    bottom_column = column(thermal, lane <= sub)
    top_row = jnp.sum(jnp.where(sub < lane, own, 0.0), axis=0, keepdims=True)
    bottom_row = jnp.sum(jnp.where(sub <= lane, own, 0.0), axis=0, keepdims=True)
    whole = jnp.sum(thermal, axis=1, keepdims=True)
    emitted = 1.0 - jnp.exp(-thermal)

    def decay(mask, gap):
        return jnp.where(mask, jnp.exp(-jnp.where(mask, gap, 0.0)), 0.0)

    below, above = lane < sub, lane > sub
    matrix = decay(below, top_column - bottom_row) - decay(below, bottom_column - bottom_row)
    matrix = matrix + decay(above, top_row - bottom_column) - decay(above, top_row - top_column)
    matrix = (matrix - jnp.where(lane == sub, 2.0, 0.0)) * emitted
    surface = (lane == levels - 1) & (sub < levels)
    matrix = matrix + decay(surface, whole - bottom_column) - decay(surface, whole - top_column)
    matrix_ref[...] = jnp.where(valid, matrix, 0.0)
    entering = column(solar, lane < sub)
    leaving = column(solar, lane <= sub)
    absorbed = 10.0 * (jnp.exp(-entering) - jnp.exp(-leaving))
    absorbed_ref[...] = jnp.where(sub < levels, absorbed, 0.0)


def scalars_row(values, lanes):
    sums = jnp.sum(jnp.concatenate(values, axis=0), axis=1, keepdims=True)
    lane = iota((8, lanes), 1)
    parts = [jnp.where(lane == j, sums[8 * j : 8 * j + 8], 0.0) for j in range(len(values))]
    return jnp.sum(add_all(parts), axis=0, keepdims=True)


def fold(tile):
    parts = [tile[8 * j : 8 * j + 8] for j in range(tile.shape[0] // 8)]
    while len(parts) > 1:
        parts = [a + b for a, b in zip(parts[::2], parts[1::2])] + parts[len(parts) // 2 * 2 :]
    return parts[0]


def add_all(parts):
    parts = list(parts)
    while len(parts) > 1:
        parts = [a + b for a, b in zip(parts[::2], parts[1::2])] + parts[len(parts) // 2 * 2 :]
    return parts[0]


def rim_sums(fields, weights):
    weighted = add_all([fold(a * b) for a, b in zip(fields, weights)])
    every = add_all([fold(tile) for tile in fields])
    lane, across = iota(every.shape, 1), every.shape[1]
    south = jnp.where(lane == 0, every, 0.0)
    north = jnp.where(lane == across - 1, every, 0.0)
    return [weighted, fold(fields[0]), fold(fields[-1]), south, north]


def dot(matrix, tiles):
    across = tiles[0].shape[1]
    field = jnp.concatenate(tiles, axis=1)
    field = jnp.dot(matrix, field, precision=HIGHEST, preferred_element_type=F32)
    return [field[:, i * across : (i + 1) * across] for i in range(len(tiles))]


def prepare_kernel(
    levels,
    forcing_ref,
    weight_ref,
    inverse_ref,
    matrix_ref,
    absorbed_ref,
    cosine_ref,
    forced_ref,
    weight_out_ref,
    base_ref,
    matrices_ref,
    rows_ref,
    unit_ref,
    sums_ref,
):
    points, padded, across = forced_ref.shape
    inverse = inverse_ref[:, :padded]
    sun = absorbed_ref[...] * cosine_ref[...]
    forcing = load_columns(forcing_ref, points, levels, padded)
    rows_ref[16:24] = add_all([fold(tile) for tile in forcing])
    forced = [tile + sun for tile in forcing]
    for i, tile in enumerate(dot(inverse, forced)):
        forced_ref[i] = forced[i]
        base_ref[i] = tile
    weight = load_columns(weight_ref, points, levels, padded)
    for i, tile in enumerate(weight):
        weight_out_ref[i] = tile
    matrices_ref[0:padded] = matrix_ref[...]
    matrices_ref[padded : 2 * padded] = dot(inverse, [matrix_ref[...]])[0]
    heated = jnp.sum(fold(matrix_ref[...]), axis=0, keepdims=True)
    matrices_ref[2 * padded :] = jnp.broadcast_to(heated, (8, across))
    unit_ref[...] = jnp.broadcast_to(
        jnp.sum(inverse_ref[...], axis=1, keepdims=True), unit_ref.shape
    )
    rows_ref[0:8] = add_all([fold(tile) for tile in weight])
    for j, value in enumerate(rim_sums(weight, weight)):
        sums_ref[8 * j : 8 * j + 8] = value
    solar = jnp.sum(fold(sun), axis=0, keepdims=True)
    rows_ref[8:16] = jnp.broadcast_to(solar, (8, across))


def smooth_kernel(levels, tiles, groups, swap, *refs):
    *refs, message_ref, message_sem = refs
    count = len(refs) - 6 - 2 * swap
    *kelvin_refs, forced_ref, weight_ref, base_ref, matrices_ref, rows_ref, unit_ref = refs[:count]
    sent_ref, residual_ref, smooth_ref, rim_ref, inner_ref, outer_ref, *refs = refs[count:]
    points, padded, across = residual_ref.shape
    if swap:
        state_ref, scratch_ref = refs
        tile = lax.axis_index("tile")
        packed_ref, near_ref, *far_refs = kelvin_refs
        scratch_ref[tile], scratch_ref[tile ^ 1] = packed_ref[tile], near_ref[tile >> 1]
        for step, far_ref in zip(far_steps(points), far_refs):
            scratch_ref[tile ^ step], scratch_ref[tile ^ (step + 1)] = far_ref[0], far_ref[1]
        kelvin = swap_groups([scratch_ref[i] for i in range(points)])
    else:
        kelvin = [kelvin_refs[0][i] for i in range(points)]
    squares = [tile * tile for tile in kelvin]
    emission = [tile * tile for tile in squares]
    both = dot(matrices_ref[padded:, :padded], emission)
    solar, unit = rows_ref[8:9, :], unit_ref[...]
    means = [(tile[padded : padded + 1] + solar) * (1.0 / levels) for tile in both]
    smooth = [base_ref[i] + (both[i][:padded] - unit * means[i]) for i in range(points)]
    for i in range(points):
        smooth_ref[i] = smooth[i]
    weight = [weight_ref[i] for i in range(points)]
    folded = [fold(tile) for tile in smooth]
    loss = add_all([fold(a * b) for a, b in zip(smooth, weight)])
    mass = rows_ref[0:8, :]
    every = add_all(folded)
    lane = iota(every.shape, 1)
    scalars = scalars_row(
        [
            rows_ref[16:24, :] - loss,
            folded[0],
            folded[-1],
            jnp.where(lane == 0, every, 0.0),
            jnp.where(lane == across - 1, every, 0.0),
            mass,
        ],
        across,
    )
    lane = iota((padded, across), 1)
    corner = jnp.where((lane == 0) | (lane == across - 1), smooth[0], turn(smooth[-1], 2))
    rows = jnp.concatenate([corner, jnp.zeros((across - padded, across), F32)], axis=0).T
    scalars = turn(scalars, padded)
    message_ref[...] = jnp.zeros(message_ref.shape, F32)
    message_ref[:, 0, :] = jnp.broadcast_to(scalars, (message_ref.shape[0], across))
    corners = (0, 2, across - 1, 1)
    for place, corner in zip(neighbours(tiles, groups)[5:], corners):
        message_ref[pl.ds(place, 1), 0, :] = rows[corner : corner + 1] + scalars
    send = pltpu.make_async_copy(message_ref, sent_ref, message_sem.at[0])
    send.start()

    heat = dot(matrices_ref[:padded, :padded], emission)
    real = iota((padded, across), 0) < levels
    for i in range(points):
        residual_ref[i] = forced_ref[i] + jnp.where(real, heat[i] - means[i], 0.0)
    stride = across // points
    rim = jnp.zeros((padded, across), F32)
    for i in range(points):
        place = (lane - stride * i + 2) & (across - 1)
        rim = jnp.where(place < 4, turn(smooth[i], stride * i), rim)
        rim = jnp.where((place == 5) | (place == 6), turn(weight[i], stride * i + 4), rim)
    rim_ref[...] = rim
    even = lax.rem(lax.axis_index("tile"), 2) == 0
    sides = zip((smooth[0], smooth[1], weight[0]), (smooth[-2], smooth[-1], weight[-1]))
    for j, (west, east) in enumerate(sides):
        inner_ref[j] = jnp.where(even, east, west)
        outer_ref[j] = jnp.where(even, west, east)
    if swap:
        for s, tile in enumerate(swap_groups(smooth)):
            state_ref[s] = tile
    send.wait()


def send_kernel(near_ref, smooth_ref, second_ref, *out_refs):
    tile = lax.axis_index("tile")
    for step, out_ref in zip(far_steps(smooth_ref.shape[0]), out_refs):
        place = tile ^ step
        out_ref[0], out_ref[1] = smooth_ref[place], second_ref[place]
        out_ref[2], out_ref[3] = near_ref[place >> 1, 0], near_ref[place >> 1, 1]


def neighbours(tiles, groups):
    tile, group = lax.axis_index("tile"), lax.axis_index("grp")
    west, east = lax.rem(tile + tiles - 1, tiles), lax.rem(tile + 1, tiles)
    south, north = jnp.maximum(group - 1, 0), jnp.minimum(group + 1, groups - 1)
    pairs = [(tile, group), (west, group), (east, group), (tile, south), (tile, north)]
    pairs += [(west, south), (east, south), (west, north), (east, north)]
    return [x * groups + y for x, y in pairs]


def small_inverse(block):
    size = len(block)
    block = [list(row) for row in block]
    for k in range(size):
        pivot = 1.0 / block[k][k]
        row = [block[k][j] * pivot for j in range(size)]
        for i in range(size):
            if i != k:
                factor = block[i][k]
                for j in range(size):
                    if j != k:
                        block[i][j] = block[i][j] - factor * row[j]
                block[i][k] = -factor * pivot
        for j in range(size):
            block[k][j] = row[j]
        block[k][k] = pivot
    return block


def product(a, b):
    size = range(len(a))
    return [[add_all([a[i][k] * b[k][j] for k in size]) for j in size] for i in size]


def apply(a, v):
    size = range(len(a))
    return [add_all([a[i][k] * v[k] for k in size]) for i in size]


def flip(a):
    return [list(row) for row in zip(*a)]


def turn_block(a, shift):
    return [[turn(value, shift) for value in row] for row in a]


def with_diagonal(block, row_sums, beside):
    size = range(len(block))
    return [
        [
            row_sums[i] - add_all([block[i][k] for k in size if k != i] + beside[i]) if i == j else block[i][j]
            for j in size
        ]
        for i in size
    ]


def coarse_factor(mass, tiles, groups, x_face, y_face):
    zero = jnp.zeros_like(mass)
    size = range(groups)
    diagonal = [[zero - y_face if abs(i - j) == 1 else zero for i in size] for j in size]
    coupling = [[zero - x_face if i == j else zero for i in size] for j in size]
    row_sums = [turn(mass, -j) for j in size]
    diagonal = with_diagonal(diagonal, row_sums, [[zero - 2.0 * x_face]] * groups)
    steps = []
    step = 1
    while step < tiles:
        inverse = small_inverse(diagonal)
        shift = step * groups
        steps.append((inverse, coupling))
        left = product(coupling, turn_block(inverse, shift))
        low = product(left, flip(coupling))
        high = turn_block(product(flip(coupling), product(inverse, coupling)), -shift)
        row_sums = reduce_sums(inverse, coupling, row_sums, shift)
        diagonal = [[diagonal[i][j] - (low[i][j] + high[i][j]) for j in size] for i in size]
        coupling = [[-v for v in row] for row in product(left, turn_block(coupling, shift))]
        step *= 2
        beside = [
            [add_all(coupling[i]), turn(add_all(flip(coupling)[i]), -step * groups)] for i in size
        ]
        diagonal = with_diagonal(diagonal, row_sums, beside)
    last = [[diagonal[i][j] + (coupling[i][j] + coupling[j][i]) for j in size] for i in size]
    last = with_diagonal(last, row_sums, [[]] * groups)
    return steps, small_inverse(last)


def reduce_sums(inverse, coupling, values, shift):
    scaled = apply(inverse, values)
    low = apply(coupling, [turn(v, shift) for v in scaled])
    high = [turn(v, -shift) for v in apply(flip(coupling), scaled)]
    return [v - (a + b) for v, a, b in zip(values, low, high)]


def coarse_solve(steps, last, sums, groups):
    values = [turn(sums, -j) for j in range(groups)]
    shift = groups
    for inverse, coupling in steps:
        values = reduce_sums(inverse, coupling, values, shift)
        shift *= 2
    values = apply(last, values)
    residue = iota(sums.shape, 1) % groups
    result = values[0]
    for j in range(1, groups):
        result = jnp.where(residue == j, turn(values[j], j), result)
    return result


def around(row, groups):
    residue = iota(row.shape, 1) % groups
    south = jnp.where(residue == 0, row, turn(row, 1))
    north = jnp.where(residue == groups - 1, row, turn(row, -1))
    return turn(row, groups), turn(row, -groups), south, north


def by_block(received):
    blocks, lanes = received.shape
    if blocks < lanes:
        received = jnp.concatenate([received] * (lanes // blocks), axis=0)
    return received.T


def save_steps(ref, steps, last):
    rows = [v for inverse, coupling in steps for block in (inverse, coupling) for row in block for v in row]
    rows += [v for row in last for v in row]
    for n, row in enumerate(rows):
        ref[n : n + 1, :] = row


def saved_rows(tiles, groups):
    steps = max(tiles - 1, 0).bit_length()
    return (2 * steps + 1) * groups * groups


def load_steps(ref, tiles, groups):
    place = 0
    blocks = []
    for _ in range(2 * max(tiles - 1, 0).bit_length() + 1):
        block = []
        for _ in range(groups):
            block.append([ref[place + j : place + j + 1, :] for j in range(groups)])
            place += groups
        blocks.append(block)
    return list(zip(blocks[:-1:2], blocks[1::2])), blocks[-1]


def coarse_kernel(levels, points, tiles, groups, received_ref, steps_ref, coarse_ref):
    padded = -(-levels // 8) * 8
    scalars = by_block(received_ref[:, 0, :])
    base, west, east, south, north, mass = [scalars[padded + j : padded + j + 1, :] for j in range(6)]
    residue = iota(base.shape, 1) % groups
    facing_south = jnp.where(residue == 0, south, turn(north, 1))
    facing_north = jnp.where(residue == groups - 1, north, turn(south, -1))
    sums = base + (
        (turn(east, groups) - west)
        + (turn(west, -groups) - east)
        + (facing_south - south)
        + (facing_north - north)
    )
    steps, last = coarse_factor(
        mass, tiles, groups, float(levels * received_ref.shape[2]), float(levels * points)
    )
    coarse = coarse_solve(steps, last, sums, groups)
    save_steps(steps_ref, steps, last)
    coarse_ref[...] = coarse


def beyond(groups, lane, across, none=-1):
    group = lax.axis_index("grp")
    south = jnp.where(group == 0, 0, none)
    north = jnp.where(group == groups - 1, across - 1, none)
    return (lane == south) | (lane == north)


def inside_kernel(
    levels,
    tiles,
    groups,
    received_ref,
    coarse_ref,
    inner_ref,
    outer_ref,
    smooth_ref,
    residual_ref,
    weight_ref,
    inverse_ref,
    image_ref,
    second_ref,
    values_ref,
    corners_ref,
    sums_ref,
):
    points, padded, across = smooth_ref.shape
    coarse = coarse_ref[...]
    places = neighbours(tiles, groups)
    lane = iota(coarse.shape, 1)
    picked = [jnp.sum(jnp.where(lane == place, coarse, 0.0), axis=1, keepdims=True) for place in places]
    for j, value in enumerate(picked):
        values_ref[j : j + 1, :] = jnp.broadcast_to(value, (1, across))
    shape = (padded, across)
    real = iota(shape, 0) < levels
    own, e_west, e_east, e_south, e_north, e_sw, e_se, e_nw, e_ne = [
        jnp.where(real, value, 0.0) for value in picked
    ]

    corner_rows = [received_ref[pl.ds(place, 1), 0, :] for place in places[5:]]
    corner_rows = [jnp.where(iota(row.shape, 1) < padded, row, 0.0) for row in corner_rows]
    corners = jnp.concatenate(corner_rows + [jnp.zeros((across - 4, across), F32)], axis=0).T
    c_sw, c_se, c_nw, c_ne = [corners[:padded, j : j + 1] for j in range(4)]

    for j, corner in enumerate((c_sw, c_se, c_nw, c_ne)):
        corners_ref[j] = jnp.broadcast_to(corner, shape)

    lane = iota(shape, 1)
    first, final = lane == 0, lane == across - 1

    outside = beyond(groups, lane, across)

    def across_sum(tile, ends):
        ends = jnp.where(outside, tile, ends)
        return jnp.where(first, ends, turn(tile, 1)) + jnp.where(final, ends, turn(tile, -1))

    even_tile = lax.rem(lax.axis_index("tile"), 2) == 0
    weight = [weight_ref[i] for i in range(points)]
    from_west = [jnp.where(even_tile, outer_ref[j], inner_ref[j]) for j in range(3)]
    from_east = [jnp.where(even_tile, inner_ref[j], outer_ref[j]) for j in range(3)]
    weight = from_west[2:] + weight + from_east[2:]
    field = from_west[:2] + [smooth_ref[i] for i in range(points)] + from_east[:2]

    ends = [jnp.where(first, c_sw, c_nw), *[jnp.zeros(shape, F32)] * points, jnp.where(first, c_se, c_ne)]

    def steps(here, low, high):
        return jnp.where(first, here - low, jnp.where(final, here - high, 0.0))

    here = [e_west] + [own] * points + [e_east]
    jumps = [steps(e_west, e_sw, e_nw) + (e_west - own)]
    jumps += [steps(own, e_south, e_north)] * points
    jumps += [steps(e_east, e_se, e_ne) + (e_east - own)]
    jumps[1] = jumps[1] + (own - e_west)
    jumps[points] = jumps[points] + (own - e_east)
    image = [
        (field[i] + field[i + 2])
        + across_sum(field[i + 1], ends[i])
        - (weight[i] * (field[i + 1] + here[i]) + jumps[i])
        for i in range(points + 2)
    ]
    residual = [residual_ref[i] for i in range(points)]
    for j, value in enumerate(rim_sums(residual, weight[1 : points + 1])):
        sums_ref[8 * j : 8 * j + 8] = value
    smoothed = dot(inverse_ref[:, :padded], image)
    for i in range(points + 2):
        image_ref[i] = image[i]
        second_ref[i] = field[i + 1] - smoothed[i]


def second_kernel(
    levels,
    groups,
    low_ref,
    high_ref,
    rim_ref,
    residual_ref,
    weight_ref,
    inverse_ref,
    image_ref,
    second_ref_in,
    values_ref,
    corners_ref,
    residual_sums_ref,
    weight_sums_ref,
    *refs,
):
    *refs, message_ref, message_sem = refs
    swap = len(refs) > 2
    if swap:
        packed_smooth_ref, sent_ref, second_ref, packed_ref, near_ref = refs
    else:
        sent_ref, second_ref = refs
    points, padded, across = residual_ref.shape
    blocks = message_ref.shape[0]
    stride = across // points
    even_group = lax.rem(lax.axis_index("grp"), 2) == 0

    shape = (padded, across)
    real = iota(shape, 0) < levels
    values = [values_ref[j : j + 1, :] for j in range(9)]
    own, e_west, e_east, e_south, e_north, e_sw, e_se, e_nw, e_ne = [
        jnp.where(real, value, 0.0) for value in values
    ]
    c_sw, c_se, c_nw, c_ne = [corners_ref[j] for j in range(4)]
    weight = [weight_ref[i] for i in range(points)]
    lane = iota(shape, 1)
    first, final = lane == 0, lane == across - 1
    outside = beyond(groups, lane, across)
    inside = lane & (stride - 1)
    is_south, is_north = inside == stride - 1, inside == 0
    rim, low, high = rim_ref[...], low_ref[...], high_ref[...]
    from_south = jnp.where(even_group, high, low)
    from_north = jnp.where(even_group, low, high)
    outer = beyond(groups, jnp.where(is_north, 0, jnp.where(is_south, across - 1, 1)), across)
    both = jnp.where(is_north, turn(from_south, 1), turn(from_north, -1))
    both = jnp.where((is_north | is_south) & jnp.logical_not(outer), both, 0.0)
    edge = stride * (points - 1)

    def ring_image(tile, step, here, west, east, west_lane, east_lane, c_west, c_east):
        rim_weight = turn(tile, -4)
        spread = (here - own) + jnp.where(lane == west_lane, here - west, jnp.where(lane == east_lane, here - east, 0.0))
        return (
            jnp.where(lane == west_lane, c_west, turn(tile, stride))
            + jnp.where(lane == east_lane, c_east, turn(tile, -stride))
            + (turn(tile, step) + turn(rim, -step))
            - (rim_weight * (tile + here) + spread)
        )

    ring_south = ring_image(from_south, 1, e_south, e_sw, e_se, across - 1, edge - 1, c_sw, c_se)
    ring_north = ring_image(from_north, -1, e_north, e_nw, e_ne, 0, edge, c_nw, c_ne)
    ring = jnp.where(is_south, ring_south, jnp.where(is_north, ring_north, 0.0))
    ring_field = jnp.where(is_south, from_south, from_north)
    ring, smoothed = dot(inverse_ref[:, :padded], [ring, both])
    ring = ring_field - ring
    second, image = [second_ref_in[0]], [None]
    ends = first | final
    for i in range(1, points + 1):
        shift = -stride * (i - 1)
        image.append(jnp.where(ends, image_ref[i] + turn(both, shift), image_ref[i]))
        second.append(jnp.where(ends, second_ref_in[i] - turn(smoothed, shift), second_ref_in[i]))
    second.append(second_ref_in[points + 1])
    both = jnp.where(is_north, turn(ring, 1), turn(ring, -1))

    names = ("image", "change")
    pairs = {}
    sides = {name: [] for name in names}
    left = []

    def collect(key, value):
        pairs.setdefault(key, []).append(fold(value))

    for i in range(points):
        tile = second[i + 1]
        second_ref[i] = tile
        ends = jnp.where(outside, tile, turn(both, -stride * i))
        again = (
            (second[i] + second[i + 2])
            + (jnp.where(first, ends, turn(tile, 1)) + jnp.where(final, ends, turn(tile, -1)))
            - weight[i] * tile
        )
        residual = residual_ref[i]
        result = residual - image[i + 1]
        change = result - again
        left.append(fold(again + (result - 4.0 * tile)))
        heavy = weight[i]
        collect("qq", result * result)
        collect("rq", residual * result)
        collect("qd", result * change)
        collect("dd", change * change)
        collect("rd", residual * change)
        for name, value in zip(names, (result, change)):
            sides[name].append(fold(value))
            collect("w" + name, heavy * value)
    pairs = {key: add_all(value) for key, value in pairs.items()}
    lane = iota(pairs["qq"].shape, 1)
    out = [pairs[key] for key in ("qq", "rq", "qd", "dd", "rd")]
    for name in names:
        every = add_all(sides[name])
        out += [
            pairs["w" + name],
            sides[name][0],
            sides[name][-1],
            jnp.where(lane == 0, every, 0.0),
            jnp.where(lane == across - 1, every, 0.0),
        ]
    for sums_ref in (residual_sums_ref, weight_sums_ref):
        out += [sums_ref[8 * j : 8 * j + 8] for j in range(5)]
    out.append(add_all(left))
    row = scalars_row(out, across)
    message_ref[...] = jnp.zeros(message_ref.shape, F32)
    message_ref[:, 0, :] = jnp.broadcast_to(row, (blocks, across))
    send = pltpu.make_async_copy(message_ref, sent_ref, message_sem.at[0])
    send.start()
    if swap:
        for s, tile in enumerate(swap_groups(second[1 : points + 1])):
            packed_ref[s] = tile
        other = 1 - (lax.axis_index("tile") & 1)
        for j in range(points // 2):
            near_ref[j, 0] = packed_smooth_ref[2 * j + other]
            near_ref[j, 1] = packed_ref[2 * j + other]
    send.wait()


def final_kernel(
    levels,
    tiles,
    groups,
    swap,
    received_ref,
    steps_ref,
    coarse_ref,
    smooth_ref,
    second_ref,
    field_ref,
    other_ref,
):
    points, padded, across = smooth_ref.shape
    blocks = tiles * groups
    rows = by_block(received_ref[:, 0, :])
    rows = [rows[j : j + 1, :] for j in range(26)]
    steps, last = load_steps(steps_ref, tiles, groups)
    coarse = coarse_solve(steps, last, rows[25], groups)
    jumps = [coarse - near for near in around(coarse, groups)]

    def against(part):
        return add_all([rows[part] * coarse] + [rows[part + 1 + j] * jumps[j] for j in range(4)])

    j_w, j_e, j_s, j_n = jumps
    x_face, y_face = float(levels * across), float(levels * points)
    weighted = add_all([rows[21 + j] * jumps[j] for j in range(4)])
    square = (
        coarse * (rows[20] * coarse + 2.0 * weighted)
        + x_face * (j_w * j_w + j_e * j_e)
        + y_face * (j_s * j_s + j_n * j_n)
        + (2.0 * levels) * ((j_w + j_e) * (j_s + j_n))
    )
    lane = iota(coarse.shape, 1)
    tile, group = lax.axis_index("tile"), lax.axis_index("grp")
    parts = [
        rows[0],
        rows[1],
        rows[2] + against(5),
        rows[3] + 2.0 * against(10) + square,
        rows[4] + against(15),
    ]
    parts = [jnp.where(lane < blocks, part, 0.0) for part in parts]
    parts += [jnp.zeros_like(coarse)] * 3
    sums = jnp.sum(jnp.concatenate(parts, axis=0), axis=1, keepdims=True)
    qq, rq, qv, vv, rv = [sums[j : j + 1, :] for j in range(5)]
    alpha = rq / qq
    beta = qv / qq
    kappa = (rv - alpha * qv) / (vv - beta * qv)
    scale = alpha - kappa * beta
    constant = scale * coarse_ref[...] + kappa * coarse
    others = tiles if swap else 1
    parts = [jnp.where(lane == (tile ^ k) * groups + group, constant, 0.0) for k in range(others)]
    parts += [jnp.zeros_like(coarse)] * (-others % 8)
    shifts = jnp.sum(jnp.concatenate(parts, axis=0), axis=1, keepdims=True)
    shifts = [shifts[k : k + 1, :] for k in range(others)]
    result = [scale * smooth_ref[i] + (kappa * second_ref[i] + shifts[0]) for i in range(points)]
    store_columns(field_ref, result, levels)
    if swap:
        rows = jnp.concatenate([scale, kappa] + shifts, axis=0)
        rows = jnp.concatenate([rows, jnp.zeros((other_ref.shape[0] - rows.shape[0], 1), F32)], axis=0)
        other_ref[...] = jnp.broadcast_to(rows, other_ref.shape)
    else:
        for i in range(points):
            other_ref[i] = result[i]


def state_kernel(levels, scalars_ref, *refs):
    smooth_ref, second_ref, near_ref, *part_refs, state_ref, scratch_ref = refs
    tile = lax.axis_index("tile")
    scale, kappa = scalars_ref[0:1, :], scalars_ref[1:2, :]
    pairs = {0: (smooth_ref[tile], second_ref[tile]), 1: (near_ref[tile >> 1, 0], near_ref[tile >> 1, 1])}
    for step, part_ref in zip(far_steps(smooth_ref.shape[0]), part_refs):
        pairs[step] = (part_ref[0], part_ref[1])
        pairs[step + 1] = (part_ref[2], part_ref[3])
    for k, (smooth, second) in pairs.items():
        scratch_ref[tile ^ k] = scale * smooth + (kappa * second + scalars_ref[2 + k : 3 + k, :])
    store_columns(state_ref, swap_groups([scratch_ref[s] for s in range(len(pairs))]), levels)


def per_device(
    forcing_vector,
    shift_weights,
    layer_link_factor,
    previous_kelvin_field,
    longwave_opacity,
    shortwave_opacity,
):
    tiles, groups = lax.axis_size("tile"), lax.axis_size("grp")
    levels, points, across = forcing_vector.shape
    padded = -(-levels // 8) * 8
    blocks = tiles * groups
    lanes = max(across, blocks)
    width = across // tiles
    swap = tiles == points
    flat = (levels * points, across)
    field = (points, padded, across)

    def to_tiles(value):
        return lax.all_to_all(value, "tile", split_axis=0, concat_axis=0, tiled=True)

    def gather(value):
        return lax.all_to_all(value, ("tile", "grp"), split_axis=0, concat_axis=0, tiled=True)

    def part(kernel, *settings):
        return lambda *refs: kernel(*settings, *refs)

    kelvin = previous_kelvin_field
    if swap:
        near = (tiles // 2, padded, across)
        packed, near = call(part(pack_kernel, levels), [field, near], kelvin.reshape(flat))
        near = lax.ppermute(near, "tile", [(i, i ^ 1) for i in range(tiles)])
        far = call(relay_kernel, [(2, padded, across)] * (tiles // 2 - 1), near, packed)
        kelvin = [packed, near] + [
            lax.ppermute(value, "tile", [(i, i ^ step) for i in range(tiles)])
            for step, value in zip(far_steps(tiles), far)
        ]
    else:
        kelvin = kelvin.reshape(levels, points, tiles, width).transpose(2, 1, 0, 3)
        kelvin = to_tiles(kelvin).transpose(1, 2, 0, 3).reshape(points, levels, across)
        kelvin = jnp.pad(kelvin, ((0, 0), (0, padded - levels), (0, 0)))

    vectors = [v[None, :] for v in (layer_link_factor, longwave_opacity, shortwave_opacity)]
    inverse, matrix, absorbed = call(
        part(tables_kernel, levels),
        [(padded, across)] * 3,
        *vectors,
        scratch=[v.shape for v in vectors],
        copies=len(vectors),
    )
    global_row = lax.axis_index("grp") * across + jnp.arange(across)
    latitude = ((global_row.astype(F32) + 0.5) / (across * groups) - 0.5) * (math.pi / 2)
    cosine = jnp.cos(latitude - 0.4)[None, :]

    forcing = forcing_vector.reshape(flat)
    weights = shift_weights.reshape(flat)
    forced, weights, *prepared, weight_sums = call(
        part(prepare_kernel, levels),
        [field, field, field, (2 * padded + 8, across), (24, across), (padded, across), (40, across)],
        forcing,
        weights,
        inverse,
        matrix,
        absorbed,
        cosine,
    )
    prepared = [forced, weights, *prepared]
    message = (blocks, MESSAGE_ROWS, across)
    tile, side = (padded, across), (3, padded, across)
    message, residual, smooth, rim, inner, outer, *packed = call(
        part(smooth_kernel, levels, tiles, groups, swap),
        [message, field, field, tile, side, side] + [field] * swap,
        *(kelvin if swap else [kelvin]),
        *prepared,
        scratch=[field] * swap,
        sends=True,
    )
    received = gather(message)

    def inner_pairs(size):
        return [(i, i ^ 1) for i in range(size) if i ^ 1 < size]

    def outer_pairs(size, around):
        pairs = [(i, (i + 1) % size) for i in range(1, size, 2) if around or i + 1 < size]
        return pairs + [(j, i) for i, j in pairs]

    inner = lax.ppermute(inner, "tile", inner_pairs(tiles))
    outer = lax.ppermute(outer, "tile", outer_pairs(tiles, True))
    low = lax.ppermute(rim, "grp", inner_pairs(groups))
    high = lax.ppermute(rim, "grp", outer_pairs(groups, False))
    wide = (points + 2, padded, across)
    steps, coarse = call(
        part(coarse_kernel, levels, points, tiles, groups),
        [(saved_rows(tiles, groups), lanes), (1, lanes)],
        received,
    )
    image, second, values, corners, residual_sums = call(
        part(inside_kernel, levels, tiles, groups),
        [wide, wide, (16, across), (4, padded, across), (40, across)],
        received,
        coarse,
        inner,
        outer,
        smooth,
        residual,
        weights,
        inverse,
    )
    near = (tiles // 2, 2, padded, across)
    message, second, *sent = call(
        part(second_kernel, levels, groups),
        [(blocks, LAST_ROWS, across), field] + [field, near] * swap,
        low,
        high,
        rim,
        residual,
        weights,
        inverse,
        image,
        second,
        values,
        corners,
        residual_sums,
        weight_sums,
        *packed,
        sends=True,
    )
    received = gather(message)
    parts = []
    if swap:
        near = lax.ppermute(sent[1], "tile", inner_pairs(tiles))
        parts = [packed[0], sent[0], near]
        far = call(send_kernel, [(4, padded, across)] * (tiles // 2 - 1), near, packed[0], sent[0])
        for step, value in zip(far_steps(tiles), far):
            parts.append(lax.ppermute(value, "tile", [(i, i ^ step) for i in range(tiles)]))
    solution_field, state = call(
        part(final_kernel, levels, tiles, groups, swap),
        [flat, (-(-(tiles + 2) // 8) * 8, across) if swap else field],
        received,
        steps,
        coarse,
        smooth,
        second,
    )
    if swap:
        (state,) = call(part(state_kernel, levels), [flat], state, *parts, scratch=[field])
    if not swap:
        state = state[:, :levels].reshape(points, levels, tiles, width).transpose(2, 1, 0, 3)
        state = to_tiles(state).transpose(1, 2, 0, 3)
    shape = (levels, points, across)
    return solution_field.reshape(shape), state.reshape(shape)


def solution(mesh):
    return jax.shard_map(
        per_device,
        mesh=mesh,
        in_specs=(
            P(None, "tile", "grp"),
            P(None, "tile", "grp"),
            P(),
            P(None, None, ("tile", "grp")),
            P(),
            P(),
        ),
        out_specs=(P(None, "tile", "grp"), P(None, None, ("tile", "grp"))),
        check_vma=False,
    )
```

```python
import math

import jax
import jax.numpy as jnp
from jax import lax
from jax.experimental import pallas as pl
from jax.experimental.pallas import tpu as pltpu
from jax.sharding import PartitionSpec as P

F32 = jnp.float32
HIGHEST = lax.Precision.HIGHEST
MESSAGE_ROWS = 4
LAST_ROWS = 8
VMEM = pl.BlockSpec(memory_space=pltpu.VMEM)
HBM = pl.BlockSpec(memory_space=pltpu.HBM)


def iota(shape, dim):
    return lax.broadcasted_iota(jnp.int32, shape, dim)


def turn(value, shift, axis=1):
    shift = shift % value.shape[axis]
    return pltpu.roll(value, shift, axis) if shift else value


def total(value):
    return jnp.sum(value, axis=(0, 1), keepdims=True)


def call(kernel, outs, *args, scratch=(), copies=0, sends=False):
    return pl.pallas_call(
        kernel,
        out_shape=[jax.ShapeDtypeStruct(shape, F32) for shape in outs],
        in_specs=[HBM if copies else VMEM] * len(args),
        out_specs=[HBM] * sends + [VMEM] * (len(outs) - sends),
        scratch_shapes=[pltpu.VMEM(shape, F32) for shape in [*scratch, *outs[:sends]]]
        + [pltpu.SemaphoreType.DMA((max(copies, 1),))] * bool(copies or sends),
        compiler_params=pltpu.CompilerParams(vmem_limit_bytes=32 * 1024 * 1024),
    )(*args)


def load_columns(ref, points, levels, padded):
    tiles = []
    whole = levels // 8 * 8
    for i in range(points):
        parts = [ref[pl.ds(i, whole, stride=points), :]]
        if padded > levels:
            last = ref[pl.ds((levels - 8) * points + i, 8, stride=points), :]
            parts += [last[8 - (levels - whole) :], jnp.zeros((padded - levels, last.shape[1]), F32)]
        tiles.append(jnp.concatenate(parts, axis=0))
    return tiles


def store_columns(ref, tiles, levels):
    points, whole = len(tiles), levels // 8 * 8
    for i, tile in enumerate(tiles):
        ref[pl.ds(i, whole, stride=points), :] = tile[:whole]
        if whole < levels:
            ref[pl.ds((levels - 8) * points + i, 8, stride=points), :] = tile[levels - 8 : levels]


def swap_groups(tiles):
    count, lanes = len(tiles), tiles[0].shape[1]
    width = lanes // count
    group = iota(tiles[0].shape, 1) // width
    tiles = [turn(tile, i * width) for i, tile in enumerate(tiles)]
    step = 1
    while step < count:
        here = (group & step) == 0
        tiles = [jnp.where(here, tiles[u], tiles[(u + step) % count]) for u in range(count)]
        step *= 2
    return [turn(tiles[-s % count], -s * width) for s in range(count)]


def pack_kernel(levels, x_ref, packed_ref, near_ref):
    points, padded, _ = packed_ref.shape
    for s, tile in enumerate(swap_groups(load_columns(x_ref, points, levels, padded))):
        packed_ref[s] = tile
    other = 1 - (lax.axis_index("tile") & 1)
    for j in range(points // 2):
        near_ref[j] = packed_ref[2 * j + other]


def far_steps(tiles):
    return list(range(tiles - 2, 0, -2))


def relay_kernel(near_ref, packed_ref, *out_refs):
    tile = lax.axis_index("tile")
    for step, out_ref in zip(far_steps(packed_ref.shape[0]), out_refs):
        place = tile ^ step
        out_ref[0], out_ref[1] = packed_ref[place], near_ref[place >> 1]


def tables_kernel(levels, *refs):
    *vector_refs, inverse_ref, matrix_ref, absorbed_ref = refs[:6]
    *buffer_refs, sems = refs[6:]
    copies = [
        pltpu.make_async_copy(vector_ref, buffer_ref, sems.at[n])
        for n, (vector_ref, buffer_ref) in enumerate(zip(vector_refs, buffer_refs))
    ]
    for copy in copies:
        copy.start()
    for copy in copies:
        copy.wait()
    shape = inverse_ref.shape
    sub, lane = iota(shape, 0), iota(shape, 1)

    def column(row, mask):
        return jnp.broadcast_to(jnp.sum(jnp.where(mask, row, 0.0), axis=1, keepdims=True), shape)

    link, thermal, solar = [
        jnp.concatenate([ref[...], jnp.zeros((1, shape[1] - ref.shape[1]), F32)], axis=1)
        for ref in buffer_refs
    ]
    lower = column(link, lane == sub - 1)
    upper = column(link, lane == sub)
    diagonal = 4.0 + lower + upper
    lower, upper = -lower, -upper
    result = jnp.where(lane == sub, 1.0, 0.0).astype(F32)
    step = 1
    while step < levels:
        inverse = 1.0 / diagonal
        a = -lower * turn(inverse, step, 0)
        c = -upper * turn(inverse, -step, 0)
        diagonal = diagonal + a * turn(upper, step, 0) + c * turn(lower, -step, 0)
        result = result + a * turn(result, step, 0) + c * turn(result, -step, 0)
        lower, upper = a * turn(lower, step, 0), c * turn(upper, -step, 0)
        step *= 2
    valid = (sub < levels) & (lane < levels)
    inverse_ref[...] = jnp.where(valid, result / diagonal, 0.0)

    own = column(thermal, lane == sub)
    top_column = column(thermal, lane < sub)
    bottom_column = column(thermal, lane <= sub)
    top_row = jnp.sum(jnp.where(sub < lane, own, 0.0), axis=0, keepdims=True)
    bottom_row = jnp.sum(jnp.where(sub <= lane, own, 0.0), axis=0, keepdims=True)
    whole = jnp.sum(thermal, axis=1, keepdims=True)
    emitted = 1.0 - jnp.exp(-thermal)

    def decay(mask, gap):
        return jnp.where(mask, jnp.exp(-jnp.where(mask, gap, 0.0)), 0.0)

    below, above = lane < sub, lane > sub
    matrix = decay(below, top_column - bottom_row) - decay(below, bottom_column - bottom_row)
    matrix = matrix + decay(above, top_row - bottom_column) - decay(above, top_row - top_column)
    matrix = (matrix - jnp.where(lane == sub, 2.0, 0.0)) * emitted
    surface = (lane == levels - 1) & (sub < levels)
    matrix = matrix + decay(surface, whole - bottom_column) - decay(surface, whole - top_column)
    matrix_ref[...] = jnp.where(valid, matrix, 0.0)
    entering = column(solar, lane < sub)
    leaving = column(solar, lane <= sub)
    absorbed = 10.0 * (jnp.exp(-entering) - jnp.exp(-leaving))
    absorbed_ref[...] = jnp.where(sub < levels, absorbed, 0.0)


def scalars_row(values, lanes):
    count = len(values)
    padded = -(-count // 8) * 8
    rows = [jnp.sum(value, axis=0, keepdims=True) for value in values]
    rows += [jnp.zeros_like(rows[0])] * (padded - count)
    sums = jnp.sum(jnp.concatenate(rows, axis=0), axis=1, keepdims=True)
    shape = (padded, lanes)
    spread = jnp.where(iota(shape, 0) == iota(shape, 1), sums, 0.0)
    return jnp.sum(spread, axis=0, keepdims=True)


def fold(tile):
    parts = [tile[8 * j : 8 * j + 8] for j in range(tile.shape[0] // 8)]
    while len(parts) > 1:
        parts = [a + b for a, b in zip(parts[::2], parts[1::2])] + parts[len(parts) // 2 * 2 :]
    return parts[0]


def add_all(parts):
    parts = list(parts)
    while len(parts) > 1:
        parts = [a + b for a, b in zip(parts[::2], parts[1::2])] + parts[len(parts) // 2 * 2 :]
    return parts[0]


def dot(matrix, tiles):
    across = tiles[0].shape[1]
    field = jnp.concatenate(tiles, axis=1)
    field = jnp.dot(matrix, field, precision=HIGHEST, preferred_element_type=F32)
    return [field[:, i * across : (i + 1) * across] for i in range(len(tiles))]


def prepare_kernel(
    levels,
    forcing_ref,
    weight_ref,
    inverse_ref,
    matrix_ref,
    absorbed_ref,
    cosine_ref,
    forced_ref,
    weight_out_ref,
    base_ref,
    matrices_ref,
    rows_ref,
    unit_ref,
):
    points, padded, across = forced_ref.shape
    inverse = inverse_ref[:, :padded]
    sun = absorbed_ref[...] * cosine_ref[...]
    forcing = load_columns(forcing_ref, points, levels, padded)
    rows_ref[16:24] = add_all([fold(tile) for tile in forcing])
    forced = [tile + sun for tile in forcing]
    for i, tile in enumerate(dot(inverse, forced)):
        forced_ref[i] = forced[i]
        base_ref[i] = tile
    weight = load_columns(weight_ref, points, levels, padded)
    for i, tile in enumerate(weight):
        weight_out_ref[i] = tile
    matrices_ref[0:padded] = matrix_ref[...]
    matrices_ref[padded : 2 * padded] = dot(inverse, [matrix_ref[...]])[0]
    heated = jnp.sum(fold(matrix_ref[...]), axis=0, keepdims=True)
    matrices_ref[2 * padded :] = jnp.broadcast_to(heated, (8, across))
    unit_ref[...] = jnp.broadcast_to(
        jnp.sum(inverse_ref[...], axis=1, keepdims=True), unit_ref.shape
    )
    rows_ref[0:8] = add_all([fold(tile) for tile in weight])
    solar = jnp.sum(fold(sun), axis=0, keepdims=True)
    rows_ref[8:16] = jnp.broadcast_to(solar, (8, across))


def smooth_kernel(levels, tiles, groups, swap, *refs):
    *refs, message_ref, message_sem = refs
    count = len(refs) - 6 - 2 * swap
    *kelvin_refs, forced_ref, weight_ref, base_ref, matrices_ref, rows_ref, unit_ref = refs[:count]
    sent_ref, residual_ref, smooth_ref, rim_ref, inner_ref, outer_ref, *refs = refs[count:]
    points, padded, across = residual_ref.shape
    if swap:
        state_ref, scratch_ref = refs
        tile = lax.axis_index("tile")
        packed_ref, near_ref, *far_refs = kelvin_refs
        scratch_ref[tile], scratch_ref[tile ^ 1] = packed_ref[tile], near_ref[tile >> 1]
        for step, far_ref in zip(far_steps(points), far_refs):
            scratch_ref[tile ^ step], scratch_ref[tile ^ (step + 1)] = far_ref[0], far_ref[1]
        kelvin = swap_groups([scratch_ref[i] for i in range(points)])
    else:
        kelvin = [kelvin_refs[0][i] for i in range(points)]
    squares = [tile * tile for tile in kelvin]
    emission = [tile * tile for tile in squares]
    both = dot(matrices_ref[padded:, :padded], emission)
    solar, unit = rows_ref[8:9, :], unit_ref[...]
    means = [(tile[padded : padded + 1] + solar) * (1.0 / levels) for tile in both]
    smooth = [base_ref[i] + (both[i][:padded] - unit * means[i]) for i in range(points)]
    for i in range(points):
        smooth_ref[i] = smooth[i]
    weight = [weight_ref[i] for i in range(points)]
    folded = [fold(tile) for tile in smooth]
    loss = add_all([fold(a * b) for a, b in zip(smooth, weight)])
    mass = rows_ref[0:8, :]
    every = add_all(folded)
    lane = iota(every.shape, 1)
    scalars = scalars_row(
        [
            rows_ref[16:24, :] - loss,
            folded[0],
            folded[-1],
            jnp.where(lane == 0, every, 0.0),
            jnp.where(lane == across - 1, every, 0.0),
            mass,
        ],
        across,
    )
    lane = iota((padded, across), 1)
    corner = jnp.where((lane == 0) | (lane == across - 1), smooth[0], turn(smooth[-1], 2))
    rows = jnp.concatenate([corner, jnp.zeros((across - padded, across), F32)], axis=0).T
    scalars = turn(scalars, padded)
    message_ref[...] = jnp.broadcast_to(scalars[None], message_ref.shape)
    corners = (0, 2, across - 1, 1)
    for place, corner in zip(neighbours(tiles, groups)[5:], corners):
        message_ref[pl.ds(place, 1), 0, :] = rows[corner : corner + 1] + scalars
    send = pltpu.make_async_copy(message_ref, sent_ref, message_sem.at[0])
    send.start()

    heat = dot(matrices_ref[:padded, :padded], emission)
    real = iota((padded, across), 0) < levels
    for i in range(points):
        residual_ref[i] = forced_ref[i] + jnp.where(real, heat[i] - means[i], 0.0)
    stride = across // points
    rim = jnp.zeros((padded, across), F32)
    for i in range(points):
        place = (lane - stride * i + 2) & (across - 1)
        rim = jnp.where(place < 4, turn(smooth[i], stride * i), rim)
        rim = jnp.where((place == 5) | (place == 6), turn(weight[i], stride * i + 4), rim)
    rim_ref[...] = rim
    even = lax.rem(lax.axis_index("tile"), 2) == 0
    sides = zip((smooth[0], smooth[1], weight[0]), (smooth[-2], smooth[-1], weight[-1]))
    for j, (west, east) in enumerate(sides):
        inner_ref[j] = jnp.where(even, east, west)
        outer_ref[j] = jnp.where(even, west, east)
    if swap:
        for s, tile in enumerate(swap_groups(smooth)):
            state_ref[s] = tile
    send.wait()


def send_kernel(near_ref, smooth_ref, second_ref, *out_refs):
    tile = lax.axis_index("tile")
    for step, out_ref in zip(far_steps(smooth_ref.shape[0]), out_refs):
        place = tile ^ step
        out_ref[0], out_ref[1] = smooth_ref[place], second_ref[place]
        out_ref[2], out_ref[3] = near_ref[place >> 1, 0], near_ref[place >> 1, 1]


def neighbours(tiles, groups):
    tile, group = lax.axis_index("tile"), lax.axis_index("grp")
    west, east = lax.rem(tile + tiles - 1, tiles), lax.rem(tile + 1, tiles)
    south, north = jnp.maximum(group - 1, 0), jnp.minimum(group + 1, groups - 1)
    pairs = [(tile, group), (west, group), (east, group), (tile, south), (tile, north)]
    pairs += [(west, south), (east, south), (west, north), (east, north)]
    return [x * groups + y for x, y in pairs]


def small_inverse(block):
    size = len(block)
    block = [list(row) for row in block]
    for k in range(size):
        pivot = 1.0 / block[k][k]
        row = [block[k][j] * pivot for j in range(size)]
        for i in range(size):
            if i != k:
                factor = block[i][k]
                for j in range(size):
                    if j != k:
                        block[i][j] = block[i][j] - factor * row[j]
                block[i][k] = -factor * pivot
        for j in range(size):
            block[k][j] = row[j]
        block[k][k] = pivot
    return block


def product(a, b):
    size = range(len(a))
    return [[add_all([a[i][k] * b[k][j] for k in size]) for j in size] for i in size]


def apply(a, v):
    size = range(len(a))
    return [add_all([a[i][k] * v[k] for k in size]) for i in size]


def flip(a):
    return [list(row) for row in zip(*a)]


def turn_block(a, shift):
    return [[turn(value, shift) for value in row] for row in a]


def with_diagonal(block, row_sums, beside):
    size = range(len(block))
    return [
        [
            row_sums[i] - add_all([block[i][k] for k in size if k != i] + beside[i]) if i == j else block[i][j]
            for j in size
        ]
        for i in size
    ]


def coarse_factor(mass, tiles, groups, x_face, y_face):
    zero = jnp.zeros_like(mass)
    size = range(groups)
    diagonal = [[zero - y_face if abs(i - j) == 1 else zero for i in size] for j in size]
    coupling = [[zero - x_face if i == j else zero for i in size] for j in size]
    row_sums = [turn(mass, -j) for j in size]
    diagonal = with_diagonal(diagonal, row_sums, [[zero - 2.0 * x_face]] * groups)
    steps = []
    step = 1
    while step < tiles:
        inverse = small_inverse(diagonal)
        shift = step * groups
        steps.append((inverse, coupling))
        left = product(coupling, turn_block(inverse, shift))
        low = product(left, flip(coupling))
        high = turn_block(product(flip(coupling), product(inverse, coupling)), -shift)
        row_sums = reduce_sums(inverse, coupling, row_sums, shift)
        diagonal = [[diagonal[i][j] - (low[i][j] + high[i][j]) for j in size] for i in size]
        coupling = [[-v for v in row] for row in product(left, turn_block(coupling, shift))]
        step *= 2
        beside = [
            [add_all(coupling[i]), turn(add_all(flip(coupling)[i]), -step * groups)] for i in size
        ]
        diagonal = with_diagonal(diagonal, row_sums, beside)
    last = [[diagonal[i][j] + (coupling[i][j] + coupling[j][i]) for j in size] for i in size]
    last = with_diagonal(last, row_sums, [[]] * groups)
    return steps, small_inverse(last)


def reduce_sums(inverse, coupling, values, shift):
    scaled = apply(inverse, values)
    low = apply(coupling, [turn(v, shift) for v in scaled])
    high = [turn(v, -shift) for v in apply(flip(coupling), scaled)]
    return [v - (a + b) for v, a, b in zip(values, low, high)]


def coarse_solve(steps, last, sums, groups):
    values = [turn(sums, -j) for j in range(groups)]
    shift = groups
    for inverse, coupling in steps:
        values = reduce_sums(inverse, coupling, values, shift)
        shift *= 2
    values = apply(last, values)
    residue = iota(sums.shape, 1) % groups
    result = values[0]
    for j in range(1, groups):
        result = jnp.where(residue == j, turn(values[j], j), result)
    return result


def around(row, groups):
    residue = iota(row.shape, 1) % groups
    south = jnp.where(residue == 0, row, turn(row, 1))
    north = jnp.where(residue == groups - 1, row, turn(row, -1))
    return turn(row, groups), turn(row, -groups), south, north


def by_block(received):
    blocks, lanes = received.shape
    if blocks < lanes:
        received = jnp.concatenate([received] * (lanes // blocks), axis=0)
    return received.T


def save_steps(ref, steps, last):
    rows = [v for inverse, coupling in steps for block in (inverse, coupling) for row in block for v in row]
    rows += [v for row in last for v in row]
    for n, row in enumerate(rows):
        ref[n : n + 1, :] = row


def saved_rows(tiles, groups):
    steps = max(tiles - 1, 0).bit_length()
    return (2 * steps + 1) * groups * groups


def load_steps(ref, tiles, groups):
    place = 0
    blocks = []
    for _ in range(2 * max(tiles - 1, 0).bit_length() + 1):
        block = []
        for _ in range(groups):
            block.append([ref[place + j : place + j + 1, :] for j in range(groups)])
            place += groups
        blocks.append(block)
    return list(zip(blocks[:-1:2], blocks[1::2])), blocks[-1]


def coarse_kernel(levels, points, tiles, groups, received_ref, steps_ref, coarse_ref):
    padded = -(-levels // 8) * 8
    scalars = by_block(received_ref[:, 0, :])
    base, west, east, south, north, mass = [scalars[padded + j : padded + j + 1, :] for j in range(6)]
    residue = iota(base.shape, 1) % groups
    facing_south = jnp.where(residue == 0, south, turn(north, 1))
    facing_north = jnp.where(residue == groups - 1, north, turn(south, -1))
    sums = base + (
        (turn(east, groups) - west)
        + (turn(west, -groups) - east)
        + (facing_south - south)
        + (facing_north - north)
    )
    steps, last = coarse_factor(
        mass, tiles, groups, float(levels * received_ref.shape[2]), float(levels * points)
    )
    coarse = coarse_solve(steps, last, sums, groups)
    save_steps(steps_ref, steps, last)
    coarse_ref[...] = coarse


def beyond(groups, lane, across, none=-1):
    group = lax.axis_index("grp")
    south = jnp.where(group == 0, 0, none)
    north = jnp.where(group == groups - 1, across - 1, none)
    return (lane == south) | (lane == north)


def inside_kernel(
    levels,
    tiles,
    groups,
    received_ref,
    coarse_ref,
    inner_ref,
    outer_ref,
    smooth_ref,
    weight_ref,
    inverse_ref,
    image_ref,
    second_ref,
    values_ref,
    corners_ref,
):
    points, padded, across = smooth_ref.shape
    coarse = coarse_ref[...]
    places = neighbours(tiles, groups)
    lane = iota(coarse.shape, 1)
    picked = [jnp.sum(jnp.where(lane == place, coarse, 0.0), axis=1, keepdims=True) for place in places]
    for j, value in enumerate(picked):
        values_ref[j : j + 1, :] = jnp.broadcast_to(value, (1, across))
    shape = (padded, across)
    real = iota(shape, 0) < levels
    own, e_west, e_east, e_south, e_north, e_sw, e_se, e_nw, e_ne = [
        jnp.where(real, value, 0.0) for value in picked
    ]

    corner_rows = [received_ref[pl.ds(place, 1), 0, :] for place in places[5:]]
    corner_rows = [jnp.where(iota(row.shape, 1) < padded, row, 0.0) for row in corner_rows]
    corners = jnp.concatenate(corner_rows + [jnp.zeros((across - 4, across), F32)], axis=0).T
    c_sw, c_se, c_nw, c_ne = [corners[:padded, j : j + 1] for j in range(4)]

    for j, corner in enumerate((c_sw, c_se, c_nw, c_ne)):
        corners_ref[j] = jnp.broadcast_to(corner, shape)

    lane = iota(shape, 1)
    first, final = lane == 0, lane == across - 1

    outside = beyond(groups, lane, across)

    def across_sum(tile, ends):
        ends = jnp.where(outside, tile, ends)
        return jnp.where(first, ends, turn(tile, 1)) + jnp.where(final, ends, turn(tile, -1))

    even_tile = lax.rem(lax.axis_index("tile"), 2) == 0
    weight = [weight_ref[i] for i in range(points)]
    from_west = [jnp.where(even_tile, outer_ref[j], inner_ref[j]) for j in range(3)]
    from_east = [jnp.where(even_tile, inner_ref[j], outer_ref[j]) for j in range(3)]
    weight = from_west[2:] + weight + from_east[2:]
    field = from_west[:2] + [smooth_ref[i] for i in range(points)] + from_east[:2]

    ends = [jnp.where(first, c_sw, c_nw), *[jnp.zeros(shape, F32)] * points, jnp.where(first, c_se, c_ne)]

    def steps(here, low, high):
        return jnp.where(first, here - low, jnp.where(final, here - high, 0.0))

    here = [e_west] + [own] * points + [e_east]
    jumps = [steps(e_west, e_sw, e_nw) + (e_west - own)]
    jumps += [steps(own, e_south, e_north)] * points
    jumps += [steps(e_east, e_se, e_ne) + (e_east - own)]
    jumps[1] = jumps[1] + (own - e_west)
    jumps[points] = jumps[points] + (own - e_east)
    image = [
        (field[i] + field[i + 2])
        + across_sum(field[i + 1], ends[i])
        - (weight[i] * (field[i + 1] + here[i]) + jumps[i])
        for i in range(points + 2)
    ]
    smoothed = dot(inverse_ref[:, :padded], image)
    for i in range(points + 2):
        image_ref[i] = image[i]
        second_ref[i] = field[i + 1] - smoothed[i]


def second_kernel(
    levels,
    groups,
    low_ref,
    high_ref,
    rim_ref,
    residual_ref,
    weight_ref,
    inverse_ref,
    image_ref,
    second_ref_in,
    values_ref,
    corners_ref,
    *refs,
):
    *refs, message_ref, message_sem = refs
    swap = len(refs) > 2
    if swap:
        packed_smooth_ref, sent_ref, second_ref, packed_ref, near_ref = refs
    else:
        sent_ref, second_ref = refs
    points, padded, across = residual_ref.shape
    blocks = message_ref.shape[0]
    stride = across // points
    even_group = lax.rem(lax.axis_index("grp"), 2) == 0

    shape = (padded, across)
    real = iota(shape, 0) < levels
    values = [values_ref[j : j + 1, :] for j in range(9)]
    own, e_west, e_east, e_south, e_north, e_sw, e_se, e_nw, e_ne = [
        jnp.where(real, value, 0.0) for value in values
    ]
    c_sw, c_se, c_nw, c_ne = [corners_ref[j] for j in range(4)]
    weight = [weight_ref[i] for i in range(points)]
    lane = iota(shape, 1)
    first, final = lane == 0, lane == across - 1
    outside = beyond(groups, lane, across)
    inside = lane & (stride - 1)
    is_south, is_north = inside == stride - 1, inside == 0
    rim, low, high = rim_ref[...], low_ref[...], high_ref[...]
    from_south = jnp.where(even_group, high, low)
    from_north = jnp.where(even_group, low, high)
    outer = beyond(groups, jnp.where(is_north, 0, jnp.where(is_south, across - 1, 1)), across)
    both = jnp.where(is_north, turn(from_south, 1), turn(from_north, -1))
    both = jnp.where((is_north | is_south) & jnp.logical_not(outer), both, 0.0)
    edge = stride * (points - 1)

    def ring_image(tile, step, here, west, east, west_lane, east_lane, c_west, c_east):
        rim_weight = turn(tile, -4)
        spread = (here - own) + jnp.where(lane == west_lane, here - west, jnp.where(lane == east_lane, here - east, 0.0))
        return (
            jnp.where(lane == west_lane, c_west, turn(tile, stride))
            + jnp.where(lane == east_lane, c_east, turn(tile, -stride))
            + (turn(tile, step) + turn(rim, -step))
            - (rim_weight * (tile + here) + spread)
        )

    ring_south = ring_image(from_south, 1, e_south, e_sw, e_se, across - 1, edge - 1, c_sw, c_se)
    ring_north = ring_image(from_north, -1, e_north, e_nw, e_ne, 0, edge, c_nw, c_ne)
    ring = jnp.where(is_south, ring_south, jnp.where(is_north, ring_north, 0.0))
    ring_field = jnp.where(is_south, from_south, from_north)
    ring, smoothed = dot(inverse_ref[:, :padded], [ring, both])
    ring = ring_field - ring
    second, image = [second_ref_in[0]], [None]
    ends = first | final
    for i in range(1, points + 1):
        shift = -stride * (i - 1)
        image.append(jnp.where(ends, image_ref[i] + turn(both, shift), image_ref[i]))
        second.append(jnp.where(ends, second_ref_in[i] - turn(smoothed, shift), second_ref_in[i]))
    second.append(second_ref_in[points + 1])
    both = jnp.where(is_north, turn(ring, 1), turn(ring, -1))

    names = ("image", "change", "residual")
    pairs = {}
    sides = {name: [] for name in names}
    left = []

    def collect(key, value):
        pairs.setdefault(key, []).append(fold(value))

    for i in range(points):
        tile = second[i + 1]
        second_ref[i] = tile
        ends = jnp.where(outside, tile, turn(both, -stride * i))
        again = (
            (second[i] + second[i + 2])
            + (jnp.where(first, ends, turn(tile, 1)) + jnp.where(final, ends, turn(tile, -1)))
            - weight[i] * tile
        )
        residual = residual_ref[i]
        result = residual - image[i + 1]
        change = result - again
        left.append(fold(again + (result - 4.0 * tile)))
        heavy = weight[i]
        collect("qq", result * result)
        collect("rq", residual * result)
        collect("qd", result * change)
        collect("dd", change * change)
        collect("rd", residual * change)
        collect("ww", heavy * heavy)
        sides.setdefault("weight", []).append(fold(heavy))
        for name, value in zip(names, (result, change, residual)):
            sides[name].append(fold(value))
            collect("w" + name, heavy * value)
    pairs = {key: add_all(value) for key, value in pairs.items()}
    lane = iota(pairs["qq"].shape, 1)
    out = [pairs[key] for key in ("qq", "rq", "qd", "dd", "rd")]
    for name in names + ("weight",):
        every = add_all(sides[name])
        out += [
            pairs["ww"] if name == "weight" else pairs["w" + name],
            sides[name][0],
            sides[name][-1],
            jnp.where(lane == 0, every, 0.0),
            jnp.where(lane == across - 1, every, 0.0),
        ]
    out.append(add_all(left))
    row = scalars_row(out, across)
    message_ref[...] = jnp.broadcast_to(row[None], message_ref.shape)
    send = pltpu.make_async_copy(message_ref, sent_ref, message_sem.at[0])
    send.start()
    if swap:
        for s, tile in enumerate(swap_groups(second[1 : points + 1])):
            packed_ref[s] = tile
        other = 1 - (lax.axis_index("tile") & 1)
        for j in range(points // 2):
            near_ref[j, 0] = packed_smooth_ref[2 * j + other]
            near_ref[j, 1] = packed_ref[2 * j + other]
    send.wait()


def final_kernel(
    levels,
    tiles,
    groups,
    swap,
    received_ref,
    steps_ref,
    coarse_ref,
    smooth_ref,
    second_ref,
    field_ref,
    other_ref,
):
    points, padded, across = smooth_ref.shape
    blocks = tiles * groups
    rows = by_block(received_ref[:, 0, :])
    rows = [rows[j : j + 1, :] for j in range(26)]
    steps, last = load_steps(steps_ref, tiles, groups)
    coarse = coarse_solve(steps, last, rows[25], groups)
    jumps = [coarse - near for near in around(coarse, groups)]

    def against(part):
        return add_all([rows[part] * coarse] + [rows[part + 1 + j] * jumps[j] for j in range(4)])

    j_w, j_e, j_s, j_n = jumps
    x_face, y_face = float(levels * across), float(levels * points)
    weighted = add_all([rows[21 + j] * jumps[j] for j in range(4)])
    square = (
        coarse * (rows[20] * coarse + 2.0 * weighted)
        + x_face * (j_w * j_w + j_e * j_e)
        + y_face * (j_s * j_s + j_n * j_n)
        + (2.0 * levels) * ((j_w + j_e) * (j_s + j_n))
    )
    lane = iota(coarse.shape, 1)
    tile, group = lax.axis_index("tile"), lax.axis_index("grp")
    parts = [
        rows[0],
        rows[1],
        rows[2] + against(5),
        rows[3] + 2.0 * against(10) + square,
        rows[4] + against(15),
    ]
    parts = [jnp.where(lane < blocks, part, 0.0) for part in parts]
    parts += [jnp.zeros_like(coarse)] * 3
    sums = jnp.sum(jnp.concatenate(parts, axis=0), axis=1, keepdims=True)
    qq, rq, qv, vv, rv = [sums[j : j + 1, :] for j in range(5)]
    alpha = rq / qq
    beta = qv / qq
    kappa = (rv - alpha * qv) / (vv - beta * qv)
    scale = alpha - kappa * beta
    constant = scale * coarse_ref[...] + kappa * coarse
    others = tiles if swap else 1
    parts = [jnp.where(lane == (tile ^ k) * groups + group, constant, 0.0) for k in range(others)]
    parts += [jnp.zeros_like(coarse)] * (-others % 8)
    shifts = jnp.sum(jnp.concatenate(parts, axis=0), axis=1, keepdims=True)
    shifts = [shifts[k : k + 1, :] for k in range(others)]
    result = [scale * smooth_ref[i] + (kappa * second_ref[i] + shifts[0]) for i in range(points)]
    store_columns(field_ref, result, levels)
    if swap:
        rows = jnp.concatenate([scale, kappa] + shifts, axis=0)
        rows = jnp.concatenate([rows, jnp.zeros((other_ref.shape[0] - rows.shape[0], 1), F32)], axis=0)
        other_ref[...] = jnp.broadcast_to(rows, other_ref.shape)
    else:
        for i in range(points):
            other_ref[i] = result[i]


def state_kernel(levels, scalars_ref, *refs):
    smooth_ref, second_ref, near_ref, *part_refs, state_ref, scratch_ref = refs
    tile = lax.axis_index("tile")
    scale, kappa = scalars_ref[0:1, :], scalars_ref[1:2, :]
    pairs = {0: (smooth_ref[tile], second_ref[tile]), 1: (near_ref[tile >> 1, 0], near_ref[tile >> 1, 1])}
    for step, part_ref in zip(far_steps(smooth_ref.shape[0]), part_refs):
        pairs[step] = (part_ref[0], part_ref[1])
        pairs[step + 1] = (part_ref[2], part_ref[3])
    for k, (smooth, second) in pairs.items():
        scratch_ref[tile ^ k] = scale * smooth + (kappa * second + scalars_ref[2 + k : 3 + k, :])
    store_columns(state_ref, swap_groups([scratch_ref[s] for s in range(len(pairs))]), levels)


def per_device(
    forcing_vector,
    shift_weights,
    layer_link_factor,
    previous_kelvin_field,
    longwave_opacity,
    shortwave_opacity,
):
    tiles, groups = lax.axis_size("tile"), lax.axis_size("grp")
    levels, points, across = forcing_vector.shape
    padded = -(-levels // 8) * 8
    blocks = tiles * groups
    lanes = max(across, blocks)
    width = across // tiles
    swap = tiles == points
    flat = (levels * points, across)
    field = (points, padded, across)

    def to_tiles(value):
        return lax.all_to_all(value, "tile", split_axis=0, concat_axis=0, tiled=True)

    def gather(value):
        return lax.all_to_all(value, ("tile", "grp"), split_axis=0, concat_axis=0, tiled=True)

    def part(kernel, *settings):
        return lambda *refs: kernel(*settings, *refs)

    kelvin = previous_kelvin_field
    if swap:
        near = (tiles // 2, padded, across)
        packed, near = call(part(pack_kernel, levels), [field, near], kelvin.reshape(flat))
        near = lax.ppermute(near, "tile", [(i, i ^ 1) for i in range(tiles)])
        far = call(relay_kernel, [(2, padded, across)] * (tiles // 2 - 1), near, packed)
        kelvin = [packed, near] + [
            lax.ppermute(value, "tile", [(i, i ^ step) for i in range(tiles)])
            for step, value in zip(far_steps(tiles), far)
        ]
    else:
        kelvin = kelvin.reshape(levels, points, tiles, width).transpose(2, 1, 0, 3)
        kelvin = to_tiles(kelvin).transpose(1, 2, 0, 3).reshape(points, levels, across)
        kelvin = jnp.pad(kelvin, ((0, 0), (0, padded - levels), (0, 0)))

    vectors = [v[None, :] for v in (layer_link_factor, longwave_opacity, shortwave_opacity)]
    inverse, matrix, absorbed = call(
        part(tables_kernel, levels),
        [(padded, across)] * 3,
        *vectors,
        scratch=[v.shape for v in vectors],
        copies=len(vectors),
    )
    global_row = lax.axis_index("grp") * across + jnp.arange(across)
    latitude = ((global_row.astype(F32) + 0.5) / (across * groups) - 0.5) * (math.pi / 2)
    cosine = jnp.cos(latitude - 0.4)[None, :]

    forcing = forcing_vector.reshape(flat)
    weights = shift_weights.reshape(flat)
    forced, weights, *prepared = call(
        part(prepare_kernel, levels),
        [field, field, field, (2 * padded + 8, across), (24, across), (padded, across)],
        forcing,
        weights,
        inverse,
        matrix,
        absorbed,
        cosine,
    )
    prepared = [forced, weights, *prepared]
    message = (blocks, MESSAGE_ROWS, across)
    tile, side = (padded, across), (3, padded, across)
    message, residual, smooth, rim, inner, outer, *packed = call(
        part(smooth_kernel, levels, tiles, groups, swap),
        [message, field, field, tile, side, side] + [field] * swap,
        *(kelvin if swap else [kelvin]),
        *prepared,
        scratch=[field] * swap,
        sends=True,
    )
    received = gather(message)

    def inner_pairs(size):
        return [(i, i ^ 1) for i in range(size) if i ^ 1 < size]

    def outer_pairs(size, around):
        pairs = [(i, (i + 1) % size) for i in range(1, size, 2) if around or i + 1 < size]
        return pairs + [(j, i) for i, j in pairs]

    inner = lax.ppermute(inner, "tile", inner_pairs(tiles))
    outer = lax.ppermute(outer, "tile", outer_pairs(tiles, True))
    low = lax.ppermute(rim, "grp", inner_pairs(groups))
    high = lax.ppermute(rim, "grp", outer_pairs(groups, False))
    wide = (points + 2, padded, across)
    steps, coarse = call(
        part(coarse_kernel, levels, points, tiles, groups),
        [(saved_rows(tiles, groups), lanes), (1, lanes)],
        received,
    )
    image, second, values, corners = call(
        part(inside_kernel, levels, tiles, groups),
        [wide, wide, (16, across), (4, padded, across)],
        received,
        coarse,
        inner,
        outer,
        smooth,
        weights,
        inverse,
    )
    near = (tiles // 2, 2, padded, across)
    message, second, *sent = call(
        part(second_kernel, levels, groups),
        [(blocks, LAST_ROWS, across), field] + [field, near] * swap,
        low,
        high,
        rim,
        residual,
        weights,
        inverse,
        image,
        second,
        values,
        corners,
        *packed,
        sends=True,
    )
    received = gather(message)
    parts = []
    if swap:
        near = lax.ppermute(sent[1], "tile", inner_pairs(tiles))
        parts = [packed[0], sent[0], near]
        far = call(send_kernel, [(4, padded, across)] * (tiles // 2 - 1), near, packed[0], sent[0])
        for step, value in zip(far_steps(tiles), far):
            parts.append(lax.ppermute(value, "tile", [(i, i ^ step) for i in range(tiles)]))
    solution_field, state = call(
        part(final_kernel, levels, tiles, groups, swap),
        [flat, (-(-(tiles + 2) // 8) * 8, across) if swap else field],
        received,
        steps,
        coarse,
        smooth,
        second,
    )
    if swap:
        (state,) = call(part(state_kernel, levels), [flat], state, *parts, scratch=[field])
    if not swap:
        state = state[:, :levels].reshape(points, levels, tiles, width).transpose(2, 1, 0, 3)
        state = to_tiles(state).transpose(1, 2, 0, 3)
    shape = (levels, points, across)
    return solution_field.reshape(shape), state.reshape(shape)


def solution(mesh):
    return jax.shard_map(
        per_device,
        mesh=mesh,
        in_specs=(
            P(None, "tile", "grp"),
            P(None, "tile", "grp"),
            P(),
            P(None, None, ("tile", "grp")),
            P(),
            P(),
        ),
        out_specs=(P(None, "tile", "grp"), P(None, None, ("tile", "grp"))),
        check_vma=False,
    )
```
